32 devices in a mesh: dp: 8 (over y, x, core), blk: 4 (over z).
Axes of the slice: x: 2, y: 2, z: 4, core: 2. Of those that a mesh axis runs over, the one named last changes fastest.
Arguments:
- inputs: bfloat16 [8192, 1024], P(('dp', 'blk')), may hold values from -6 to 6
- positions: int32 [8192], P(('dp', 'blk')), may hold values from 0 to 1023, as said below
- w_query: bfloat16 [1024, 1024], P(('dp', 'blk')), may hold values from -0.21875 to 0.21875
- w_key: bfloat16 [1024, 1024], P(('dp', 'blk')), may hold values from -0.21875 to 0.21875
- w_value: bfloat16 [1024, 1024], P(('dp', 'blk')), may hold values from -0.1875 to 0.1875
- w_out: bfloat16 [1024, 1024], P(('dp', 'blk')), may hold values from -0.75 to 0.75
- w_up: bfloat16 [1024, 4096], P(('dp', 'blk')), may hold values from -0.1875 to 0.1875
- w_down: bfloat16 [4096, 1024], P(('dp', 'blk')), may hold values from -0.09375 to 0.09375
- up_bias: bfloat16 [4096], P(('dp', 'blk')), may hold values from -3 to 3
- down_bias: bfloat16 [1024], P(('dp', 'blk')), may hold values from -3 to 3
- ln1_gain: bfloat16 [1024], P(('dp', 'blk')), may hold values from 0.5 to 1.5
- ln1_bias: bfloat16 [1024], P(('dp', 'blk')), may hold values from -3 to 3
- ln2_gain: bfloat16 [1024], P(('dp', 'blk')), may hold values from 0.5 to 1.5
- ln2_bias: bfloat16 [1024], P(('dp', 'blk')), may hold values from -3 to 3
- cotangent: bfloat16 [8192, 1024], P(('dp', 'blk')), may hold values from -6 to 6
Outputs:
- output: bfloat16 [8192, 1024], P(('dp', 'blk'))
- input_grad: bfloat16 [8192, 1024], P(('dp', 'blk'))
- grad_query: float32 [1024, 1024], P(('dp', 'blk'))
- grad_key: float32 [1024, 1024], P(('dp', 'blk'))
- grad_value: float32 [1024, 1024], P(('dp', 'blk'))
- grad_out: float32 [1024, 1024], P(('dp', 'blk'))
- grad_up: float32 [1024, 4096], P(('dp', 'blk'))
- grad_down: float32 [4096, 1024], P(('dp', 'blk'))
- grad_up_bias: float32 [4096], P(('dp', 'blk'))
- grad_down_bias: float32 [1024], P(('dp', 'blk'))
- grad_ln1_gain: float32 [1024], P(('dp', 'blk'))
- grad_ln1_bias: float32 [1024], P(('dp', 'blk'))
- grad_ln2_gain: float32 [1024], P(('dp', 'blk'))
- grad_ln2_bias: float32 [1024], P(('dp', 'blk'))
The draws below stay inside these ranges and needn't reach their ends.
Inputs may be any that keep to these rules, and one draw needn't show every extreme that they name: The rows of a group are its 1024 stream positions in order. A group holds either one sequence of 1024 tokens or two sequences of 512 tokens one after the other; positions count 0, 1, 2, ... from each sequence's start. 8 // 2 of the groups hold one sequence.
All inputs are finite; a program needn't handle non-finite values.
Results may differ from the reference program's by a relative error of at most 0.015.
Values may be sent and summed in bfloat16 or wider, within the bound.
A program may use at most 256 MiB of HBM per device.

```python
import math
import jax
import jax.numpy as jnp
from jax import lax

D = 1024
HEADS = 8
FF = 4096
TOK_DEV = 256
GROUPS = 8
GROUP_TOK = 1024
TOKENS = 8192
N_DP = 8
N_BLK = 4


def draw_positions(key, part):
    order = jax.random.permutation(jax.random.fold_in(key, 11), GROUPS)
    longer = order < GROUPS // 2
    index = jnp.arange(GROUP_TOK, dtype=jnp.int32)
    shorter = index % (GROUP_TOK // 2)
    table = jnp.where(longer[:, None], index[None, :], shorter[None, :])
    return table.reshape(-1).astype(jnp.int32)


def draw_inputs(key, part):
    key = jax.random.fold_in(key, 31)
    row_shift = jax.random.uniform(jax.random.fold_in(key, 1), (TOKENS, 1), jnp.float32, minval=-1.5, maxval=1.5)
    row_scale = jax.random.uniform(jax.random.fold_in(key, 2), (TOKENS, 1), jnp.float32, minval=0.5, maxval=1.5)
    noise = jnp.clip(jax.random.normal(jax.random.fold_in(key, 4), (TOKENS, D), jnp.float32), -3.0, 3.0)
    return (noise * row_scale + row_shift).astype(jnp.bfloat16)


def draw_cotangent(key, part):
    key = jax.random.fold_in(key, 37)
    noise = jnp.clip(jax.random.normal(jax.random.fold_in(key, 2), (TOKENS, D), jnp.float32), -4.0, 4.0)
    return noise.astype(jnp.bfloat16)


def shard_levels(stream_key, dims, pieces, smallest, high):
    level = 1.0
    for axis_at, blocks in pieces:
        heights = jax.random.uniform(jax.random.fold_in(jax.random.fold_in(stream_key, 6), axis_at), (blocks,), jnp.float32, smallest / len(pieces), high / len(pieces))
        level = level * jnp.repeat(jnp.exp(heights), dims[axis_at] // blocks).reshape((-1,) + (1,) * (len(dims) - 1 - axis_at))
    return level


def bell_draw(rng, dims, scale, most, cuts=(), kind=jnp.bfloat16):
    entries = scale * jax.random.normal(rng, dims, jnp.float32)
    if cuts:
        entries = entries * shard_levels(rng, dims, cuts, -0.22, 0.18)
    return jnp.clip(entries, -most, most).astype(kind)


def setup_inputs(seed: int = 0) -> dict:
    splits = jax.random.split(jax.random.key(seed), 16)
    inputs = draw_inputs(jax.random.fold_in(splits[15], 71), 0)
    positions = draw_positions(jax.random.fold_in(splits[15], 71), 0)
    w_query = bell_draw(splits[2], (D, D), (2 * D // 3) ** -0.5, 0.21875, ((0, 32),))
    w_key = bell_draw(splits[3], (D, D), (2 * D // 3) ** -0.5, 0.21875, ((0, 32),))
    w_value = bell_draw(splits[4], (D, D), D ** -0.5, 0.1875, ((0, 32),))
    w_out = bell_draw(splits[5], (D, D), (D // 16) ** -0.5, 0.75, ((0, 32),))
    w_up = bell_draw(splits[6], (D, FF), D ** -0.5, 0.1875, ((0, 32),))
    w_down = bell_draw(splits[7], (FF, D), FF ** -0.5, 0.09375, ((0, 32),))
    up_bias = bell_draw(splits[8], (FF,), 0.5, 3.0, ((0, 32),))
    down_bias = bell_draw(splits[9], (D,), 0.5, 3.0, ((0, 32),))
    ln1_gain = jnp.clip(1.0 + 0.1 * jax.random.normal(splits[10], (D,), jnp.float32), 0.5, 1.5).astype(jnp.bfloat16)
    ln1_bias = bell_draw(splits[11], (D,), 0.5, 3.0, ((0, 32),))
    ln2_gain = jnp.clip(1.0 + 0.1 * jax.random.normal(splits[12], (D,), jnp.float32), 0.5, 1.5).astype(jnp.bfloat16)
    ln2_bias = bell_draw(splits[13], (D,), 0.5, 3.0, ((0, 32),))
    cotangent = draw_cotangent(jax.random.fold_in(splits[15], 71), 0)
    return {"inputs": inputs, "positions": positions, "w_query": w_query, "w_key": w_key, "w_value": w_value, "w_out": w_out, "w_up": w_up, "w_down": w_down, "up_bias": up_bias, "down_bias": down_bias, "ln1_gain": ln1_gain, "ln1_bias": ln1_bias, "ln2_gain": ln2_gain, "ln2_bias": ln2_bias, "cotangent": cotangent}


eps = 1e-05
masked_value = -1e+30

@jax.custom_vjp
def low(v):
    return lax.optimization_barrier(v.astype(jnp.bfloat16)).astype(jnp.float32)

@jax.custom_vjp
def low_back(v):
    return v

def low_keep(v):
    return (low(v), None)

def low_pass(kept, grad):
    return (grad,)

def back_keep(v):
    return (v, None)

def back_low(kept, grad):
    return (low(grad),)
low.defvjp(low_keep, low_pass)
low_back.defvjp(back_keep, back_low)

def layer_norm(values, gain, offset):
    centre = lax.optimization_barrier(jnp.mean(values, axis=-1, keepdims=True))
    centred = values - centre
    variance = lax.optimization_barrier(jnp.mean(centred * centred, axis=-1, keepdims=True))
    return centred * lax.rsqrt(variance + eps) * gain + offset

def decoder_layer(group_rows, group_positions, weights):
    query_weight, key_weight, value_weight, out_weight, up_weight, down_weight, up_shift, down_shift, gain_one, shift_one, gain_two, shift_two = weights
    count, length, model_width = group_rows.shape
    head_size = model_width // HEADS
    highest = lax.Precision.HIGHEST
    token_rows = group_rows.reshape(count * length, model_width)
    normed = low(layer_norm(token_rows, gain_one, shift_one))
    query = low(low_back(jnp.dot(normed, query_weight, precision=highest)))
    keys = low(low_back(jnp.dot(normed, key_weight, precision=highest)))
    values = low(low_back(jnp.dot(normed, value_weight, precision=highest)))
    query_heads = query.reshape(count, length, HEADS, head_size)
    key_heads = keys.reshape(count, length, HEADS, head_size)
    value_heads = values.reshape(count, length, HEADS, head_size)
    raw_scores = jnp.einsum('gqhd,gkhd->ghqk', query_heads, key_heads, precision=highest)
    scores = low_back(raw_scores) * (1.0 / math.sqrt(head_size))
    index = jnp.arange(length, dtype=jnp.int32)
    starts = index[None, :] - group_positions
    allowed = (index[None, None, :] <= index[None, :, None]) & (index[None, None, :] >= starts[:, :, None])
    scores = jnp.where(allowed[:, None], scores, masked_value)
    probs = jax.nn.softmax(scores, axis=-1)
    mixed_heads = jnp.einsum('ghqk,gkhd->gqhd', low(probs), value_heads, precision=highest)
    mixed = low(low_back(mixed_heads.reshape(count * length, model_width)))
    branch = low_back(jnp.dot(mixed, out_weight, precision=highest))
    residual = token_rows + branch
    normed_two = low(layer_norm(residual, gain_two, shift_two))
    preact = low_back(jnp.dot(normed_two, up_weight, precision=highest) + up_shift)
    hidden = low(jax.nn.gelu(preact, approximate=True))
    result = residual + jnp.dot(hidden, down_weight, precision=highest) + down_shift
    return result.reshape(count, length, model_width)

def reference(inputs, positions, w_query, w_key, w_value, w_out, w_up, w_down, up_bias, down_bias, ln1_gain, ln1_bias, ln2_gain, ln2_bias, cotangent):
    length = TOK_DEV * N_BLK
    groups = N_DP
    per_step = math.gcd(groups, max(1, 4096 // length))
    step_count = groups // per_step
    stacked_rows = inputs.astype(jnp.float32).reshape(step_count, per_step, length, D)
    places = positions.reshape(step_count, per_step, length)
    params = (w_query.astype(jnp.float32), w_key.astype(jnp.float32), w_value.astype(jnp.float32), w_out.astype(jnp.float32), w_up.astype(jnp.float32), w_down.astype(jnp.float32), up_bias.astype(jnp.float32), down_bias.astype(jnp.float32), ln1_gain.astype(jnp.float32), ln1_bias.astype(jnp.float32), ln2_gain.astype(jnp.float32), ln2_bias.astype(jnp.float32))

    def forward(stacked, weights):

        def one_step(stacked_pair):
            return jax.checkpoint(decoder_layer)(stacked_pair[0], stacked_pair[1], weights)
        return lax.map(one_step, (stacked, places))
    result, pullback = jax.vjp(forward, stacked_rows, params)
    grad_rows, grad_params = pullback(cotangent.astype(jnp.float32).reshape(step_count, per_step, length, D))
    output = result.reshape(TOKENS, D).astype(jnp.bfloat16)
    input_grad = grad_rows.reshape(TOKENS, D).astype(jnp.bfloat16)
    return (output, input_grad, grad_params[0], grad_params[1], grad_params[2], grad_params[3], grad_params[4], grad_params[5], grad_params[6], grad_params[7], grad_params[8], grad_params[9], grad_params[10], grad_params[11])
```

```python
import functools
import math
import types

import jax
import jax.numpy as jnp
from jax import lax
from jax.experimental import pallas as pl
from jax.experimental.pallas import tpu as pltpu
from jax.sharding import PartitionSpec as P

MESH = pl.DeviceIdType.MESH
F32 = jnp.float32
BF16 = jnp.bfloat16
HEADS = 8
VMEM_BYTES = 60 * 2**20
RANKS = 4
eps = 1e-05
masked_value = -1e30
GELU_K = math.sqrt(2.0 / math.pi)
GELU_C = 0.044715


def dot_nn(a, b):
    return lax.dot_general(a, b, (((1,), (0,)), ((), ())), preferred_element_type=F32)


def dot_nt(a, b):
    return lax.dot_general(a, b, (((1,), (1,)), ((), ())), preferred_element_type=F32)


def dot_tn(a, b):
    return lax.dot_general(a, b, (((0,), (0,)), ((), ())), preferred_element_type=F32)


def norm_parts(v):
    centre = jnp.mean(v, axis=-1, keepdims=True)
    centred = v - centre
    variance = jnp.mean(centred * centred, axis=-1, keepdims=True)
    rstd = lax.rsqrt(variance + eps)
    return centred * rstd, rstd


def norm_back(g, gain, xhat, rstd):
    e = g * gain
    return rstd * (
        e
        - jnp.mean(e, axis=-1, keepdims=True)
        - xhat * jnp.mean(e * xhat, axis=-1, keepdims=True)
    )


def hidden_at(k, tt):
    return ((k // 2) * 2 + tt % 2) * 4 + (k % 2) * 2 + tt // 2


IN_NAMES = ("x_in", "dz_in", "pos", "wq", "wk", "wv", "wo", "wup", "wdn", "db", "g1", "b1", "g2", "b2", "ub")
OUT_NAMES = ("out", "ig", "peq", "peu", "go", "gdn", "gvec")


def scratch_of(rows, width, hid, rw, fw):
    half = rows // 2
    hd = width // HEADS
    cols = 3 * 2 * hd
    dma = pltpu.SemaphoreType.DMA
    V = pltpu.VMEM
    names = dict(
        X=V((4, 2, half, width), BF16),
        DZ=V((4, 2, half, width), BF16),
        ST=V((4, 2, 16, 128), BF16),
        WA=V((4, 2, 2, 2 * rw, cols), BF16),
        WOP=V((8, rw, width), BF16),
        WO=V((2, 2, 2, rw, width), BF16),
        VEC=V((8, 16, width), BF16),
        WU=V((4, 2, 2, 2 * rw, hid), BF16),
        WD=V((8, fw, width), BF16),
        PV=V((4, 16, width), BF16),
        VF=V((8, width), F32),
        SV=V((8, rw), F32),
        VT=V((16, width), F32),
        vec=V((16, width), BF16),
        st_in=V((16, 128), BF16),
        TU=V((256, 4 * rows), BF16),
        N1=V((4 * rows, width), BF16),
        QKV=V((4 * rows, cols), BF16),
        P0=V((2, rows, rows), BF16),
        P1=V((2, rows, 2 * rows), BF16),
        P2=V((2, rows, 3 * rows), BF16),
        P3=V((2, rows, 4 * rows), BF16),
        MIX=V((4 * rows, 2 * hd), BF16),
        DMIX=V((rows, 2 * hd), BF16),
        PR0=V((4, 2, half, width), BF16),
        PR1=V((4, 2, half, width), BF16),
        RBa=V((4, half, width), BF16),
        RBb=V((4, half, width), BF16),
        RBc=V((4, half, width), BF16),
        RXa=V((4, half, width), BF16),
        RXb=V((2, half, width), BF16),
        RXc=V((4, half, width), BF16),
        RXd=V((2, half, width), BF16),
        RES=V((4, half, width), F32),
        KEEP=V((2, half, width), F32),
        N2=V((4, 2, half, width), BF16),
        HID=V((4 * rows, hid), BF16),
        DP=V((4 * rows, hid), BF16),
        DB=V((4, 2, half, width), BF16),
        ACC=V((4 * rows, 4 * hd), F32),
        TT=V((width // 2, 4 * rows), BF16),
        YSF=V((2, 4, fw, width), BF16),
        R1F=V((2, 4, fw, width), BF16),
        R2F=V((2, 2, fw, width), BF16),
        R3F=V((2, fw, width), BF16),
        YSQ=V((2, 4, 2 * rw, cols), BF16),
        R1Q=V((2, 4, 2 * rw, cols), BF16),
        R2Q=V((2, 2, 2 * rw, cols), BF16),
        R3Q=V((2, 2 * rw, cols), BF16),
        GOB=V((2, 2, 2, rw, width), BF16),
        GOR=V((2, 2, rw, width), BF16),
        GOS=V((8, rw, width), BF16),
        GOT=V((8, rw, width), BF16),
        OD=V((fw, width), F32),
        OO=V((rw, width), F32),
        OUTB=V((2, half, width), BF16),
        IGB=V((2, half, width), BF16),
        VSUM=V((8, width), F32),
        VMID=V((8, width), F32),
        VR1=V((4, 8, width), F32),
        VR2=V((8, 8, width), F32),
        sp_s=dma((3, 8)),
        sp_r=dma((3, 4, 2)),
        loc=dma((4,)),
        load=dma((7,)),
        pre_s=dma((3, 3)),
        pre_r=dma((3, 4)),
        ag_s=dma((6, 7)),
        ag_r=dma((6, 8)),
        sw_s=dma((4,)),
        sw_r=dma((4,)),
        sw_s2=dma((4,)),
        sw_r2=dma((4,)),
        FIN=V((2, 2 * rw, cols), BF16),
        FIU=V((fw, hid), BF16),
        sib_s=dma((4, 4)),
        sib_r=dma((4, 4)),
        xs=dma((4, 4)),
        xr=dma((4, 4)),
        n2_s=dma((4,)),
        n2_r=dma((4,)),
        db_s=dma((4,)),
        db_r=dma((4,)),
        r1_s=dma((4, 4)),
        r1_r=dma((4, 4)),
        up_s=dma((4, 4)),
        up_r=dma((4, 4)),
        r2_s=dma((4, 2)),
        r2_r=dma((4, 2)),
        r3_s=dma((4,)),
        r3_r=dma((4,)),
        go_s=dma((8,)),
        go_r=dma((8,)),
        pe_s=dma((2, 4)),
        pe_r=dma((2, 4)),
        v1_s=dma((3,)),
        v1_r=dma((4,)),
        v2_s=dma((7,)),
        v2_r=dma((8,)),
        ret_s=dma((2, 2)),
        ret_r=dma((2, 2)),
    )
    return names


def fused(names, *all_refs):
    m = types.SimpleNamespace(**dict(zip(names, all_refs)))
    half, width = m.X.shape[2:]
    rows = 2 * half
    hid = m.HID.shape[1]
    rw = m.WOP.shape[1]
    fw = m.WD.shape[1]
    hd = width // HEADS
    two = 2 * hd
    scale = 1.0 / math.sqrt(hd)

    dp = lax.axis_index("dp")
    z = lax.axis_index("blk")
    yx = lax.div(dp, 2)
    y, x, c = lax.div(dp, 4), lax.rem(yx, 2), lax.rem(dp, 2)
    q, p = lax.div(z, 2), lax.rem(z, 2)
    t = p * 2 + c
    me = yx * 2 + q

    def dev(yy, xx, cc, zz):
        return ((yy * 2 + xx) * 2 + cc, zz)

    def mate(tt):
        return dev(y, x, lax.rem(tt, 2), q * 2 + lax.div(tt, 2))

    def peer(yy, xx, qq):
        return dev(yy, xx, c, qq * 2 + p)

    def at8(yy, xx, qq):
        return yy * 4 + xx * 2 + qq

    sib = dev(y, x, 1 - c, z)
    nbr = dev(y, x, c, q * 2 + 1 - p)
    over = {"q": peer(y, x, 1 - q), "x": peer(y, 1 - x, q), "y": peer(1 - y, x, q)}

    mine = (p, p + 2)
    theirs = (1 - p, 3 - p)

    sent = []

    def remote(src, dst, ssem, rsem, device):
        return pltpu.make_async_remote_copy(
            src_ref=src,
            dst_ref=dst,
            send_sem=ssem,
            recv_sem=rsem,
            device_id=device,
            device_id_type=MESH,
        )

    def push(src, dst, ssem, rsem, device, keep=True):
        copy = remote(src, dst, ssem, rsem, device)
        copy.start()
        if keep:
            sent.append(copy)
        return copy

    homes = []

    def push_if(cond, src, dst, ssem, rsem, device):
        copy = remote(src, dst, ssem, rsem, device)

        @pl.when(cond)
        def _():
            copy.start()

        homes.append((jnp.logical_not(cond), copy))

    def arrived(dst, rsem):
        pltpu.make_async_copy(dst, dst, rsem).wait()

    loads = [pltpu.make_async_copy(ref, m.PR1.at[k, 0, pl.ds(0, rw)], m.load.at[k]) for k, ref in enumerate((m.wq, m.wk, m.wv))]
    loads += [
        pltpu.make_async_copy(m.wup.at[:, pl.ds(k * width, width)], m.PR1.at[k, 1, pl.ds(0, rw)], m.load.at[3 + k])
        for k in range(4)
    ]
    for copy in loads:
        copy.start()
    m.st_in[...] = jnp.broadcast_to((z * rows - m.pos[0:1, 0:1]).astype(F32), (16, 128)).astype(BF16)
    for k, ref in enumerate((m.db, m.g1, m.b1, m.g2, m.b2)):
        m.SV[k : k + 1] = ref[...].astype(F32)
    m.SV[5:8] = jnp.zeros((3, rw), F32)
    spot = lax.broadcasted_iota(jnp.int32, (rw, width), 1) - (dp * 4 + z) * rw
    hot = jnp.where(spot == lax.broadcasted_iota(jnp.int32, (rw, width), 0), 1.0, 0.0).astype(BF16)
    m.VT[0:8] = dot_nn(m.SV[...].astype(BF16), hot)
    m.VT[8:16] = jnp.zeros((8, width), F32)
    m.VT[5:6, pl.ds(pl.multiple_of(me * fw, 128), fw)] = m.ub[...].astype(F32)
    m.vec[...] = m.VT[...].astype(BF16)

    barrier = pltpu.get_barrier_semaphore()
    flips = [(a, b, d) for a in range(2) for b in range(2) for d in range(2)]

    def flipped(a, b, d):
        return ((1 - y if a else y), (1 - x if b else x), (1 - q if d else q))

    others = [dev(y, x, lax.rem(c + a, 2), lax.rem(z + b, 4)) for a in range(2) for b in range(4) if a or b] + [
        peer(*flipped(*f)) for f in flips if f[0] or f[1]
    ]
    for device in others:
        pl.semaphore_signal(barrier, inc=1, device_id=device, device_id_type=MESH)
    pl.semaphore_wait(barrier, len(others))

    def half_rows(ref):
        return lambda k: ref.at[pl.ds(k * half, half)]

    streams = (
        (half_rows(m.x_in), m.X),
        (lambda k: m.st_in, m.ST),
        (half_rows(m.dz_in), m.DZ),
    )
    to_z = 2 * c + p

    def spread_home(k):
        src, buf = streams[k]
        for cc in range(2):
            own = (q == c) & (c == cc)
            dst = buf.at[z, cc]
            rsem = m.sp_r.at[k, z, cc]

            @pl.when(own)
            def _():
                pltpu.make_async_copy(src(cc), dst, rsem).start()

            copy = remote(src(cc), dst, m.sp_s.at[k, cc], rsem, dev(y, x, cc, to_z))

            @pl.when(jnp.logical_not(own))
            def _():
                copy.start()

            homes.append((own, copy))

    def spread_own(k):
        _, buf = streams[k]
        for kk in range(2):
            i = mine[kk]
            arrived(buf.at[i, c], m.sp_r.at[k, i, c])
            push(buf.at[i, c], buf.at[i, c], m.sp_s.at[k, 2 + 2 * kk], m.sp_r.at[k, i, c], nbr)
            push(buf.at[i, c], buf.at[i, c], m.sp_s.at[k, 3 + 2 * kk], m.sp_r.at[k, i, c], sib)

    def spread_nbr(k):
        _, buf = streams[k]
        for kk in range(2):
            j = theirs[kk]
            arrived(buf.at[j, c], m.sp_r.at[k, j, c])
            push(buf.at[j, c], buf.at[j, c], m.sp_s.at[k, 6 + kk], m.sp_r.at[k, j, c], sib)

    def spread_end(k):
        _, buf = streams[k]
        for i in mine + theirs:
            arrived(buf.at[i, 1 - c], m.sp_r.at[k, i, 1 - c])

    spread_home(0)
    spread_home(1)

    for copy in loads:
        copy.wait()
    for tt in range(4):
        at = 0
        for k in range(3):
            for j in range(2):
                m.PR0[tt, 1, 0:rw, at : at + hd] = m.PR1[k, 0, 0:rw, (j * 4 + tt) * hd : (j * 4 + tt + 1) * hd]
                at += hd
        for k in range(8):
            row, at = divmod(hidden_at(k, tt) * fw, width)
            m.PR0[tt, 0, 0:rw, k * fw : (k + 1) * fw] = m.PR1[row, 1, 0:rw, at : at + fw]
    cols = 3 * two

    def pre_src(n, tt):
        if n == 0:
            return m.PR0.at[tt, 1, pl.ds(0, rw), pl.ds(0, cols)]
        if n == 1:
            return m.vec
        return m.PR0.at[tt, 0, pl.ds(0, rw), pl.ds(0, hid)]

    def rank_rows(cc, pp):
        return (yx, cc, q, pl.ds(pl.multiple_of(pp * rw, rw), rw))

    def pre_dst(n, tt):
        if n == 1:
            return m.PV.at[tt]
        return (m.WA if n == 0 else m.WU).at[rank_rows(lax.rem(tt, 2), lax.div(tt, 2))]

    pre_sent = []
    for n in (1, 0, 2):
        for d in (1, 2, 3):
            tt = lax.rem(t + d, 4)
            pre_sent.append(
                push(pre_src(n, tt), pre_dst(n, t), m.pre_s.at[n, d - 1], m.pre_r.at[n, t], mate(tt), keep=False)
            )
    local_o = pltpu.make_async_copy(m.wo, m.WOP.at[me], m.loc.at[0])
    local_o.start()
    local_d = pltpu.make_async_copy(m.wdn, m.WD.at[me], m.loc.at[1])
    local_d.start()
    m.WA[rank_rows(c, p)] = m.PR0[t, 1, 0:rw, 0:cols]
    m.WU[rank_rows(c, p)] = m.PR0[t, 0, 0:rw, 0:hid]
    m.PV[t] = m.vec[...]

    def pre_wait(n):
        for d in (1, 2, 3):
            tt = lax.rem(t + d, 4)
            arrived(pre_dst(n, tt), m.pre_r.at[n, tt])

    def piece(n, yy, xx, qq):
        if n < 2:
            return m.WA.at[yy * 2 + xx, n, qq]
        if n == 4:
            return m.WU.at[yy * 2 + xx, :, qq]
        return {2: m.VEC, 3: m.WOP, 5: m.WD}[n].at[at8(yy, xx, qq)]

    def order(n):
        return "xy" if n in (0, 2, 4) else "yx"

    def beyond(first, qq):
        return (y, 1 - x, qq) if first == "x" else (1 - y, x, qq)

    def gather_send(n, spot, k, to):
        ref = piece(n, *spot)
        push(ref, ref, m.ag_s.at[n, k], m.ag_r.at[n, at8(*spot)], over[to])

    def gather_own(group):
        for k in range(3):
            for n in group:
                gather_send(n, (y, x, q), k, ("q" + order(n))[k])

    def gather_pass(group, k):
        for n in group:
            first, second = order(n)
            spot = (y, x, 1 - q) if k == 0 else beyond(first, q if k == 1 else 1 - q)
            arrived(piece(n, *spot), m.ag_r.at[n, at8(*spot)])
            if k == 0:
                gather_send(n, spot, 3, first)
                gather_send(n, spot, 4, second)
            else:
                gather_send(n, spot, 4 + k, second)

    def gather_end(group):
        for n in group:
            second = order(n)[1]
            for a in range(2):
                for qq in range(2):
                    spot = (1 - y, a, qq) if second == "y" else (a, 1 - x, qq)
                    arrived(piece(n, *spot), m.ag_r.at[n, at8(*spot)])

    VECS, ATT, WOUT, FFN = (2,), (0, 1), (3,), (4, 5)

    def norm_one(i, h):
        xhat, _ = norm_parts(m.X[i, h].astype(F32))
        at = pl.ds(pl.multiple_of(i * rows + h * half, half), half)
        m.N1[at, :] = (xhat * m.VF[1:2] + m.VF[2:3]).astype(BF16)

    pre_wait(1)
    total = sum((m.PV[a].astype(F32) for a in range(1, 4)), m.PV[0].astype(F32))
    line = lax.broadcasted_iota(jnp.int32, (16, width), 0)
    own_vec = jnp.where(line == 5, m.vec[...].astype(F32), total)
    m.VEC[me] = own_vec.astype(BF16)
    gather_own(VECS)
    pre_wait(0)
    gather_own(ATT)
    local_o.wait()
    local_d.wait()
    pre_wait(2)
    for copy in pre_sent:
        copy.wait_send()
    gather_pass(VECS, 0)
    gather_pass(VECS, 1)
    gather_pass(VECS, 2)
    spread_own(0)
    spread_own(1)
    gather_pass(ATT, 0)
    gather_own(WOUT)
    gather_own(FFN)
    gather_end(VECS)
    every = m.VEC[0].astype(F32)
    for a in range(1, 8):
        every = every + m.VEC[a].astype(F32)
    m.VF[...] = every[0:8]
    for i in mine:
        norm_one(i, c)
    gather_pass(ATT, 1)
    spread_nbr(0)
    spread_nbr(1)
    gather_pass(ATT, 2)
    spread_home(2)
    for i in theirs:
        norm_one(i, c)
    spread_end(0)
    spread_end(1)
    for i in mine + theirs:
        norm_one(i, 1 - c)
    for k in range(3):
        gather_pass(WOUT, k)
    gather_end(ATT)

    def swap_out():
        gather_end(WOUT)
        for yy in range(2):
            for qq in range(2):
                k = yy * 2 + qq
                push(
                    m.WOP.at[at8(yy, 1 - p, qq)], m.WO.at[yy, qq, p], m.sw_s.at[k], m.sw_r.at[k], nbr
                )
                m.WO[yy, qq, p] = m.WOP[at8(yy, p, qq)]

    def swap_end():
        for yy in range(2):
            for qq in range(2):
                arrived(m.WO.at[yy, qq, 1 - p], m.sw_r.at[yy * 2 + qq])

    def row_tile(i):
        return pl.ds(pl.multiple_of(i * rows, rows), rows)

    def col_tile(n, size=256):
        return pl.ds(pl.multiple_of(n * size, size), size)

    @pl.loop(0, 3)
    def _(n):
        w = m.WA[:, :, :, :, col_tile(n)].reshape(width, 256)

        @pl.loop(0, 4)
        def _(i):
            m.QKV[row_tile(i), col_tile(n)] = dot_nn(m.N1[row_tile(i), :], w).astype(BF16)

    EX = (
        (m.PR0, m.RBa, m.RXa),
        (m.PR1, m.RBb, m.RXb),
        (m.PR0, m.RBa, m.RXc),
        (m.PR1, m.RBc, m.RXd),
    )
    ex_open = {}
    ex_far = {1: [], 3: []}

    def ex_put(e, i, cols_at, value):
        pair = EX[e][0]
        low = value.astype(BF16)
        pair[i, 0, :, cols_at] = low[0:half]
        pair[i, 1, :, cols_at] = low[half:rows]

    def ex_send(e, i):
        pair, rb, _ = EX[e]
        ex_open[e, i] = [push(pair.at[i, 1 - c], rb.at[i], m.sib_s.at[e, i], m.sib_r.at[e, i], sib, keep=False)]

    def ex_mid(e, i):
        pair, rb, rx = EX[e]
        arrived(rb.at[i], m.sib_r.at[e, i])
        pair[i, c] = (pair[i, c].astype(F32) + rb[i].astype(F32)).astype(BF16)
        if e in (0, 2):
            ex_open[e, i].append(push(pair.at[i, c], rx.at[i], m.xs.at[e, i], m.xr.at[e, i], nbr, keep=False))
        else:
            copy = remote(pair.at[i, c], rx.at[i // 2], m.xs.at[e, i], m.xr.at[e, i // 2], nbr)
            far = p != i % 2

            @pl.when(far)
            def _():
                copy.start()

            ex_far[e].append((jnp.logical_not(far), copy))

    def ex_close(e, i):
        for copy in ex_open[e, i]:
            copy.wait_send()
        ex_open[e, i] = []

    def ex_total(e, i):
        pair, _, rx = EX[e]
        arrived(rx.at[i], m.xr.at[e, i])
        return pair[i, c].astype(F32) + rx[i].astype(F32)

    PS = (m.P0, m.P1, m.P2, m.P3)

    def attend(i):
        span = (i + 1) * rows
        r0 = i * rows
        start = m.ST[i, 0][0:1, 0:1].astype(F32)
        for j in range(2):
            q = m.QKV[r0 : r0 + rows, j * hd : (j + 1) * hd]
            k = m.QKV[0:span, two + j * hd : two + (j + 1) * hd]
            s = dot_nt(q, k) * scale
            row = lax.broadcasted_iota(jnp.int32, (rows, span), 0) + r0
            col = lax.broadcasted_iota(jnp.int32, (rows, span), 1)
            s = jnp.where((col <= row) & (col.astype(F32) >= start), s, masked_value)
            e = jnp.exp(s - jnp.max(s, axis=-1, keepdims=True))
            p = (e * (1.0 / jnp.sum(e, axis=-1, keepdims=True))).astype(BF16)
            PS[i][j] = p
            v = m.QKV[0:span, 2 * two + j * hd : 2 * two + (j + 1) * hd]
            m.MIX[r0 : r0 + rows, j * hd : (j + 1) * hd] = dot_nn(p, v).astype(BF16)

        @pl.loop(0, 4)
        def _(n):
            w = m.WO[:, :, :, :, col_tile(n)].reshape(two, 256)
            ex_put(0, i, col_tile(n), dot_nn(m.MIX[r0 : r0 + rows, :], w))

        ex_send(0, i)

    def second_norm(i):
        res = m.X[i, c].astype(F32) + ex_total(0, i)
        m.RES[i] = res
        xhat, _ = norm_parts(res)
        m.N2[i, c] = (xhat * m.VF[3:4] + m.VF[4:5]).astype(BF16)
        push(m.N2.at[i, c], m.N2.at[i, c], m.n2_s.at[i], m.n2_r.at[i], sib)

    m.VSUM[...] = jnp.zeros((8, width), F32)

    def feed(n):
        tile = col_tile(n)
        w_in = m.WU[:, :, :, :, tile].reshape(width, 256)
        w_back = m.WD[pl.ds(n * (256 // fw), 256 // fw)].reshape(256, width)

        @pl.loop(0, 4)
        def _(i):
            pre = dot_nn(m.N2[i].reshape(rows, width), w_in) + m.VF[5:6, tile]
            back = dot_nt(m.DZ[i].reshape(rows, width), w_back)
            sq = pre * pre
            th = jnp.tanh(GELU_K * pre * (1.0 + GELU_C * sq))
            m.HID[row_tile(i), tile] = (0.5 * pre * (1.0 + th)).astype(BF16)
            slope = 0.5 * (1.0 + th) + 0.5 * pre * (1.0 - th * th) * (GELU_K * (1.0 + 3.0 * GELU_C * sq))
            dpre = back * slope
            m.VSUM[5:6, tile] += jnp.sum(dpre, axis=0, keepdims=True)
            m.DP[row_tile(i), tile] = dpre.astype(BF16)

    def feed_two(i):
        r0 = i * rows
        ex_close(0, i)

        @pl.loop(0, width // 256)
        def _(n):
            w = m.WU[n].reshape(256, hid)
            ex_put(2, i, col_tile(n), dot_nt(m.DP[r0 : r0 + rows, :], w))

        ex_send(2, i)

    def feed_out(i):
        r0 = i * rows

        @pl.loop(0, width // 256)
        def _(n):
            w = m.WD[:, :, col_tile(n)].reshape(hid, 256)
            ex_put(1, i, col_tile(n), dot_nn(m.HID[r0 : r0 + rows, :], w))

        ex_send(1, i)

    def feed_back(i):
        xhat, rstd = norm_parts(m.RES[i])
        g = ex_total(2, i)
        a = 0.5 * jnp.sum(g * xhat, axis=0, keepdims=True)
        b = 0.5 * jnp.sum(g, axis=0, keepdims=True)
        m.VSUM[3:4] += a
        m.VSUM[4:5] += b

        @pl.when(p == i % 2)
        def _():
            m.KEEP[i // 2] = m.RES[i]

        dres = m.DZ[i, c].astype(F32) + norm_back(g, m.VF[3:4], xhat, rstd)
        m.RES[i] = dres
        m.DB[i, c] = dres.astype(BF16)
        push(m.DB.at[i, c], m.DB.at[i, c], m.db_s.at[i], m.db_r.at[i], sib)

    def lane(ref, at):
        return ref[:, pl.ds(pl.multiple_of(at * 128, 128), 128)]

    def lane_n2(at):
        return m.N2[:, :, :, pl.ds(pl.multiple_of(at * 128, 128), 128)].reshape(4 * rows, 128)

    def flip(parts):
        for a, part in enumerate(parts):
            m.TT[a * 128 : (a + 1) * 128, :] = part.T

    SEND = (m.YSF.at[0], m.YSF.at[1], m.YSQ.at[0], m.YSQ.at[1])
    GOT1 = (m.R1F.at[0], m.R1F.at[1], m.R1Q.at[0], m.R1Q.at[1])
    GOT2 = (m.R2F.at[0], m.R2F.at[1], m.R2Q.at[0], m.R2Q.at[1])
    GOT3 = (m.R3F.at[0], m.R3F.at[1], m.R3Q.at[0], m.R3Q.at[1])
    AXES = ("yx", "xy", "yx", "xy")
    open1 = {0: [], 1: [], 2: [], 3: []}
    fh = fw // 2

    def step1(w, slots):
        for k in slots:
            open1[w].append(
                push(SEND[w].at[k], GOT1[w].at[k], m.r1_s.at[w, k], m.r1_r.at[w, k], over[AXES[w][0]], keep=False)
            )

    def up_lhs(yy):
        flip([lane_n2((yy * 2 + a // 2) * 2 + a % 2) for a in range(4)])

    def up_parts(res):
        return [
            ((a // 2) * 2 + b, (a % 2) * fh, res[a * 128 + b * fh : a * 128 + (b + 1) * fh])
            for a in range(4)
            for b in range(2)
        ]

    def far_tile(k):
        return 2 * k + 1 - x if k < 2 else 2 * (k - 2) + x

    def up_far(k):
        s = col_tile(far_tile(k))
        for slot, at, part in up_parts(dot_nn(m.TT[...], m.DP[:, s])):
            m.YSF[0, slot, at : at + fh, s] = part.astype(BF16)
        for slot in range(4):
            src, dst = m.YSF.at[0, slot, :, s], m.R1F.at[0, slot, :, s]
            open1[0].append(push(src, dst, m.up_s.at[k, slot], m.up_r.at[k, slot], over["y"], keep=False))

    def down_far(k):
        for a in range(2):
            m.TU[a * 128 : (a + 1) * 128, :] = lane(m.HID, far_tile(k) * 2 + a).T

        @pl.loop(0, width // 256)
        def _(n):
            s = col_tile(n)
            res = dot_nn(m.TU[...], m.DZ[:, :, :, s].reshape(4 * rows, 256)).astype(BF16)
            m.YSF[1, 2 * k, :, s] = res[0:fw]
            m.YSF[1, 2 * k + 1, :, s] = res[fw : 2 * fw]

        step1(1, (2 * k, 2 * k + 1))

    def qkv_lhs(yy, xx):
        flip([lane(m.N1, (yy * 2 + a) * 2) for a in range(2)] + [lane(m.N1, (a * 2 + xx) * 2 + 1) for a in range(2)])

    def qkv_parts(res):
        return [
            (a // 2, (a % 2) * 2 + b, res[a * 128 + b * fh : a * 128 + (b + 1) * fh]) for a in range(4) for b in range(2)
        ]

    def qkv_far():
        qkv_lhs(1 - y, 1 - x)

        @pl.loop(0, 3)
        def _(n):
            s = col_tile(n)
            for e, slot, part in qkv_parts(dot_nn(m.TT[...], m.QKV[:, s])):
                m.YSQ[e, slot, :, s] = part.astype(BF16)

        step1(2, range(4))
        step1(3, range(4))

    def near_wait(w):
        for copy in open1[w]:
            copy.wait_send()
        for slot in range(4):
            if w:
                arrived(GOT1[w].at[slot], m.r1_r.at[w, slot])
            else:
                for k in range(4):
                    arrived(m.R1F.at[0, slot, :, col_tile(far_tile(k))], m.up_r.at[k, slot])

    def step2(w):
        first, second = AXES[w]
        there = 1 - (x if second == "x" else y)
        for qq in range(2):
            push(
                SEND[w].at[there * 2 + qq], GOT2[w].at[qq], m.r2_s.at[w, qq], m.r2_r.at[w, qq], over[second]
            )

    def up_near():
        up_lhs(y)
        near_wait(0)

        @pl.loop(0, hid // 256)
        def _(n):
            s = col_tile(n)
            for slot, at, part in up_parts(dot_nn(m.TT[...], m.DP[:, s])):
                to = slice(at, at + fh)
                m.YSF[0, slot, to, s] = (part + m.R1F[0, slot, to, s].astype(F32)).astype(BF16)

        step2(0)

    def down_near():
        near_wait(1)
        for k in range(2):
            for a in range(2):
                m.TU[a * 128 : (a + 1) * 128, :] = lane(m.HID, far_tile(k + 2) * 2 + a).T

            @pl.loop(0, width // 256)
            def _(n):
                s = col_tile(n)
                res = dot_nn(m.TU[...], m.DZ[:, :, :, s].reshape(4 * rows, 256))
                for b in range(2):
                    got = m.R1F[1, 2 * k + b, :, s].astype(F32)
                    m.YSF[1, 2 * k + b, :, s] = (res[b * fw : (b + 1) * fw] + got).astype(BF16)

        step2(1)

    def qkv_near():
        qkv_lhs(y, x)
        near_wait(2)
        near_wait(3)

        @pl.loop(0, 3)
        def _(n):
            s = col_tile(n)
            for e, slot, part in qkv_parts(dot_nn(m.TT[...], m.QKV[:, s])):
                m.YSQ[e, slot, :, s] = (part + m.R1Q[e, slot, :, s].astype(F32)).astype(BF16)

        step2(2)
        step2(3)

    def here(w):
        return x if AXES[w][1] == "x" else y

    def grad_mid(w):
        for qq in range(2):
            arrived(GOT2[w].at[qq], m.r2_r.at[w, qq])
            slot = here(w) * 2 + qq
            SEND[w][slot] = (SEND[w][slot].astype(F32) + GOT2[w][qq].astype(F32)).astype(BF16)
        push(SEND[w].at[here(w) * 2 + 1 - q], GOT3[w], m.r3_s.at[w], m.r3_r.at[w], over["q"])

    def grad_sum(w):
        arrived(GOT3[w], m.r3_r.at[w])
        return SEND[w][here(w) * 2 + q].astype(F32) + GOT3[w][...].astype(F32)

    def out_first():
        flip([lane(m.MIX, a) for a in range(2)])

        @pl.loop(0, width // 256)
        def _(n):
            s = col_tile(n)
            res = dot_nn(m.TT[0:two, :], m.DB[:, :, :, s].reshape(4 * rows, 256)).astype(BF16)
            m.GOB[:, :, :, :, s] = res.reshape(2, 2, 2, rw, 256)

        for yy in range(2):
            for qq in range(2):
                k = yy * 2 + qq
                push(m.GOB.at[yy, qq, 1 - p], m.GOR.at[yy, qq], m.sw_s2.at[k], m.sw_r2.at[k], nbr)

    def out_second():
        for yy in range(2):
            for qq in range(2):
                arrived(m.GOR.at[yy, qq], m.sw_r2.at[yy * 2 + qq])
                m.GOS[at8(yy, p, qq)] = m.GOB[yy, qq, p]
                m.GOS[at8(yy, 1 - p, qq)] = m.GOR[yy, qq]
        for k, f in enumerate(flips):
            if k:
                spot = flipped(*f)
                push(m.GOS.at[at8(*spot)], m.GOT.at[me], m.go_s.at[k], m.go_r.at[me], peer(*spot))

    def out_sum():
        value = m.GOS[me].astype(F32)
        for k, f in enumerate(flips):
            if k:
                at = at8(*flipped(*f))
                arrived(m.GOT.at[at], m.go_r.at[at])
                value = value + m.GOT[at].astype(F32)
        m.OO[...] = value

    def give(e, src_of, dst):
        pltpu.make_async_copy(src_of(c, p), dst.at[t], m.pe_r.at[e, t]).start()
        for d in (1, 2, 3):
            tt = lax.rem(t + d, 4)
            push(src_of(lax.rem(tt, 2), lax.div(tt, 2)), dst.at[t], m.pe_s.at[e, d - 1], m.pe_r.at[e, t], mate(tt))

    def give_end():
        for e, dst in ((0, m.peu), (1, m.peq)):
            for tt in range(4):
                arrived(dst.at[tt], m.pe_r.at[e, tt])

    swap_out()
    gather_pass(FFN, 0)
    swap_end()
    attend(0)
    attend(1)
    ex_mid(0, 0)
    gather_pass(FFN, 1)
    attend(2)
    ex_mid(0, 1)
    second_norm(0)
    attend(3)
    ex_mid(0, 2)
    second_norm(1)
    ex_mid(0, 3)
    gather_pass(FFN, 2)
    spread_own(2)
    second_norm(2)
    second_norm(3)
    spread_nbr(2)
    for i in range(4):
        arrived(m.N2.at[i, 1 - c], m.n2_r.at[i])
    up_lhs(1 - y)
    spread_end(2)
    gather_end(FFN)
    for k in range(4):
        feed(far_tile(k))
        if k < 2:
            down_far(k)
        up_far(k)
    for i in range(4):
        feed_two(i)
        if i:
            ex_mid(2, i - 1)
    ex_mid(2, 3)
    for i in range(4):
        feed_out(i)
    feed_back(0)
    feed_back(1)
    for i in range(4):
        ex_mid(1, i)

    def attend_back(i):
        arrived(m.DB.at[i, 1 - c], m.db_r.at[i])
        span = (i + 1) * rows
        r0 = i * rows
        m.DMIX[...] = dot_nt(m.DB[i].reshape(rows, width), m.WO[...].reshape(two, width)).astype(BF16)
        for j in range(2):
            k0, v0 = two + j * hd, 2 * two + j * hd
            do = m.DMIX[:, j * hd : (j + 1) * hd]
            p = PS[i][j]
            pf = p.astype(F32)
            g = dot_nt(do, m.QKV[0:span, v0 : v0 + hd])
            delta = jnp.sum(pf * g, axis=-1, keepdims=True)
            ds = (pf * (g - delta) * scale).astype(BF16)
            q = m.QKV[r0 : r0 + rows, j * hd : (j + 1) * hd]
            dk = dot_tn(ds, q)
            dv = dot_tn(p, do)
            dq = dot_nn(ds, m.QKV[0:span, k0 : k0 + hd])
            ka, va = slice(j * hd, (j + 1) * hd), slice(two + j * hd, two + (j + 1) * hd)
            if i:
                m.ACC[0:r0, ka] += dk[0:r0]
                m.ACC[0:r0, va] += dv[0:r0]
            m.ACC[r0:span, ka] = dk[r0:span]
            m.ACC[r0:span, va] = dv[r0:span]
            m.QKV[r0 : r0 + rows, j * hd : (j + 1) * hd] = dq.astype(BF16)

    def give_back(k, kk, buf, dst):
        i = mine[kk]
        near = (q == c) & (i == z)
        to = dst.at[pl.ds(pl.multiple_of(c * half, half), half)]
        rsem = m.ret_r.at[k, c]

        @pl.when(near)
        def _():
            pltpu.make_async_copy(buf.at[kk], to, rsem).start()

        copy = remote(buf.at[kk], to, m.ret_s.at[k, kk], rsem, dev(y, x, q, i))

        @pl.when(jnp.logical_not(near))
        def _():
            copy.start()

        homes.append((near, copy))

    def far_close(e):
        for near, copy in ex_far.pop(e):

            @pl.when(jnp.logical_not(near))
            def _():
                copy.wait_send()

    def finish_out(kk):
        i = mine[kk]
        arrived(m.RXb.at[kk], m.xr.at[1, kk])
        value = m.KEEP[kk] + m.PR1[i, c].astype(F32) + m.RXb[kk].astype(F32) + m.VF[0:1]
        m.OUTB[kk] = value.astype(BF16)
        give_back(0, kk, m.OUTB, m.out)

    def first_back(i):
        r0 = i * rows

        @pl.loop(0, width // 256)
        def _(n):
            w = m.WA[n].reshape(256, cols)
            ex_put(3, i, col_tile(n), dot_nt(m.QKV[r0 : r0 + rows, :], w))

        ex_send(3, i)

    def finish_in(kk):
        i = mine[kk]
        arrived(m.RXd.at[kk], m.xr.at[3, kk])
        g = m.PR1[i, c].astype(F32) + m.RXd[kk].astype(F32)
        xhat, rstd = norm_parts(m.X[i, c].astype(F32))
        parts = (
            jnp.sum(m.DZ[i, c].astype(F32), axis=0, keepdims=True),
            jnp.sum(g * xhat, axis=0, keepdims=True),
            jnp.sum(g, axis=0, keepdims=True),
        )
        for k, part in enumerate(parts):
            m.VSUM[k : k + 1] += part
        m.IGB[kk] = (m.RES[i] + norm_back(g, m.VF[1:2], xhat, rstd)).astype(BF16)
        give_back(1, kk, m.IGB, m.ig)

    attend_back(0)
    feed_back(2)
    attend_back(1)
    feed_back(3)
    finish_out(0)
    finish_out(1)
    attend_back(2)
    down_near()
    attend_back(3)

    @pl.loop(0, 4)
    def _(i):
        m.QKV[row_tile(i), two : 3 * two] = m.ACC[row_tile(i), :].astype(BF16)

    qkv_far()
    out_first()
    up_near()
    far_close(1)
    for i in range(4):
        ex_close(1, i)
    for i in range(4):
        first_back(i)
        if i:
            ex_mid(3, i - 1)
    grad_mid(1)
    ex_mid(3, 3)
    out_second()
    grad_mid(0)
    finish_in(0)
    finish_in(1)

    for d in (1, 2, 3):
        tt = lax.rem(t + d, 4)
        push(m.VSUM, m.VR1.at[t], m.v1_s.at[d - 1], m.v1_r.at[t], mate(tt))
    qkv_near()
    rest = m.VSUM[...]
    for d in (1, 2, 3):
        tt = lax.rem(t + d, 4)
        arrived(m.VR1.at[tt], m.v1_r.at[tt])
        rest = rest + m.VR1[tt]
    row8 = lax.broadcasted_iota(jnp.int32, (8, width), 0)
    m.VMID[...] = jnp.where(row8 == 5, m.VSUM[...], rest)
    for k, f in enumerate(flips):
        if k:
            push(m.VMID, m.VR2.at[me], m.v2_s.at[k - 1], m.v2_r.at[me], peer(*flipped(*f)))
    m.OD[...] = grad_sum(1)
    keep_down = pltpu.make_async_copy(m.OD, m.gdn, m.loc.at[2])
    keep_down.start()
    m.FIU[...] = grad_sum(0).astype(BF16)
    give(0, lambda cc, pp: m.FIU.at[pl.ds(pl.multiple_of((cc * 2 + pp) * rw, rw), rw)], m.peu)
    grad_mid(2)
    grad_mid(3)
    out_sum()
    keep_out = pltpu.make_async_copy(m.OO, m.go, m.loc.at[3])
    keep_out.start()
    for e in range(2):
        m.FIN[e] = grad_sum(2 + e).astype(BF16)
    give(1, lambda cc, pp: m.FIN.at[cc, pl.ds(pl.multiple_of(pp * rw, rw), rw)], m.peq)
    final = m.VMID[...]
    for k, f in enumerate(flips):
        if k:
            at = at8(*flipped(*f))
            arrived(m.VR2.at[at], m.v2_r.at[at])
            final = final + m.VR2[at]
    m.gvec[...] = final

    for k, dst in enumerate((m.out, m.ig)):
        for cc in range(2):
            arrived(dst.at[pl.ds(cc * half, half)], m.ret_r.at[k, cc])
    give_end()
    keep_down.wait()
    keep_out.wait()
    for copy in sent:
        copy.wait_send()
    for e, i in ex_open:
        ex_close(e, i)
    far_close(3)
    for near, copy in homes:

        @pl.when(jnp.logical_not(near))
        def _():
            copy.wait_send()


def place_outputs(out_i, ig_i, peq, peu, go_i, gdn_i, out, ig, gq, gk, gv, go, gup, gdn, PQ, PU, GQ, GU, A, B, GO, GD, sem):
    pairs = ((peq, PQ), (peu, PU), (out_i, A), (ig_i, B), (go_i, GO), (gdn_i, GD))
    moves = [pltpu.make_async_copy(src, dst, sem.at[k]) for k, (src, dst) in enumerate(pairs)]
    for move in moves:
        move.start()
    results = ((A, out), (B, ig), (GO, go), (GD, gdn), (GQ.at[0], gq), (GQ.at[1], gk), (GQ.at[2], gv), (GU, gup))
    last = [pltpu.make_async_copy(src, dst, sem.at[6 + k]) for k, (src, dst) in enumerate(results)]
    hd = PQ.shape[2] // 6
    fw = PU.shape[2] // 8
    moves[0].wait()
    moves[1].wait()
    for tt in range(RANKS):
        for j in range(2):
            a = (j * RANKS + tt) * hd
            for n in range(3):
                GQ[n, :, a : a + hd] = PQ[tt, :, (n * 2 + j) * hd : (n * 2 + j + 1) * hd].astype(F32)
        for k in range(8):
            a = hidden_at(k, tt) * fw
            GU[:, a : a + fw] = PU[tt, :, k * fw : (k + 1) * fw].astype(F32)
    for k in range(4):
        last[4 + k].start()
    for k in range(4):
        moves[2 + k].wait()
        last[k].start()
    for move in last:
        move.wait()


def call_fused(inputs, positions, w_query, w_key, w_value, w_out, w_up, w_down, up_bias, down_bias,
               ln1_gain, ln1_bias, ln2_gain, ln2_bias, cotangent):
    rows, width = inputs.shape
    hid = w_up.shape[1] // RANKS
    rw, fw = w_query.shape[0], w_down.shape[0]
    shapes = scratch_of(rows, width, hid, rw, fw)
    dp, blk = lax.axis_index("dp"), lax.axis_index("blk")
    n_blk = lax.axis_size("blk")
    place = dp * n_blk + blk
    at_up = dp // 2 * 2 + blk // 2
    small_in = [v.reshape(1, -1) for v in (down_bias, ln1_gain, ln1_bias, ln2_gain, ln2_bias, up_bias)]
    names = IN_NAMES + OUT_NAMES + tuple(shapes)
    any_, vm = pl.BlockSpec(memory_space=pl.ANY), pl.BlockSpec(memory_space=pltpu.VMEM)
    S = jax.ShapeDtypeStruct
    cols = 3 * 2 * (width // HEADS)
    tokens, wide = S((rows, width), BF16), S((rw, width), F32)
    moved = (S((RANKS, rw, cols), BF16), S((RANKS, rw, hid), BF16))
    out, ig, peq, peu, go, gdn, gvec = pl.pallas_call(
        functools.partial(fused, names),
        out_shape=(tokens, tokens) + moved + (wide, S(w_down.shape, F32), S((8, width), F32)),
        in_specs=[any_, any_, vm] + [any_] * 6 + [vm] * 6,
        out_specs=[any_] * 6 + [vm],
        scratch_shapes=list(shapes.values()),
        compiler_params=pltpu.CompilerParams(
            collective_id=0, has_side_effects=True, vmem_limit_bytes=VMEM_BYTES
        ),
        cost_estimate=pl.CostEstimate(flops=23 * 10**9, bytes_accessed=10**7, transcendentals=10**6),
    )(inputs, cotangent, positions.reshape(2, -1), w_query, w_key, w_value, w_out, w_up, w_down, *small_in)
    out, ig, gq, gk, gv, go, gup, gdn = pl.pallas_call(
        place_outputs,
        out_shape=(tokens, tokens, wide, wide, wide, wide, S(w_up.shape, F32), S(w_down.shape, F32)),
        in_specs=[any_] * 6,
        out_specs=[any_] * 8,
        scratch_shapes=[
            pltpu.VMEM(moved[0].shape, BF16),
            pltpu.VMEM(moved[1].shape, BF16),
            pltpu.VMEM((3, rw, width), F32),
            pltpu.VMEM(w_up.shape, F32),
            pltpu.VMEM((rows, width), BF16),
            pltpu.VMEM((rows, width), BF16),
            pltpu.VMEM((rw, width), F32),
            pltpu.VMEM(w_down.shape, F32),
            pltpu.SemaphoreType.DMA((14,)),
        ],
        compiler_params=pltpu.CompilerParams(vmem_limit_bytes=VMEM_BYTES),
    )(out, ig, peq, peu, go, gdn)
    small = lax.dynamic_slice(gvec, (0, place * rw), (5, rw))
    gup_bias = lax.dynamic_slice(gvec, (5, at_up * fw), (1, fw))[0]
    return (out, ig, gq, gk, gv, go, gup, gdn, gup_bias, small[0], small[1], small[2], small[3], small[4])


def layer_norm(values, gain, offset):
    centre = jnp.mean(values, axis=-1, keepdims=True)
    centred = values - centre
    variance = jnp.mean(centred * centred, axis=-1, keepdims=True)
    return centred * lax.rsqrt(variance + eps) * gain + offset


def smooth_gate(values):
    return jax.nn.gelu(values, approximate=True)


def keep_same(carry):
    return carry


def local(
    inputs,
    positions,
    w_query,
    w_key,
    w_value,
    w_out,
    w_up,
    w_down,
    up_bias,
    down_bias,
    ln1_gain,
    ln1_bias,
    ln2_gain,
    ln2_bias,
    cotangent,
):
    attn_full = (
        lax.all_gather(w_query, ("dp", "blk"), axis=0, tiled=True),
        lax.all_gather(w_key, ("dp", "blk"), axis=0, tiled=True),
        lax.all_gather(w_value, ("dp", "blk"), axis=0, tiled=True),
        lax.all_gather(w_out, ("dp", "blk"), axis=0, tiled=True),
        lax.all_gather(ln1_gain, ("dp", "blk"), axis=0, tiled=True),
        lax.all_gather(ln1_bias, ("dp", "blk"), axis=0, tiled=True),
    )
    ffn_full = (
        lax.all_gather(w_up, ("dp", "blk"), axis=0, tiled=True),
        lax.all_gather(w_down, ("dp", "blk"), axis=0, tiled=True),
        lax.all_gather(up_bias, ("dp", "blk"), axis=0, tiled=True),
        lax.all_gather(down_bias, ("dp", "blk"), axis=0, tiled=True),
        lax.all_gather(ln2_gain, ("dp", "blk"), axis=0, tiled=True),
        lax.all_gather(ln2_bias, ("dp", "blk"), axis=0, tiled=True),
    )
    token_rows = inputs.astype(jnp.float32)
    local_rows, model_width = token_rows.shape
    head_count = HEADS
    head_size = model_width // head_count
    score_scale = 1.0 / math.sqrt(head_size)
    normed_first, first_pull = jax.vjp(
        layer_norm, token_rows, attn_full[4].astype(jnp.float32), attn_full[5].astype(jnp.float32)
    )
    normed_low = normed_first.astype(jnp.bfloat16)
    query_low = jnp.dot(normed_low, attn_full[0], preferred_element_type=jnp.float32).astype(
        jnp.bfloat16
    )
    key_low = jnp.dot(normed_low, attn_full[1], preferred_element_type=jnp.float32).astype(
        jnp.bfloat16
    )
    value_low = jnp.dot(normed_low, attn_full[2], preferred_element_type=jnp.float32).astype(
        jnp.bfloat16
    )
    keys_all, values_all = (
        lax.all_gather(key_low, "blk", axis=0, tiled=True),
        lax.all_gather(value_low, "blk", axis=0, tiled=True),
    )
    group_rows = keys_all.shape[0]
    key_rows = max(min(512, group_rows), local_rows)
    block_count = group_rows // key_rows
    first_row = lax.axis_index("blk") * local_rows
    query_index = first_row + jnp.arange(local_rows, dtype=jnp.int32)
    seq_start = query_index - positions
    earliest = jnp.min(seq_start)
    query_heads = query_low.reshape(local_rows, head_count, head_size)
    key_parts = []
    for which in range(block_count):
        begin = which * key_rows
        key_part = keys_all[begin : begin + key_rows].reshape(key_rows, head_count, head_size)
        value_part = values_all[begin : begin + key_rows].reshape(key_rows, head_count, head_size)
        key_index = begin + jnp.arange(key_rows, dtype=jnp.int32)
        allowed = (key_index[None, :] <= query_index[:, None]) & (
            key_index[None, :] >= seq_start[:, None]
        )
        needed = (begin <= first_row + local_rows - 1) & (begin + key_rows - 1 >= earliest)
        key_parts.append((key_part, value_part, allowed, needed))

    def scores_of(key_part, allowed):
        scores = (
            jnp.einsum("qhd,khd->hqk", query_heads, key_part, preferred_element_type=jnp.float32)
            * score_scale
        )
        return jnp.where(allowed[None], scores, masked_value)

    running_max = jnp.full((head_count, local_rows), masked_value, jnp.float32)
    running_sum = jnp.zeros((head_count, local_rows), jnp.float32)
    for key_part, value_part, allowed, needed in key_parts:

        def extend(carry):
            old_max, old_sum = carry
            scores = scores_of(key_part, allowed)
            new_max = jnp.maximum(old_max, jnp.max(scores, axis=-1))
            terms = jnp.where(allowed[None], jnp.exp(scores - new_max[..., None]), 0.0)
            return (new_max, old_sum * jnp.exp(old_max - new_max) + jnp.sum(terms, axis=-1))

        running_max, running_sum = lax.cond(needed, extend, keep_same, (running_max, running_sum))
    log_total = running_max + jnp.log(running_sum)

    def probs_of(key_part, allowed):
        scores = scores_of(key_part, allowed)
        return jnp.where(allowed[None], jnp.exp(scores - log_total[..., None]), 0.0)

    attended = jnp.zeros((local_rows, head_count, head_size), jnp.float32)
    for key_part, value_part, allowed, needed in key_parts:

        def gather_values(total):
            weights_low = probs_of(key_part, allowed).astype(jnp.bfloat16)
            return total + jnp.einsum(
                "hqk,khd->qhd", weights_low, value_part, preferred_element_type=jnp.float32
            )

        attended = lax.cond(needed, gather_values, keep_same, attended)
    mixed_low = attended.reshape(local_rows, model_width).astype(jnp.bfloat16)
    residual = token_rows + jnp.dot(mixed_low, attn_full[3], preferred_element_type=jnp.float32)
    normed_second, second_pull = jax.vjp(
        layer_norm, residual, ffn_full[4].astype(jnp.float32), ffn_full[5].astype(jnp.float32)
    )
    normed_two = normed_second.astype(jnp.bfloat16)
    preact = jnp.dot(normed_two, ffn_full[0], preferred_element_type=jnp.float32) + ffn_full[
        2
    ].astype(jnp.float32)
    gated, gate_pull = jax.vjp(smooth_gate, preact)
    hidden = gated.astype(jnp.bfloat16)
    output = (
        residual
        + jnp.dot(hidden, ffn_full[1], preferred_element_type=jnp.float32)
        + ffn_full[3].astype(jnp.float32)
    ).astype(jnp.bfloat16)
    up_back, down_back = (ffn_full[0], ffn_full[1])
    grad_final = cotangent.astype(jnp.float32)
    grad_down_w = jnp.einsum("tf,td->fd", hidden, cotangent, preferred_element_type=jnp.float32)
    grad_down_shift = jnp.sum(grad_final, axis=0)
    grad_hidden = jnp.einsum("td,fd->tf", cotangent, down_back, preferred_element_type=jnp.float32)
    grad_preact = gate_pull(grad_hidden)[0].astype(jnp.bfloat16)
    grad_up_shift = jnp.sum(grad_preact.astype(jnp.float32), axis=0)
    grad_up_w = jnp.einsum("td,tf->df", normed_two, grad_preact, preferred_element_type=jnp.float32)
    grad_normed_two = jnp.einsum(
        "tf,df->td", grad_preact, up_back, preferred_element_type=jnp.float32
    )
    grad_resid_two, grad_gain_two, grad_shift_two = second_pull(grad_normed_two)
    grad_residual = grad_final + grad_resid_two
    query_back, key_back, value_back, out_back = (
        attn_full[0],
        attn_full[1],
        attn_full[2],
        attn_full[3],
    )
    grad_branch = grad_residual.astype(jnp.bfloat16)
    grad_out_w = jnp.einsum("te,td->ed", mixed_low, grad_branch, preferred_element_type=jnp.float32)
    grad_mixed = jnp.einsum(
        "td,ed->te", grad_branch, out_back, preferred_element_type=jnp.float32
    ).astype(jnp.bfloat16)
    grad_heads = grad_mixed.reshape(local_rows, head_count, head_size)
    delta = jnp.zeros((head_count, local_rows), jnp.float32)
    for key_part, value_part, allowed, needed in key_parts:

        def add_delta(total):
            probs = probs_of(key_part, allowed)
            grad_probs = jnp.einsum(
                "qhd,khd->hqk", grad_heads, value_part, preferred_element_type=jnp.float32
            )
            return total + jnp.sum(probs * grad_probs, axis=-1)

        delta = lax.cond(needed, add_delta, keep_same, delta)
    grad_query_sum = jnp.zeros((local_rows, head_count, head_size), jnp.float32)
    kv_terms = []
    for key_part, value_part, allowed, needed in key_parts:

        def backward_part(total):
            probs = probs_of(key_part, allowed)
            grad_probs = jnp.einsum(
                "qhd,khd->hqk", grad_heads, value_part, preferred_element_type=jnp.float32
            )
            grad_scores = (probs * (grad_probs - delta[..., None]) * score_scale).astype(
                jnp.bfloat16
            )
            new_total = total + jnp.einsum(
                "hqk,khd->qhd", grad_scores, key_part, preferred_element_type=jnp.float32
            )
            grad_keys = jnp.einsum(
                "hqk,qhd->khd", grad_scores, query_heads, preferred_element_type=jnp.float32
            ).reshape(key_rows, model_width)
            grad_values = jnp.einsum(
                "hqk,qhd->khd",
                probs.astype(jnp.bfloat16),
                grad_heads,
                preferred_element_type=jnp.float32,
            ).reshape(key_rows, model_width)
            return (new_total, jnp.concatenate([grad_keys, grad_values], axis=1))

        def skip_part(total):
            return (total, jnp.zeros((key_rows, 2 * model_width), jnp.float32))

        grad_query_sum, kv_term = lax.cond(needed, backward_part, skip_part, grad_query_sum)
        kv_terms.append(kv_term)
    kv_shares = lax.psum_scatter(
        jnp.concatenate(kv_terms, axis=0).astype(jnp.bfloat16),
        "blk",
        scatter_dimension=0,
        tiled=True,
    ).astype(jnp.float32)
    grad_key_low = kv_shares[:, :model_width].astype(jnp.bfloat16)
    grad_value_low = kv_shares[:, model_width:].astype(jnp.bfloat16)
    grad_query_low = grad_query_sum.reshape(local_rows, model_width).astype(jnp.bfloat16)
    grad_query_w = jnp.einsum(
        "td,te->de", normed_low, grad_query_low, preferred_element_type=jnp.float32
    )
    grad_key_w = jnp.einsum(
        "td,te->de", normed_low, grad_key_low, preferred_element_type=jnp.float32
    )
    grad_value_w = jnp.einsum(
        "td,te->de", normed_low, grad_value_low, preferred_element_type=jnp.float32
    )
    grad_normed = (
        jnp.einsum("te,de->td", grad_query_low, query_back, preferred_element_type=jnp.float32)
        + jnp.einsum("te,de->td", grad_key_low, key_back, preferred_element_type=jnp.float32)
        + jnp.einsum("te,de->td", grad_value_low, value_back, preferred_element_type=jnp.float32)
    )
    grad_rows_one, grad_gain_one, grad_shift_one = first_pull(grad_normed)
    input_grad = (grad_residual + grad_rows_one).astype(jnp.bfloat16)
    shares = (
        lax.psum_scatter(grad_query_w, ("dp", "blk"), scatter_dimension=0, tiled=True),
        lax.psum_scatter(grad_key_w, ("dp", "blk"), scatter_dimension=0, tiled=True),
        lax.psum_scatter(grad_value_w, ("dp", "blk"), scatter_dimension=0, tiled=True),
        lax.psum_scatter(grad_out_w, ("dp", "blk"), scatter_dimension=0, tiled=True),
        lax.psum_scatter(grad_up_w, ("dp", "blk"), scatter_dimension=0, tiled=True),
        lax.psum_scatter(grad_down_w, ("dp", "blk"), scatter_dimension=0, tiled=True),
        lax.psum_scatter(grad_up_shift, ("dp", "blk"), scatter_dimension=0, tiled=True),
        lax.psum_scatter(grad_down_shift, ("dp", "blk"), scatter_dimension=0, tiled=True),
        lax.psum_scatter(grad_gain_one, ("dp", "blk"), scatter_dimension=0, tiled=True),
        lax.psum_scatter(grad_shift_one, ("dp", "blk"), scatter_dimension=0, tiled=True),
        lax.psum_scatter(grad_gain_two, ("dp", "blk"), scatter_dimension=0, tiled=True),
        lax.psum_scatter(grad_shift_two, ("dp", "blk"), scatter_dimension=0, tiled=True),
    )
    return (
        output,
        input_grad,
        shares[0],
        shares[1],
        shares[2],
        shares[3],
        shares[4],
        shares[5],
        shares[6],
        shares[7],
        shares[8],
        shares[9],
        shares[10],
        shares[11],
    )


def solution(mesh):
    in_specs = (
        P(("dp", "blk"), None),
        P(("dp", "blk")),
        P(("dp", "blk"), None),
        P(("dp", "blk"), None),
        P(("dp", "blk"), None),
        P(("dp", "blk"), None),
        P(("dp", "blk"), None),
        P(("dp", "blk"), None),
        P(("dp", "blk")),
        P(("dp", "blk")),
        P(("dp", "blk")),
        P(("dp", "blk")),
        P(("dp", "blk")),
        P(("dp", "blk")),
        P(("dp", "blk"), None),
    )
    out_specs = (
        P(("dp", "blk"), None),
        P(("dp", "blk"), None),
        P(("dp", "blk"), None),
        P(("dp", "blk"), None),
        P(("dp", "blk"), None),
        P(("dp", "blk"), None),
        P(("dp", "blk"), None),
        P(("dp", "blk"), None),
        P(("dp", "blk")),
        P(("dp", "blk")),
        P(("dp", "blk")),
        P(("dp", "blk")),
        P(("dp", "blk")),
        P(("dp", "blk")),
    )
    n_dp, n_blk = mesh.shape["dp"], mesh.shape["blk"]

    def layer(*args):
        fits = n_blk == RANKS and n_dp == 2 * RANKS and args[2].shape[0] // (n_dp * n_blk) % 16 == 0
        call = jax.shard_map(
            call_fused if fits else local, mesh=mesh, in_specs=in_specs, out_specs=out_specs, check_vma=False
        )
        return call(*args)

    return layer
```

```python
import functools
import math
import types

import jax
import jax.numpy as jnp
from jax import lax
from jax.experimental import pallas as pl
from jax.experimental.pallas import tpu as pltpu
from jax.sharding import PartitionSpec as P

MESH = pl.DeviceIdType.MESH
F32 = jnp.float32
BF16 = jnp.bfloat16
HEADS = 8
VMEM_BYTES = 60 * 2**20
RANKS = 4
eps = 1e-05
masked_value = -1e30
GELU_K = math.sqrt(2.0 / math.pi)
GELU_C = 0.044715


def dot_nn(a, b):
    return lax.dot_general(a, b, (((1,), (0,)), ((), ())), preferred_element_type=F32)


def dot_nt(a, b):
    return lax.dot_general(a, b, (((1,), (1,)), ((), ())), preferred_element_type=F32)


def dot_tn(a, b):
    return lax.dot_general(a, b, (((0,), (0,)), ((), ())), preferred_element_type=F32)


def norm_parts(v):
    centre = jnp.mean(v, axis=-1, keepdims=True)
    centred = v - centre
    variance = jnp.mean(centred * centred, axis=-1, keepdims=True)
    rstd = lax.rsqrt(variance + eps)
    return centred * rstd, rstd


def norm_back(g, gain, xhat, rstd):
    e = g * gain
    return rstd * (
        e
        - jnp.mean(e, axis=-1, keepdims=True)
        - xhat * jnp.mean(e * xhat, axis=-1, keepdims=True)
    )


def hidden_at(k, tt):
    return ((k // 2) * 2 + tt % 2) * 4 + (k % 2) * 2 + tt // 2


IN_NAMES = ("x_in", "dz_in", "pos", "wq", "wk", "wv", "wo", "wup", "wdn", "db", "g1", "b1", "g2", "b2", "ub")
OUT_NAMES = ("out", "ig", "peq", "peu", "go", "gdn", "gvec")


def scratch_of(rows, width, hid, rw, fw):
    half = rows // 2
    hd = width // HEADS
    cols = 3 * 2 * hd
    dma = pltpu.SemaphoreType.DMA
    V = pltpu.VMEM
    names = dict(
        X=V((4, 2, half, width), BF16),
        DZ=V((4, 2, half, width), BF16),
        ST=V((4, 2, 16, 128), BF16),
        WA=V((4, 2, 2, 2 * rw, cols), BF16),
        WOP=V((8, rw, width), BF16),
        WO=V((2, 2, 2, rw, width), BF16),
        VEC=V((8, 16, width), BF16),
        WU=V((4, 2, 2, 2 * rw, hid), BF16),
        WD=V((8, fw, width), BF16),
        PV=V((4, 16, width), BF16),
        VF=V((8, width), F32),
        SV=V((8, rw), F32),
        VT=V((16, width), F32),
        vec=V((16, width), BF16),
        st_in=V((16, 128), BF16),
        TU=V((256, 4 * rows), BF16),
        N1=V((4 * rows, width), BF16),
        QKV=V((4 * rows, cols), BF16),
        P0=V((2, rows, rows), BF16),
        P1=V((2, rows, 2 * rows), BF16),
        P2=V((2, rows, 3 * rows), BF16),
        P3=V((2, rows, 4 * rows), BF16),
        MIX=V((4 * rows, 2 * hd), BF16),
        DMIX=V((rows, 2 * hd), BF16),
        PR0=V((4, 2, half, width), BF16),
        PR1=V((4, 2, half, width), BF16),
        RBa=V((4, half, width), BF16),
        RBb=V((4, half, width), BF16),
        RBc=V((4, half, width), BF16),
        RXa=V((4, half, width), BF16),
        RXb=V((2, half, width), BF16),
        RXc=V((4, half, width), BF16),
        RXd=V((2, half, width), BF16),
        RES=V((4, half, width), F32),
        KEEP=V((2, half, width), F32),
        N2=V((4, 2, half, width), BF16),
        HID=V((4 * rows, hid), BF16),
        DP=V((4 * rows, hid), BF16),
        DB=V((4, 2, half, width), BF16),
        ACC=V((4 * rows, 4 * hd), F32),
        TT=V((width // 2, 4 * rows), BF16),
        YSF=V((2, 4, fw, width), BF16),
        R1F=V((2, 4, fw, width), BF16),
        R2F=V((2, 2, fw, width), BF16),
        R3F=V((2, fw, width), BF16),
        YSQ=V((2, 4, 2 * rw, cols), BF16),
        R1Q=V((2, 4, 2 * rw, cols), BF16),
        R2Q=V((2, 2, 2 * rw, cols), BF16),
        R3Q=V((2, 2 * rw, cols), BF16),
        GOB=V((2, 2, 2, rw, width), BF16),
        GOR=V((2, 2, rw, width), BF16),
        GOS=V((8, rw, width), BF16),
        GOT=V((8, rw, width), BF16),
        OD=V((fw, width), F32),
        OO=V((rw, width), F32),
        OUTB=V((2, half, width), BF16),
        IGB=V((2, half, width), BF16),
        VSUM=V((8, width), F32),
        VMID=V((8, width), F32),
        VR1=V((4, 8, width), F32),
        VR2=V((8, 8, width), F32),
        sp_s=dma((3, 8)),
        sp_r=dma((3, 4, 2)),
        loc=dma((4,)),
        load=dma((7,)),
        pre_s=dma((3, 3)),
        pre_r=dma((3, 4)),
        ag_s=dma((6, 7)),
        ag_r=dma((6, 8)),
        sw_s=dma((4,)),
        sw_r=dma((4,)),
        sw_s2=dma((4,)),
        sw_r2=dma((4,)),
        FIN=V((2, 2 * rw, cols), BF16),
        FIU=V((fw, hid), BF16),
        sib_s=dma((4, 4)),
        sib_r=dma((4, 4)),
        xs=dma((4, 4)),
        xr=dma((4, 4)),
        n2_s=dma((4,)),
        n2_r=dma((4,)),
        db_s=dma((4,)),
        db_r=dma((4,)),
        r1_s=dma((4, 4)),
        r1_r=dma((4, 4)),
        up_s=dma((4, 4)),
        up_r=dma((4, 4)),
        r2_s=dma((4, 2)),
        r2_r=dma((4, 2)),
        r3_s=dma((4,)),
        r3_r=dma((4,)),
        go_s=dma((8,)),
        go_r=dma((8,)),
        pe_s=dma((2, 4)),
        pe_r=dma((2, 4)),
        v1_s=dma((3,)),
        v1_r=dma((4,)),
        v2_s=dma((7,)),
        v2_r=dma((8,)),
        ret_s=dma((2, 2)),
        ret_r=dma((2, 2)),
    )
    return names


def fused(names, *all_refs):
    m = types.SimpleNamespace(**dict(zip(names, all_refs)))
    half, width = m.X.shape[2:]
    rows = 2 * half
    hid = m.HID.shape[1]
    rw = m.WOP.shape[1]
    fw = m.WD.shape[1]
    hd = width // HEADS
    two = 2 * hd
    scale = 1.0 / math.sqrt(hd)

    dp = lax.axis_index("dp")
    z = lax.axis_index("blk")
    yx = lax.div(dp, 2)
    y, x, c = lax.div(dp, 4), lax.rem(yx, 2), lax.rem(dp, 2)
    q, p = lax.div(z, 2), lax.rem(z, 2)
    t = p * 2 + c
    me = yx * 2 + q

    def dev(yy, xx, cc, zz):
        return ((yy * 2 + xx) * 2 + cc, zz)

    def mate(tt):
        return dev(y, x, lax.rem(tt, 2), q * 2 + lax.div(tt, 2))

    def peer(yy, xx, qq):
        return dev(yy, xx, c, qq * 2 + p)

    def at8(yy, xx, qq):
        return yy * 4 + xx * 2 + qq

    sib = dev(y, x, 1 - c, z)
    nbr = dev(y, x, c, q * 2 + 1 - p)
    over = {"q": peer(y, x, 1 - q), "x": peer(y, 1 - x, q), "y": peer(1 - y, x, q)}

    mine = (p, p + 2)
    theirs = (1 - p, 3 - p)

    sent = []

    def remote(src, dst, ssem, rsem, device):
        return pltpu.make_async_remote_copy(
            src_ref=src,
            dst_ref=dst,
            send_sem=ssem,
            recv_sem=rsem,
            device_id=device,
            device_id_type=MESH,
        )

    def push(src, dst, ssem, rsem, device, keep=True):
        copy = remote(src, dst, ssem, rsem, device)
        copy.start()
        if keep:
            sent.append(copy)
        return copy

    homes = []

    def push_if(cond, src, dst, ssem, rsem, device):
        copy = remote(src, dst, ssem, rsem, device)

        @pl.when(cond)
        def _():
            copy.start()

        homes.append((jnp.logical_not(cond), copy))

    def arrived(dst, rsem):
        pltpu.make_async_copy(dst, dst, rsem).wait()

    loads = [pltpu.make_async_copy(ref, m.PR1.at[k, 0, pl.ds(0, rw)], m.load.at[k]) for k, ref in enumerate((m.wq, m.wk, m.wv))]
    loads += [
        pltpu.make_async_copy(m.wup.at[:, pl.ds(k * width, width)], m.PR1.at[k, 1, pl.ds(0, rw)], m.load.at[3 + k])
        for k in range(4)
    ]
    for copy in loads:
        copy.start()
    m.st_in[...] = jnp.broadcast_to((z * rows - m.pos[0:1, 0:1]).astype(F32), (16, 128)).astype(BF16)
    for k, ref in enumerate((m.db, m.g1, m.b1, m.g2, m.b2)):
        m.SV[k : k + 1] = ref[...].astype(F32)
    m.SV[5:8] = jnp.zeros((3, rw), F32)
    spot = lax.broadcasted_iota(jnp.int32, (rw, width), 1) - (dp * 4 + z) * rw
    hot = jnp.where(spot == lax.broadcasted_iota(jnp.int32, (rw, width), 0), 1.0, 0.0).astype(BF16)
    m.VT[0:8] = dot_nn(m.SV[...].astype(BF16), hot)
    m.VT[8:16] = jnp.zeros((8, width), F32)
    m.VT[5:6, pl.ds(pl.multiple_of(me * fw, 128), fw)] = m.ub[...].astype(F32)
    m.vec[...] = m.VT[...].astype(BF16)

    barrier = pltpu.get_barrier_semaphore()
    flips = [(a, b, d) for a in range(2) for b in range(2) for d in range(2)]

    def flipped(a, b, d):
        return ((1 - y if a else y), (1 - x if b else x), (1 - q if d else q))

    others = [dev(y, x, lax.rem(c + a, 2), lax.rem(z + b, 4)) for a in range(2) for b in range(4) if a or b] + [
        peer(*flipped(*f)) for f in flips if f[0] or f[1]
    ]
    for device in others:
        pl.semaphore_signal(barrier, inc=1, device_id=device, device_id_type=MESH)
    pl.semaphore_wait(barrier, len(others))

    def half_rows(ref):
        return lambda k: ref.at[pl.ds(k * half, half)]

    streams = (
        (half_rows(m.x_in), m.X),
        (lambda k: m.st_in, m.ST),
        (half_rows(m.dz_in), m.DZ),
    )
    to_z = 2 * c + p

    def spread_home(k, stays):
        src, buf = streams[k]
        for cc in range(2):
            dst = buf.at[z, cc]
            rsem = m.sp_r.at[k, z, cc]
            copy = remote(src(cc), dst, m.sp_s.at[k, cc], rsem, dev(y, x, cc, to_z))
            if stays:

                @pl.when((q == c) & (c == cc))
                def _():
                    pltpu.make_async_copy(src(cc), dst, rsem).start()

                @pl.when((q == c) & (c != cc))
                def _():
                    copy.start()

                homes.append(((q == c) & (c == cc), copy))
            else:

                @pl.when(q != c)
                def _():
                    copy.start()

    held = (z, lax.rem(z + 2, 4))
    beside = (2 * q + 1 - p, lax.rem(2 * q + 3 - p, 4))

    def spread_own(k, far):
        _, buf = streams[k]
        i = held[far]
        arrived(buf.at[i, c], m.sp_r.at[k, i, c])
        push(buf.at[i, c], buf.at[i, c], m.sp_s.at[k, 2 + 2 * far], m.sp_r.at[k, i, c], nbr)
        push(buf.at[i, c], buf.at[i, c], m.sp_s.at[k, 3 + 2 * far], m.sp_r.at[k, i, c], sib)

    def spread_nbr(k, far):
        _, buf = streams[k]
        j = beside[far]
        arrived(buf.at[j, c], m.sp_r.at[k, j, c])
        push(buf.at[j, c], buf.at[j, c], m.sp_s.at[k, 6 + far], m.sp_r.at[k, j, c], sib)

    def spread_end(k):
        _, buf = streams[k]
        for i in held + beside:
            arrived(buf.at[i, 1 - c], m.sp_r.at[k, i, 1 - c])

    for k in range(2):
        spread_home(k, False)
        spread_home(k, True)
    spread_home(2, True)

    for copy in loads:
        copy.wait()
    for tt in range(4):
        at = 0
        for k in range(3):
            for j in range(2):
                m.PR0[tt, 1, 0:rw, at : at + hd] = m.PR1[k, 0, 0:rw, (j * 4 + tt) * hd : (j * 4 + tt + 1) * hd]
                at += hd
        for k in range(8):
            row, at = divmod(hidden_at(k, tt) * fw, width)
            m.PR0[tt, 0, 0:rw, k * fw : (k + 1) * fw] = m.PR1[row, 1, 0:rw, at : at + fw]
    cols = 3 * two

    def pre_src(n, tt):
        if n == 0:
            return m.PR0.at[tt, 1, pl.ds(0, rw), pl.ds(0, cols)]
        if n == 1:
            return m.vec
        return m.PR0.at[tt, 0, pl.ds(0, rw), pl.ds(0, hid)]

    def rank_rows(cc, pp):
        return (yx, cc, q, pl.ds(pl.multiple_of(pp * rw, rw), rw))

    def pre_dst(n, tt):
        if n == 1:
            return m.PV.at[tt]
        return (m.WA if n == 0 else m.WU).at[rank_rows(lax.rem(tt, 2), lax.div(tt, 2))]

    pre_sent = []

    def pre_send(n):
        for d in (1, 2, 3):
            tt = lax.rem(t + d, 4)
            pre_sent.append(
                push(pre_src(n, tt), pre_dst(n, t), m.pre_s.at[n, d - 1], m.pre_r.at[n, t], mate(tt), keep=False)
            )

    pre_send(1)
    pre_send(0)
    local_o = pltpu.make_async_copy(m.wo, m.WOP.at[me], m.loc.at[0])
    local_o.start()
    local_d = pltpu.make_async_copy(m.wdn, m.WD.at[me], m.loc.at[1])
    local_d.start()
    m.WA[rank_rows(c, p)] = m.PR0[t, 1, 0:rw, 0:cols]
    m.WU[rank_rows(c, p)] = m.PR0[t, 0, 0:rw, 0:hid]
    m.PV[t] = m.vec[...]

    def pre_wait(n):
        for d in (1, 2, 3):
            tt = lax.rem(t + d, 4)
            arrived(pre_dst(n, tt), m.pre_r.at[n, tt])

    def piece(n, yy, xx, qq):
        if n < 2:
            return m.WA.at[yy * 2 + xx, n, qq]
        if n == 4:
            return m.WU.at[yy * 2 + xx, :, qq]
        return {2: m.VEC, 3: m.WOP, 5: m.WD}[n].at[at8(yy, xx, qq)]

    def order(n):
        return "xy" if n in (0, 2, 4) else "yx"

    def beyond(first, qq):
        return (y, 1 - x, qq) if first == "x" else (1 - y, x, qq)

    def gather_send(n, spot, k, to):
        ref = piece(n, *spot)
        push(ref, ref, m.ag_s.at[n, k], m.ag_r.at[n, at8(*spot)], over[to])

    def gather_own(group, steps=(0, 1, 2)):
        for k in steps:
            for n in group:
                gather_send(n, (y, x, q), k, ("q" + order(n))[k])

    def gather_pass(group, k):
        for n in group:
            first, second = order(n)
            spot = (y, x, 1 - q) if k == 0 else beyond(first, q if k == 1 else 1 - q)
            arrived(piece(n, *spot), m.ag_r.at[n, at8(*spot)])
            if k == 0:
                gather_send(n, spot, 3, first)
                gather_send(n, spot, 4, second)
            else:
                gather_send(n, spot, 4 + k, second)

    def gather_end(group):
        for n in group:
            second = order(n)[1]
            for a in range(2):
                for qq in range(2):
                    spot = (1 - y, a, qq) if second == "y" else (a, 1 - x, qq)
                    arrived(piece(n, *spot), m.ag_r.at[n, at8(*spot)])

    VECS, ATT, WOUT, FFN = (2,), (0, 1), (3,), (4, 5)

    def norm_one(i, h):
        xhat, _ = norm_parts(m.X[i, h].astype(F32))
        at = pl.ds(pl.multiple_of(i * rows + h * half, half), half)
        m.N1[at, :] = (xhat * m.VF[1:2] + m.VF[2:3]).astype(BF16)

    def vec_own():
        pre_wait(1)
        total = sum((m.PV[a].astype(F32) for a in range(1, 4)), m.PV[0].astype(F32))
        line = lax.broadcasted_iota(jnp.int32, (16, width), 0)
        own_vec = jnp.where(line == 5, m.vec[...].astype(F32), total)
        m.VEC[me] = own_vec.astype(BF16)
        gather_own(VECS)

    def vec_end():
        gather_end(VECS)
        every = m.VEC[0].astype(F32)
        for a in range(1, 8):
            every = every + m.VEC[a].astype(F32)
        m.VF[...] = every[0:8]

    def swap_out():
        gather_end(WOUT)
        for yy in range(2):
            for qq in range(2):
                k = yy * 2 + qq
                push(
                    m.WOP.at[at8(yy, 1 - p, qq)], m.WO.at[yy, qq, p], m.sw_s.at[k], m.sw_r.at[k], nbr
                )
                m.WO[yy, qq, p] = m.WOP[at8(yy, p, qq)]

    def swap_end():
        for yy in range(2):
            for qq in range(2):
                arrived(m.WO.at[yy, qq, 1 - p], m.sw_r.at[yy * 2 + qq])

    spread_own(0, 0)
    spread_own(1, 0)
    vec_own()
    pre_wait(0)
    gather_own(ATT)
    pre_send(2)
    local_o.wait()
    local_d.wait()
    gather_pass(VECS, 0)
    gather_own(WOUT)
    gather_pass(ATT, 0)
    spread_nbr(0, 0)
    spread_nbr(1, 0)
    pre_wait(2)
    for copy in pre_sent:
        copy.wait_send()
    gather_pass(VECS, 1)
    gather_pass(VECS, 2)
    gather_own(FFN, (1, 2))
    vec_end()
    norm_one(held[0], c)
    norm_one(beside[0], c)
    gather_pass(ATT, 1)
    gather_pass(WOUT, 0)
    spread_own(2, 0)
    spread_own(0, 1)
    spread_own(1, 1)
    gather_own(FFN, (0,))
    gather_pass(ATT, 2)
    norm_one(held[1], c)
    spread_home(2, False)
    gather_pass(WOUT, 1)
    gather_pass(WOUT, 2)
    spread_nbr(0, 1)
    spread_nbr(1, 1)
    swap_out()
    norm_one(beside[1], c)
    spread_end(0)
    spread_end(1)
    for i in held + beside:
        norm_one(i, 1 - c)
    gather_end(ATT)

    def row_tile(i):
        return pl.ds(pl.multiple_of(i * rows, rows), rows)

    def col_tile(n, size=256):
        return pl.ds(pl.multiple_of(n * size, size), size)

    @pl.loop(0, 3)
    def _(n):
        w = m.WA[:, :, :, :, col_tile(n)].reshape(width, 256)

        @pl.loop(0, 4)
        def _(i):
            m.QKV[row_tile(i), col_tile(n)] = dot_nn(m.N1[row_tile(i), :], w).astype(BF16)

    EX = (
        (m.PR0, m.RBa, m.RXa),
        (m.PR1, m.RBb, m.RXb),
        (m.PR0, m.RBa, m.RXc),
        (m.PR1, m.RBc, m.RXd),
    )
    ex_open = {}
    ex_far = {1: [], 3: []}

    def ex_put(e, i, cols_at, value):
        pair = EX[e][0]
        low = value.astype(BF16)
        pair[i, 0, :, cols_at] = low[0:half]
        pair[i, 1, :, cols_at] = low[half:rows]

    def ex_send(e, i):
        pair, rb, _ = EX[e]
        ex_open[e, i] = [push(pair.at[i, 1 - c], rb.at[i], m.sib_s.at[e, i], m.sib_r.at[e, i], sib, keep=False)]

    def ex_mid(e, i):
        pair, rb, rx = EX[e]
        arrived(rb.at[i], m.sib_r.at[e, i])
        pair[i, c] = (pair[i, c].astype(F32) + rb[i].astype(F32)).astype(BF16)
        if e in (0, 2):
            ex_open[e, i].append(push(pair.at[i, c], rx.at[i], m.xs.at[e, i], m.xr.at[e, i], nbr, keep=False))
        else:
            copy = remote(pair.at[i, c], rx.at[i // 2], m.xs.at[e, i], m.xr.at[e, i // 2], nbr)
            far = p != i % 2

            @pl.when(far)
            def _():
                copy.start()

            ex_far[e].append((jnp.logical_not(far), copy))

    def ex_close(e, i):
        for copy in ex_open[e, i]:
            copy.wait_send()
        ex_open[e, i] = []

    def ex_total(e, i):
        pair, _, rx = EX[e]
        arrived(rx.at[i], m.xr.at[e, i])
        return pair[i, c].astype(F32) + rx[i].astype(F32)

    PS = (m.P0, m.P1, m.P2, m.P3)

    def attend(i):
        span = (i + 1) * rows
        r0 = i * rows
        start = m.ST[i, 0][0:1, 0:1].astype(F32)
        for j in range(2):
            q = m.QKV[r0 : r0 + rows, j * hd : (j + 1) * hd]
            k = m.QKV[0:span, two + j * hd : two + (j + 1) * hd]
            s = dot_nt(q, k) * scale
            row = lax.broadcasted_iota(jnp.int32, (rows, span), 0) + r0
            col = lax.broadcasted_iota(jnp.int32, (rows, span), 1)
            s = jnp.where((col <= row) & (col.astype(F32) >= start), s, masked_value)
            e = jnp.exp(s - jnp.max(s, axis=-1, keepdims=True))
            p = (e * (1.0 / jnp.sum(e, axis=-1, keepdims=True))).astype(BF16)
            PS[i][j] = p
            v = m.QKV[0:span, 2 * two + j * hd : 2 * two + (j + 1) * hd]
            m.MIX[r0 : r0 + rows, j * hd : (j + 1) * hd] = dot_nn(p, v).astype(BF16)

    def attend_out(i):
        r0 = i * rows

        @pl.loop(0, 4)
        def _(n):
            w = m.WO[:, :, :, :, col_tile(n)].reshape(two, 256)
            ex_put(0, i, col_tile(n), dot_nn(m.MIX[r0 : r0 + rows, :], w))

        ex_send(0, i)

    def second_norm(i):
        res = m.X[i, c].astype(F32) + ex_total(0, i)
        m.RES[i] = res
        xhat, _ = norm_parts(res)
        m.N2[i, c] = (xhat * m.VF[3:4] + m.VF[4:5]).astype(BF16)
        push(m.N2.at[i, c], m.N2.at[i, c], m.n2_s.at[i], m.n2_r.at[i], sib)

    m.VSUM[...] = jnp.zeros((8, width), F32)

    def feed(n):
        tile = col_tile(n)
        w_in = m.WU[:, :, :, :, tile].reshape(width, 256)
        w_back = m.WD[pl.ds(n * (256 // fw), 256 // fw)].reshape(256, width)

        @pl.loop(0, 4)
        def _(i):
            pre = dot_nn(m.N2[i].reshape(rows, width), w_in) + m.VF[5:6, tile]
            back = dot_nt(m.DZ[i].reshape(rows, width), w_back)
            sq = pre * pre
            th = jnp.tanh(GELU_K * pre * (1.0 + GELU_C * sq))
            m.HID[row_tile(i), tile] = (0.5 * pre * (1.0 + th)).astype(BF16)
            slope = 0.5 * (1.0 + th) + 0.5 * pre * (1.0 - th * th) * (GELU_K * (1.0 + 3.0 * GELU_C * sq))
            dpre = back * slope
            m.VSUM[5:6, tile] += jnp.sum(dpre, axis=0, keepdims=True)
            m.DP[row_tile(i), tile] = dpre.astype(BF16)

    def feed_two(i):
        r0 = i * rows
        ex_close(0, i)

        @pl.loop(0, width // 256)
        def _(n):
            w = m.WU[n].reshape(256, hid)
            ex_put(2, i, col_tile(n), dot_nt(m.DP[r0 : r0 + rows, :], w))

        ex_send(2, i)

    def feed_out(i):
        r0 = i * rows

        @pl.loop(0, width // 256)
        def _(n):
            w = m.WD[:, :, col_tile(n)].reshape(hid, 256)
            ex_put(1, i, col_tile(n), dot_nn(m.HID[r0 : r0 + rows, :], w))

        ex_send(1, i)

    def feed_back(i):
        xhat, rstd = norm_parts(m.RES[i])
        g = ex_total(2, i)
        a = 0.5 * jnp.sum(g * xhat, axis=0, keepdims=True)
        b = 0.5 * jnp.sum(g, axis=0, keepdims=True)
        m.VSUM[3:4] += a
        m.VSUM[4:5] += b

        @pl.when(p == i % 2)
        def _():
            m.KEEP[i // 2] = m.RES[i]

        dres = m.DZ[i, c].astype(F32) + norm_back(g, m.VF[3:4], xhat, rstd)
        m.RES[i] = dres
        m.DB[i, c] = dres.astype(BF16)
        push(m.DB.at[i, c], m.DB.at[i, c], m.db_s.at[i], m.db_r.at[i], sib)

    def lane(ref, at):
        return ref[:, pl.ds(pl.multiple_of(at * 128, 128), 128)]

    def lane_n2(at):
        return m.N2[:, :, :, pl.ds(pl.multiple_of(at * 128, 128), 128)].reshape(4 * rows, 128)

    def flip(parts):
        for a, part in enumerate(parts):
            m.TT[a * 128 : (a + 1) * 128, :] = part.T

    SEND = (m.YSF.at[0], m.YSF.at[1], m.YSQ.at[0], m.YSQ.at[1])
    GOT1 = (m.R1F.at[0], m.R1F.at[1], m.R1Q.at[0], m.R1Q.at[1])
    GOT2 = (m.R2F.at[0], m.R2F.at[1], m.R2Q.at[0], m.R2Q.at[1])
    GOT3 = (m.R3F.at[0], m.R3F.at[1], m.R3Q.at[0], m.R3Q.at[1])
    AXES = ("yx", "xy", "yx", "xy")
    open1 = {0: [], 1: [], 2: [], 3: []}
    fh = fw // 2

    def step1(w, slots):
        for k in slots:
            open1[w].append(
                push(SEND[w].at[k], GOT1[w].at[k], m.r1_s.at[w, k], m.r1_r.at[w, k], over[AXES[w][0]], keep=False)
            )

    def up_lhs(yy):
        flip([lane_n2((yy * 2 + a // 2) * 2 + a % 2) for a in range(4)])

    def up_parts(res):
        return [
            ((a // 2) * 2 + b, (a % 2) * fh, res[a * 128 + b * fh : a * 128 + (b + 1) * fh])
            for a in range(4)
            for b in range(2)
        ]

    def far_tile(k):
        return 2 * k + 1 - x if k < 2 else 2 * (k - 2) + x

    def up_far(k):
        s = col_tile(far_tile(k))
        for slot, at, part in up_parts(dot_nn(m.TT[...], m.DP[:, s])):
            m.YSF[0, slot, at : at + fh, s] = part.astype(BF16)
        for slot in range(4):
            src, dst = m.YSF.at[0, slot, :, s], m.R1F.at[0, slot, :, s]
            open1[0].append(push(src, dst, m.up_s.at[k, slot], m.up_r.at[k, slot], over["y"], keep=False))

    def down_far(k):
        for a in range(2):
            m.TU[a * 128 : (a + 1) * 128, :] = lane(m.HID, far_tile(k) * 2 + a).T

        @pl.loop(0, width // 256)
        def _(n):
            s = col_tile(n)
            res = dot_nn(m.TU[...], m.DZ[:, :, :, s].reshape(4 * rows, 256)).astype(BF16)
            m.YSF[1, 2 * k, :, s] = res[0:fw]
            m.YSF[1, 2 * k + 1, :, s] = res[fw : 2 * fw]

        step1(1, (2 * k, 2 * k + 1))

    def qkv_lhs(yy, xx):
        flip([lane(m.N1, (yy * 2 + a) * 2) for a in range(2)] + [lane(m.N1, (a * 2 + xx) * 2 + 1) for a in range(2)])

    def qkv_parts(res):
        return [
            (a // 2, (a % 2) * 2 + b, res[a * 128 + b * fh : a * 128 + (b + 1) * fh]) for a in range(4) for b in range(2)
        ]

    def qkv_far():
        qkv_lhs(1 - y, 1 - x)

        @pl.loop(0, 3)
        def _(n):
            s = col_tile(n)
            for e, slot, part in qkv_parts(dot_nn(m.TT[...], m.QKV[:, s])):
                m.YSQ[e, slot, :, s] = part.astype(BF16)

        step1(2, range(4))
        step1(3, range(4))

    def near_wait(w):
        for copy in open1[w]:
            copy.wait_send()
        for slot in range(4):
            if w:
                arrived(GOT1[w].at[slot], m.r1_r.at[w, slot])
            else:
                for k in range(4):
                    arrived(m.R1F.at[0, slot, :, col_tile(far_tile(k))], m.up_r.at[k, slot])

    def step2(w):
        first, second = AXES[w]
        there = 1 - (x if second == "x" else y)
        for qq in range(2):
            push(
                SEND[w].at[there * 2 + qq], GOT2[w].at[qq], m.r2_s.at[w, qq], m.r2_r.at[w, qq], over[second]
            )

    def up_near():
        up_lhs(y)
        near_wait(0)

        @pl.loop(0, hid // 256)
        def _(n):
            s = col_tile(n)
            for slot, at, part in up_parts(dot_nn(m.TT[...], m.DP[:, s])):
                to = slice(at, at + fh)
                m.YSF[0, slot, to, s] = (part + m.R1F[0, slot, to, s].astype(F32)).astype(BF16)

        step2(0)

    def down_near():
        near_wait(1)
        for k in range(2):
            for a in range(2):
                m.TU[a * 128 : (a + 1) * 128, :] = lane(m.HID, far_tile(k + 2) * 2 + a).T

            @pl.loop(0, width // 256)
            def _(n):
                s = col_tile(n)
                res = dot_nn(m.TU[...], m.DZ[:, :, :, s].reshape(4 * rows, 256))
                for b in range(2):
                    got = m.R1F[1, 2 * k + b, :, s].astype(F32)
                    m.YSF[1, 2 * k + b, :, s] = (res[b * fw : (b + 1) * fw] + got).astype(BF16)

        step2(1)

    def qkv_near():
        qkv_lhs(y, x)
        near_wait(2)
        near_wait(3)

        @pl.loop(0, 3)
        def _(n):
            s = col_tile(n)
            for e, slot, part in qkv_parts(dot_nn(m.TT[...], m.QKV[:, s])):
                m.YSQ[e, slot, :, s] = (part + m.R1Q[e, slot, :, s].astype(F32)).astype(BF16)

        step2(2)
        step2(3)

    def here(w):
        return x if AXES[w][1] == "x" else y

    def grad_mid(w):
        for qq in range(2):
            arrived(GOT2[w].at[qq], m.r2_r.at[w, qq])
            slot = here(w) * 2 + qq
            SEND[w][slot] = (SEND[w][slot].astype(F32) + GOT2[w][qq].astype(F32)).astype(BF16)
        push(SEND[w].at[here(w) * 2 + 1 - q], GOT3[w], m.r3_s.at[w], m.r3_r.at[w], over["q"])

    def grad_sum(w):
        arrived(GOT3[w], m.r3_r.at[w])
        return SEND[w][here(w) * 2 + q].astype(F32) + GOT3[w][...].astype(F32)

    def out_first():
        flip([lane(m.MIX, a) for a in range(2)])

        @pl.loop(0, width // 256)
        def _(n):
            s = col_tile(n)
            res = dot_nn(m.TT[0:two, :], m.DB[:, :, :, s].reshape(4 * rows, 256)).astype(BF16)
            m.GOB[:, :, :, :, s] = res.reshape(2, 2, 2, rw, 256)

        for yy in range(2):
            for qq in range(2):
                k = yy * 2 + qq
                push(m.GOB.at[yy, qq, 1 - p], m.GOR.at[yy, qq], m.sw_s2.at[k], m.sw_r2.at[k], nbr)

    def out_second():
        for yy in range(2):
            for qq in range(2):
                k = yy * 2 + qq
                arrived(m.GOR.at[yy, qq], m.sw_r2.at[k])
                m.GOS[at8(yy, p, qq)] = m.GOB[yy, qq, p]
                m.GOS[at8(yy, 1 - p, qq)] = m.GOR[yy, qq]
        for yy in range(2):
            for qq in range(2):
                k = yy * 2 + qq
                push(m.GOS.at[at8(yy, 1 - x, qq)], m.GOT.at[k], m.go_s.at[k], m.go_r.at[k], over["x"])

    def out_add(at, k):
        arrived(m.GOT.at[k], m.go_r.at[k])
        m.GOS[at] = (m.GOS[at].astype(F32) + m.GOT[k].astype(F32)).astype(BF16)

    def out_third():
        for yy in range(2):
            for qq in range(2):
                out_add(at8(yy, x, qq), yy * 2 + qq)
        for qq in range(2):
            push(m.GOS.at[at8(1 - y, x, qq)], m.GOT.at[4 + qq], m.go_s.at[4 + qq], m.go_r.at[4 + qq], over["y"])

    def out_fourth():
        for qq in range(2):
            out_add(at8(y, x, qq), 4 + qq)
        push(m.GOS.at[at8(y, x, 1 - q)], m.GOT.at[6], m.go_s.at[6], m.go_r.at[6], over["q"])

    def out_sum():
        arrived(m.GOT.at[6], m.go_r.at[6])
        m.OO[...] = m.GOS[me].astype(F32) + m.GOT[6].astype(F32)

    def give(e, src_of, dst):
        pltpu.make_async_copy(src_of(c, p), dst.at[t], m.pe_r.at[e, t]).start()
        for d in (1, 2, 3):
            tt = lax.rem(t + d, 4)
            push(src_of(lax.rem(tt, 2), lax.div(tt, 2)), dst.at[t], m.pe_s.at[e, d - 1], m.pe_r.at[e, t], mate(tt))

    def give_end():
        for e, dst in ((0, m.peu), (1, m.peq)):
            for tt in range(4):
                arrived(dst.at[tt], m.pe_r.at[e, tt])

    attend(0)
    swap_end()
    attend_out(0)
    gather_pass(FFN, 0)
    attend(1)
    attend_out(1)
    ex_mid(0, 0)
    attend(2)
    attend_out(2)
    gather_pass(FFN, 1)
    ex_mid(0, 1)
    second_norm(0)
    attend(3)
    attend_out(3)
    ex_mid(0, 2)
    gather_pass(FFN, 2)
    second_norm(1)
    ex_mid(0, 3)
    spread_nbr(2, 0)
    spread_own(2, 1)
    second_norm(2)
    second_norm(3)
    spread_nbr(2, 1)
    for i in range(4):
        arrived(m.N2.at[i, 1 - c], m.n2_r.at[i])
    up_lhs(1 - y)
    spread_end(2)
    gather_end(FFN)
    for k in range(4):
        feed(far_tile(k))
        if k < 2:
            down_far(k)
        up_far(k)
    for i in range(4):
        feed_two(i)
        if i:
            ex_mid(2, i - 1)
    ex_mid(2, 3)
    for i in range(4):
        feed_out(i)
    feed_back(0)
    feed_back(1)
    down_near()
    up_near()

    def db_end(i):
        arrived(m.DB.at[i, 1 - c], m.db_r.at[i])

    def attend_back(i):
        span = (i + 1) * rows
        r0 = i * rows
        m.DMIX[...] = dot_nt(m.DB[i].reshape(rows, width), m.WO[...].reshape(two, width)).astype(BF16)
        for j in range(2):
            k0, v0 = two + j * hd, 2 * two + j * hd
            do = m.DMIX[:, j * hd : (j + 1) * hd]
            p = PS[i][j]
            pf = p.astype(F32)
            g = dot_nt(do, m.QKV[0:span, v0 : v0 + hd])
            delta = jnp.sum(pf * g, axis=-1, keepdims=True)
            ds = (pf * (g - delta) * scale).astype(BF16)
            q = m.QKV[r0 : r0 + rows, j * hd : (j + 1) * hd]
            dk = dot_tn(ds, q)
            dv = dot_tn(p, do)
            dq = dot_nn(ds, m.QKV[0:span, k0 : k0 + hd])
            ka, va = slice(j * hd, (j + 1) * hd), slice(two + j * hd, two + (j + 1) * hd)
            if i:
                m.ACC[0:r0, ka] += dk[0:r0]
                m.ACC[0:r0, va] += dv[0:r0]
            m.ACC[r0:span, ka] = dk[r0:span]
            m.ACC[r0:span, va] = dv[r0:span]
            m.QKV[r0 : r0 + rows, j * hd : (j + 1) * hd] = dq.astype(BF16)

    def give_back(k, kk, buf, dst):
        i = mine[kk]
        near = (q == c) & (i == z)
        to = dst.at[pl.ds(pl.multiple_of(c * half, half), half)]
        rsem = m.ret_r.at[k, c]

        @pl.when(near)
        def _():
            pltpu.make_async_copy(buf.at[kk], to, rsem).start()

        copy = remote(buf.at[kk], to, m.ret_s.at[k, kk], rsem, dev(y, x, q, i))

        @pl.when(jnp.logical_not(near))
        def _():
            copy.start()

        homes.append((near, copy))

    def far_close(e):
        for near, copy in ex_far.pop(e):

            @pl.when(jnp.logical_not(near))
            def _():
                copy.wait_send()

    def finish_out(kk):
        i = mine[kk]
        arrived(m.RXb.at[kk], m.xr.at[1, kk])
        value = m.KEEP[kk] + m.PR1[i, c].astype(F32) + m.RXb[kk].astype(F32) + m.VF[0:1]
        m.OUTB[kk] = value.astype(BF16)
        give_back(0, kk, m.OUTB, m.out)

    def first_back(i):
        r0 = i * rows

        @pl.loop(0, width // 256)
        def _(n):
            w = m.WA[n].reshape(256, cols)
            ex_put(3, i, col_tile(n), dot_nt(m.QKV[r0 : r0 + rows, :], w))

        ex_send(3, i)

    def finish_in(kk):
        i = mine[kk]
        arrived(m.RXd.at[kk], m.xr.at[3, kk])
        g = m.PR1[i, c].astype(F32) + m.RXd[kk].astype(F32)
        xhat, rstd = norm_parts(m.X[i, c].astype(F32))
        parts = (
            jnp.sum(m.DZ[i, c].astype(F32), axis=0, keepdims=True),
            jnp.sum(g * xhat, axis=0, keepdims=True),
            jnp.sum(g, axis=0, keepdims=True),
        )
        for k, part in enumerate(parts):
            m.VSUM[k : k + 1] += part
        m.IGB[kk] = (m.RES[i] + norm_back(g, m.VF[1:2], xhat, rstd)).astype(BF16)
        give_back(1, kk, m.IGB, m.ig)

    db_end(0)
    attend_back(0)
    feed_back(2)
    db_end(1)
    attend_back(1)
    feed_back(3)
    for i in range(4):
        ex_mid(1, i)
    grad_mid(1)
    db_end(2)
    db_end(3)
    out_first()
    attend_back(2)
    grad_mid(0)
    finish_out(0)
    finish_out(1)
    out_second()
    attend_back(3)

    @pl.loop(0, 4)
    def _(i):
        m.QKV[row_tile(i), two : 3 * two] = m.ACC[row_tile(i), :].astype(BF16)

    qkv_far()
    far_close(1)
    for i in range(4):
        ex_close(1, i)
    out_third()
    for i in range(4):
        first_back(i)
        if i:
            ex_mid(3, i - 1)
    ex_mid(3, 3)
    out_fourth()
    qkv_near()
    finish_in(0)
    finish_in(1)

    for d in (1, 2, 3):
        tt = lax.rem(t + d, 4)
        push(m.VSUM, m.VR1.at[t], m.v1_s.at[d - 1], m.v1_r.at[t], mate(tt))
    grad_mid(2)
    grad_mid(3)
    rest = m.VSUM[...]
    for d in (1, 2, 3):
        tt = lax.rem(t + d, 4)
        arrived(m.VR1.at[tt], m.v1_r.at[tt])
        rest = rest + m.VR1[tt]
    row8 = lax.broadcasted_iota(jnp.int32, (8, width), 0)
    m.VMID[...] = jnp.where(row8 == 5, m.VSUM[...], rest)
    for k, f in enumerate(flips):
        if k:
            push(m.VMID, m.VR2.at[me], m.v2_s.at[k - 1], m.v2_r.at[me], peer(*flipped(*f)))
    m.OD[...] = grad_sum(1)
    keep_down = pltpu.make_async_copy(m.OD, m.gdn, m.loc.at[2])
    keep_down.start()
    m.FIU[...] = grad_sum(0).astype(BF16)
    give(0, lambda cc, pp: m.FIU.at[pl.ds(pl.multiple_of((cc * 2 + pp) * rw, rw), rw)], m.peu)
    out_sum()
    keep_out = pltpu.make_async_copy(m.OO, m.go, m.loc.at[3])
    keep_out.start()
    for e in range(2):
        m.FIN[e] = grad_sum(2 + e).astype(BF16)
    give(1, lambda cc, pp: m.FIN.at[cc, pl.ds(pl.multiple_of(pp * rw, rw), rw)], m.peq)

    final = m.VMID[...]
    for k, f in enumerate(flips):
        if k:
            at = at8(*flipped(*f))
            arrived(m.VR2.at[at], m.v2_r.at[at])
            final = final + m.VR2[at]
    m.gvec[...] = final

    for k, dst in enumerate((m.out, m.ig)):
        for cc in range(2):
            arrived(dst.at[pl.ds(cc * half, half)], m.ret_r.at[k, cc])
    give_end()
    keep_down.wait()
    keep_out.wait()
    for copy in sent:
        copy.wait_send()
    for e, i in ex_open:
        ex_close(e, i)
    far_close(3)
    for near, copy in homes:

        @pl.when(jnp.logical_not(near))
        def _():
            copy.wait_send()


def place_outputs(out_i, ig_i, peq, peu, go_i, gdn_i, out, ig, gq, gk, gv, go, gup, gdn, PQ, PU, GQ, GU, A, B, GO, GD, sem):
    pairs = ((peq, PQ), (peu, PU), (out_i, A), (ig_i, B), (go_i, GO), (gdn_i, GD))
    moves = [pltpu.make_async_copy(src, dst, sem.at[k]) for k, (src, dst) in enumerate(pairs)]
    for move in moves:
        move.start()
    results = ((A, out), (B, ig), (GO, go), (GD, gdn), (GQ.at[0], gq), (GQ.at[1], gk), (GQ.at[2], gv), (GU, gup))
    last = [pltpu.make_async_copy(src, dst, sem.at[6 + k]) for k, (src, dst) in enumerate(results)]
    hd = PQ.shape[2] // 6
    fw = PU.shape[2] // 8
    moves[0].wait()
    moves[1].wait()
    for tt in range(RANKS):
        for j in range(2):
            a = (j * RANKS + tt) * hd
            for n in range(3):
                GQ[n, :, a : a + hd] = PQ[tt, :, (n * 2 + j) * hd : (n * 2 + j + 1) * hd].astype(F32)
        for k in range(8):
            a = hidden_at(k, tt) * fw
            GU[:, a : a + fw] = PU[tt, :, k * fw : (k + 1) * fw].astype(F32)
    for k in range(4):
        last[4 + k].start()
    for k in range(4):
        moves[2 + k].wait()
        last[k].start()
    for move in last:
        move.wait()


def call_fused(inputs, positions, w_query, w_key, w_value, w_out, w_up, w_down, up_bias, down_bias,
               ln1_gain, ln1_bias, ln2_gain, ln2_bias, cotangent):
    rows, width = inputs.shape
    hid = w_up.shape[1] // RANKS
    rw, fw = w_query.shape[0], w_down.shape[0]
    shapes = scratch_of(rows, width, hid, rw, fw)
    dp, blk = lax.axis_index("dp"), lax.axis_index("blk")
    n_blk = lax.axis_size("blk")
    place = dp * n_blk + blk
    at_up = dp // 2 * 2 + blk // 2
    small_in = [v.reshape(1, -1) for v in (down_bias, ln1_gain, ln1_bias, ln2_gain, ln2_bias, up_bias)]
    names = IN_NAMES + OUT_NAMES + tuple(shapes)
    any_, vm = pl.BlockSpec(memory_space=pl.ANY), pl.BlockSpec(memory_space=pltpu.VMEM)
    S = jax.ShapeDtypeStruct
    cols = 3 * 2 * (width // HEADS)
    tokens, wide = S((rows, width), BF16), S((rw, width), F32)
    moved = (S((RANKS, rw, cols), BF16), S((RANKS, rw, hid), BF16))
    out, ig, peq, peu, go, gdn, gvec = pl.pallas_call(
        functools.partial(fused, names),
        out_shape=(tokens, tokens) + moved + (wide, S(w_down.shape, F32), S((8, width), F32)),
        in_specs=[any_, any_, vm] + [any_] * 6 + [vm] * 6,
        out_specs=[any_] * 6 + [vm],
        scratch_shapes=list(shapes.values()),
        compiler_params=pltpu.CompilerParams(
            collective_id=0, has_side_effects=True, vmem_limit_bytes=VMEM_BYTES
        ),
        cost_estimate=pl.CostEstimate(flops=23 * 10**9, bytes_accessed=10**7, transcendentals=10**6),
    )(inputs, cotangent, positions.reshape(2, -1), w_query, w_key, w_value, w_out, w_up, w_down, *small_in)
    out, ig, gq, gk, gv, go, gup, gdn = pl.pallas_call(
        place_outputs,
        out_shape=(tokens, tokens, wide, wide, wide, wide, S(w_up.shape, F32), S(w_down.shape, F32)),
        in_specs=[any_] * 6,
        out_specs=[any_] * 8,
        scratch_shapes=[
            pltpu.VMEM(moved[0].shape, BF16),
            pltpu.VMEM(moved[1].shape, BF16),
            pltpu.VMEM((3, rw, width), F32),
            pltpu.VMEM(w_up.shape, F32),
            pltpu.VMEM((rows, width), BF16),
            pltpu.VMEM((rows, width), BF16),
            pltpu.VMEM((rw, width), F32),
            pltpu.VMEM(w_down.shape, F32),
            pltpu.SemaphoreType.DMA((14,)),
        ],
        compiler_params=pltpu.CompilerParams(vmem_limit_bytes=VMEM_BYTES),
    )(out, ig, peq, peu, go, gdn)
    small = lax.dynamic_slice(gvec, (0, place * rw), (5, rw))
    gup_bias = lax.dynamic_slice(gvec, (5, at_up * fw), (1, fw))[0]
    return (out, ig, gq, gk, gv, go, gup, gdn, gup_bias, small[0], small[1], small[2], small[3], small[4])


def layer_norm(values, gain, offset):
    centre = jnp.mean(values, axis=-1, keepdims=True)
    centred = values - centre
    variance = jnp.mean(centred * centred, axis=-1, keepdims=True)
    return centred * lax.rsqrt(variance + eps) * gain + offset


def smooth_gate(values):
    return jax.nn.gelu(values, approximate=True)


def keep_same(carry):
    return carry


def local(
    inputs,
    positions,
    w_query,
    w_key,
    w_value,
    w_out,
    w_up,
    w_down,
    up_bias,
    down_bias,
    ln1_gain,
    ln1_bias,
    ln2_gain,
    ln2_bias,
    cotangent,
):
    attn_full = (
        lax.all_gather(w_query, ("dp", "blk"), axis=0, tiled=True),
        lax.all_gather(w_key, ("dp", "blk"), axis=0, tiled=True),
        lax.all_gather(w_value, ("dp", "blk"), axis=0, tiled=True),
        lax.all_gather(w_out, ("dp", "blk"), axis=0, tiled=True),
        lax.all_gather(ln1_gain, ("dp", "blk"), axis=0, tiled=True),
        lax.all_gather(ln1_bias, ("dp", "blk"), axis=0, tiled=True),
    )
    ffn_full = (
        lax.all_gather(w_up, ("dp", "blk"), axis=0, tiled=True),
        lax.all_gather(w_down, ("dp", "blk"), axis=0, tiled=True),
        lax.all_gather(up_bias, ("dp", "blk"), axis=0, tiled=True),
        lax.all_gather(down_bias, ("dp", "blk"), axis=0, tiled=True),
        lax.all_gather(ln2_gain, ("dp", "blk"), axis=0, tiled=True),
        lax.all_gather(ln2_bias, ("dp", "blk"), axis=0, tiled=True),
    )
    token_rows = inputs.astype(jnp.float32)
    local_rows, model_width = token_rows.shape
    head_count = HEADS
    head_size = model_width // head_count
    score_scale = 1.0 / math.sqrt(head_size)
    normed_first, first_pull = jax.vjp(
        layer_norm, token_rows, attn_full[4].astype(jnp.float32), attn_full[5].astype(jnp.float32)
    )
    normed_low = normed_first.astype(jnp.bfloat16)
    query_low = jnp.dot(normed_low, attn_full[0], preferred_element_type=jnp.float32).astype(
        jnp.bfloat16
    )
    key_low = jnp.dot(normed_low, attn_full[1], preferred_element_type=jnp.float32).astype(
        jnp.bfloat16
    )
    value_low = jnp.dot(normed_low, attn_full[2], preferred_element_type=jnp.float32).astype(
        jnp.bfloat16
    )
    keys_all, values_all = (
        lax.all_gather(key_low, "blk", axis=0, tiled=True),
        lax.all_gather(value_low, "blk", axis=0, tiled=True),
    )
    group_rows = keys_all.shape[0]
    key_rows = max(min(512, group_rows), local_rows)
    block_count = group_rows // key_rows
    first_row = lax.axis_index("blk") * local_rows
    query_index = first_row + jnp.arange(local_rows, dtype=jnp.int32)
    seq_start = query_index - positions
    earliest = jnp.min(seq_start)
    query_heads = query_low.reshape(local_rows, head_count, head_size)
    key_parts = []
    for which in range(block_count):
        begin = which * key_rows
        key_part = keys_all[begin : begin + key_rows].reshape(key_rows, head_count, head_size)
        value_part = values_all[begin : begin + key_rows].reshape(key_rows, head_count, head_size)
        key_index = begin + jnp.arange(key_rows, dtype=jnp.int32)
        allowed = (key_index[None, :] <= query_index[:, None]) & (
            key_index[None, :] >= seq_start[:, None]
        )
        needed = (begin <= first_row + local_rows - 1) & (begin + key_rows - 1 >= earliest)
        key_parts.append((key_part, value_part, allowed, needed))

    def scores_of(key_part, allowed):
        scores = (
            jnp.einsum("qhd,khd->hqk", query_heads, key_part, preferred_element_type=jnp.float32)
            * score_scale
        )
        return jnp.where(allowed[None], scores, masked_value)

    running_max = jnp.full((head_count, local_rows), masked_value, jnp.float32)
    running_sum = jnp.zeros((head_count, local_rows), jnp.float32)
    for key_part, value_part, allowed, needed in key_parts:

        def extend(carry):
            old_max, old_sum = carry
            scores = scores_of(key_part, allowed)
            new_max = jnp.maximum(old_max, jnp.max(scores, axis=-1))
            terms = jnp.where(allowed[None], jnp.exp(scores - new_max[..., None]), 0.0)
            return (new_max, old_sum * jnp.exp(old_max - new_max) + jnp.sum(terms, axis=-1))

        running_max, running_sum = lax.cond(needed, extend, keep_same, (running_max, running_sum))
    log_total = running_max + jnp.log(running_sum)

    def probs_of(key_part, allowed):
        scores = scores_of(key_part, allowed)
        return jnp.where(allowed[None], jnp.exp(scores - log_total[..., None]), 0.0)

    attended = jnp.zeros((local_rows, head_count, head_size), jnp.float32)
    for key_part, value_part, allowed, needed in key_parts:

        def gather_values(total):
            weights_low = probs_of(key_part, allowed).astype(jnp.bfloat16)
            return total + jnp.einsum(
                "hqk,khd->qhd", weights_low, value_part, preferred_element_type=jnp.float32
            )

        attended = lax.cond(needed, gather_values, keep_same, attended)
    mixed_low = attended.reshape(local_rows, model_width).astype(jnp.bfloat16)
    residual = token_rows + jnp.dot(mixed_low, attn_full[3], preferred_element_type=jnp.float32)
    normed_second, second_pull = jax.vjp(
        layer_norm, residual, ffn_full[4].astype(jnp.float32), ffn_full[5].astype(jnp.float32)
    )
    normed_two = normed_second.astype(jnp.bfloat16)
    preact = jnp.dot(normed_two, ffn_full[0], preferred_element_type=jnp.float32) + ffn_full[
        2
    ].astype(jnp.float32)
    gated, gate_pull = jax.vjp(smooth_gate, preact)
    hidden = gated.astype(jnp.bfloat16)
    output = (
        residual
        + jnp.dot(hidden, ffn_full[1], preferred_element_type=jnp.float32)
        + ffn_full[3].astype(jnp.float32)
    ).astype(jnp.bfloat16)
    up_back, down_back = (ffn_full[0], ffn_full[1])
    grad_final = cotangent.astype(jnp.float32)
    grad_down_w = jnp.einsum("tf,td->fd", hidden, cotangent, preferred_element_type=jnp.float32)
    grad_down_shift = jnp.sum(grad_final, axis=0)
    grad_hidden = jnp.einsum("td,fd->tf", cotangent, down_back, preferred_element_type=jnp.float32)
    grad_preact = gate_pull(grad_hidden)[0].astype(jnp.bfloat16)
    grad_up_shift = jnp.sum(grad_preact.astype(jnp.float32), axis=0)
    grad_up_w = jnp.einsum("td,tf->df", normed_two, grad_preact, preferred_element_type=jnp.float32)
    grad_normed_two = jnp.einsum(
        "tf,df->td", grad_preact, up_back, preferred_element_type=jnp.float32
    )
    grad_resid_two, grad_gain_two, grad_shift_two = second_pull(grad_normed_two)
    grad_residual = grad_final + grad_resid_two
    query_back, key_back, value_back, out_back = (
        attn_full[0],
        attn_full[1],
        attn_full[2],
        attn_full[3],
    )
    grad_branch = grad_residual.astype(jnp.bfloat16)
    grad_out_w = jnp.einsum("te,td->ed", mixed_low, grad_branch, preferred_element_type=jnp.float32)
    grad_mixed = jnp.einsum(
        "td,ed->te", grad_branch, out_back, preferred_element_type=jnp.float32
    ).astype(jnp.bfloat16)
    grad_heads = grad_mixed.reshape(local_rows, head_count, head_size)
    delta = jnp.zeros((head_count, local_rows), jnp.float32)
    for key_part, value_part, allowed, needed in key_parts:

        def add_delta(total):
            probs = probs_of(key_part, allowed)
            grad_probs = jnp.einsum(
                "qhd,khd->hqk", grad_heads, value_part, preferred_element_type=jnp.float32
            )
            return total + jnp.sum(probs * grad_probs, axis=-1)

        delta = lax.cond(needed, add_delta, keep_same, delta)
    grad_query_sum = jnp.zeros((local_rows, head_count, head_size), jnp.float32)
    kv_terms = []
    for key_part, value_part, allowed, needed in key_parts:

        def backward_part(total):
            probs = probs_of(key_part, allowed)
            grad_probs = jnp.einsum(
                "qhd,khd->hqk", grad_heads, value_part, preferred_element_type=jnp.float32
            )
            grad_scores = (probs * (grad_probs - delta[..., None]) * score_scale).astype(
                jnp.bfloat16
            )
            new_total = total + jnp.einsum(
                "hqk,khd->qhd", grad_scores, key_part, preferred_element_type=jnp.float32
            )
            grad_keys = jnp.einsum(
                "hqk,qhd->khd", grad_scores, query_heads, preferred_element_type=jnp.float32
            ).reshape(key_rows, model_width)
            grad_values = jnp.einsum(
                "hqk,qhd->khd",
                probs.astype(jnp.bfloat16),
                grad_heads,
                preferred_element_type=jnp.float32,
            ).reshape(key_rows, model_width)
            return (new_total, jnp.concatenate([grad_keys, grad_values], axis=1))

        def skip_part(total):
            return (total, jnp.zeros((key_rows, 2 * model_width), jnp.float32))

        grad_query_sum, kv_term = lax.cond(needed, backward_part, skip_part, grad_query_sum)
        kv_terms.append(kv_term)
    kv_shares = lax.psum_scatter(
        jnp.concatenate(kv_terms, axis=0).astype(jnp.bfloat16),
        "blk",
        scatter_dimension=0,
        tiled=True,
    ).astype(jnp.float32)
    grad_key_low = kv_shares[:, :model_width].astype(jnp.bfloat16)
    grad_value_low = kv_shares[:, model_width:].astype(jnp.bfloat16)
    grad_query_low = grad_query_sum.reshape(local_rows, model_width).astype(jnp.bfloat16)
    grad_query_w = jnp.einsum(
        "td,te->de", normed_low, grad_query_low, preferred_element_type=jnp.float32
    )
    grad_key_w = jnp.einsum(
        "td,te->de", normed_low, grad_key_low, preferred_element_type=jnp.float32
    )
    grad_value_w = jnp.einsum(
        "td,te->de", normed_low, grad_value_low, preferred_element_type=jnp.float32
    )
    grad_normed = (
        jnp.einsum("te,de->td", grad_query_low, query_back, preferred_element_type=jnp.float32)
        + jnp.einsum("te,de->td", grad_key_low, key_back, preferred_element_type=jnp.float32)
        + jnp.einsum("te,de->td", grad_value_low, value_back, preferred_element_type=jnp.float32)
    )
    grad_rows_one, grad_gain_one, grad_shift_one = first_pull(grad_normed)
    input_grad = (grad_residual + grad_rows_one).astype(jnp.bfloat16)
    shares = (
        lax.psum_scatter(grad_query_w, ("dp", "blk"), scatter_dimension=0, tiled=True),
        lax.psum_scatter(grad_key_w, ("dp", "blk"), scatter_dimension=0, tiled=True),
        lax.psum_scatter(grad_value_w, ("dp", "blk"), scatter_dimension=0, tiled=True),
        lax.psum_scatter(grad_out_w, ("dp", "blk"), scatter_dimension=0, tiled=True),
        lax.psum_scatter(grad_up_w, ("dp", "blk"), scatter_dimension=0, tiled=True),
        lax.psum_scatter(grad_down_w, ("dp", "blk"), scatter_dimension=0, tiled=True),
        lax.psum_scatter(grad_up_shift, ("dp", "blk"), scatter_dimension=0, tiled=True),
        lax.psum_scatter(grad_down_shift, ("dp", "blk"), scatter_dimension=0, tiled=True),
        lax.psum_scatter(grad_gain_one, ("dp", "blk"), scatter_dimension=0, tiled=True),
        lax.psum_scatter(grad_shift_one, ("dp", "blk"), scatter_dimension=0, tiled=True),
        lax.psum_scatter(grad_gain_two, ("dp", "blk"), scatter_dimension=0, tiled=True),
        lax.psum_scatter(grad_shift_two, ("dp", "blk"), scatter_dimension=0, tiled=True),
    )
    return (
        output,
        input_grad,
        shares[0],
        shares[1],
        shares[2],
        shares[3],
        shares[4],
        shares[5],
        shares[6],
        shares[7],
        shares[8],
        shares[9],
        shares[10],
        shares[11],
    )


def solution(mesh):
    in_specs = (
        P(("dp", "blk"), None),
        P(("dp", "blk")),
        P(("dp", "blk"), None),
        P(("dp", "blk"), None),
        P(("dp", "blk"), None),
        P(("dp", "blk"), None),
        P(("dp", "blk"), None),
        P(("dp", "blk"), None),
        P(("dp", "blk")),
        P(("dp", "blk")),
        P(("dp", "blk")),
        P(("dp", "blk")),
        P(("dp", "blk")),
        P(("dp", "blk")),
        P(("dp", "blk"), None),
    )
    out_specs = (
        P(("dp", "blk"), None),
        P(("dp", "blk"), None),
        P(("dp", "blk"), None),
        P(("dp", "blk"), None),
        P(("dp", "blk"), None),
        P(("dp", "blk"), None),
        P(("dp", "blk"), None),
        P(("dp", "blk"), None),
        P(("dp", "blk")),
        P(("dp", "blk")),
        P(("dp", "blk")),
        P(("dp", "blk")),
        P(("dp", "blk")),
        P(("dp", "blk")),
    )
    n_dp, n_blk = mesh.shape["dp"], mesh.shape["blk"]

    def layer(*args):
        fits = n_blk == RANKS and n_dp == 2 * RANKS and args[2].shape[0] // (n_dp * n_blk) % 16 == 0
        call = jax.shard_map(
            call_fused if fits else local, mesh=mesh, in_specs=in_specs, out_specs=out_specs, check_vma=False
        )
        return call(*args)

    return layer
```

```python
import functools
import math
import types

import jax
import jax.numpy as jnp
from jax import lax
from jax.experimental import pallas as pl
from jax.experimental.pallas import tpu as pltpu
from jax.sharding import PartitionSpec as P

MESH = pl.DeviceIdType.MESH
F32 = jnp.float32
BF16 = jnp.bfloat16
HEADS = 8
VMEM_BYTES = 60 * 2**20
RANKS = 4
eps = 1e-05
masked_value = -1e30
GELU_K = math.sqrt(2.0 / math.pi)
GELU_C = 0.044715


def dot_nn(a, b):
    return lax.dot_general(a, b, (((1,), (0,)), ((), ())), preferred_element_type=F32)


def dot_nt(a, b):
    return lax.dot_general(a, b, (((1,), (1,)), ((), ())), preferred_element_type=F32)


def dot_tn(a, b):
    return lax.dot_general(a, b, (((0,), (0,)), ((), ())), preferred_element_type=F32)


def norm_parts(v):
    centre = jnp.mean(v, axis=-1, keepdims=True)
    centred = v - centre
    variance = jnp.mean(centred * centred, axis=-1, keepdims=True)
    rstd = lax.rsqrt(variance + eps)
    return centred * rstd, rstd


def norm_back(g, gain, xhat, rstd):
    e = g * gain
    return rstd * (
        e
        - jnp.mean(e, axis=-1, keepdims=True)
        - xhat * jnp.mean(e * xhat, axis=-1, keepdims=True)
    )


def hidden_at(k, tt):
    return ((k // 2) * 2 + tt % 2) * 4 + (k % 2) * 2 + tt // 2


IN_NAMES = ("x_in", "dz_in", "pos", "wq", "wk", "wv", "wo", "wup", "wdn", "db", "g1", "b1", "g2", "b2", "ub")
OUT_NAMES = ("out", "ig", "peq", "peu", "go", "gdn", "gvec")


def scratch_of(rows, width, hid, rw, fw):
    half = rows // 2
    hd = width // HEADS
    cols = 3 * 2 * hd
    dma = pltpu.SemaphoreType.DMA
    V = pltpu.VMEM
    names = dict(
        X=V((4, 2, half, width), BF16),
        DZ=V((4, 2, half, width), BF16),
        ST=V((4, 2, 16, 128), BF16),
        WA=V((4, 2, 2, 2 * rw, cols), BF16),
        WOP=V((8, rw, width), BF16),
        WO=V((2, 2, 2, rw, width), BF16),
        VEC=V((8, 16, width), BF16),
        WU=V((4, 2, 2, 2 * rw, hid), BF16),
        WD=V((8, fw, width), BF16),
        PV=V((4, 16, width), BF16),
        VF=V((8, width), F32),
        SV=V((8, rw), F32),
        VT=V((16, width), F32),
        vec=V((16, width), BF16),
        st_in=V((16, 128), BF16),
        TU=V((256, 4 * rows), BF16),
        N1=V((4 * rows, width), BF16),
        QKV=V((4 * rows, cols), BF16),
        P0=V((2, rows, rows), BF16),
        P1=V((2, rows, 2 * rows), BF16),
        P2=V((2, rows, 3 * rows), BF16),
        P3=V((2, rows, 4 * rows), BF16),
        MIX=V((4 * rows, 2 * hd), BF16),
        DMIX=V((rows, 2 * hd), BF16),
        PR0=V((4, 2, half, width), BF16),
        PR1=V((4, 2, half, width), BF16),
        RBa=V((4, half, width), BF16),
        RBb=V((4, half, width), BF16),
        RBc=V((4, half, width), BF16),
        RXa=V((4, half, width), BF16),
        RXb=V((2, half, width), BF16),
        RXc=V((4, half, width), BF16),
        RXd=V((2, half, width), BF16),
        RES=V((4, half, width), F32),
        KEEP=V((2, half, width), F32),
        N2=V((4, 2, half, width), BF16),
        HID=V((4 * rows, hid), BF16),
        DP=V((4 * rows, hid), BF16),
        DB=V((4, 2, half, width), BF16),
        ACC=V((4 * rows, 4 * hd), F32),
        TT=V((width // 2, 4 * rows), BF16),
        YSF=V((2, 4, fw, width), BF16),
        R1F=V((2, 4, fw, width), BF16),
        R2F=V((2, 2, fw, width), BF16),
        R3F=V((2, fw, width), BF16),
        YSQ=V((2, 4, 2 * rw, cols), BF16),
        R1Q=V((2, 4, 2 * rw, cols), BF16),
        R2Q=V((2, 2, 2 * rw, cols), BF16),
        R3Q=V((2, 2 * rw, cols), BF16),
        GOB=V((2, 2, 2, rw, width), BF16),
        GOR=V((2, 2, rw, width), BF16),
        GOS=V((8, rw, width), BF16),
        GOT=V((8, rw, width), BF16),
        OD=V((fw, width), F32),
        OO=V((rw, width), F32),
        OUTB=V((2, half, width), BF16),
        IGB=V((2, half, width), BF16),
        VSUM=V((8, width), F32),
        VMID=V((8, width), F32),
        VR1=V((4, 8, width), F32),
        VR2=V((8, 8, width), F32),
        sp_s=dma((3, 8)),
        sp_r=dma((3, 4, 2)),
        loc=dma((4,)),
        load=dma((7,)),
        pre_s=dma((3, 3)),
        pre_r=dma((3, 4)),
        ag_s=dma((6, 7)),
        ag_r=dma((6, 8)),
        sw_s=dma((4,)),
        sw_r=dma((4,)),
        sw_s2=dma((4,)),
        sw_r2=dma((4,)),
        FIN=V((2, 2 * rw, cols), BF16),
        FIU=V((fw, hid), BF16),
        sib_s=dma((4, 4)),
        sib_r=dma((4, 4)),
        xs=dma((4, 4)),
        xr=dma((4, 4)),
        n2_s=dma((4,)),
        n2_r=dma((4,)),
        db_s=dma((4,)),
        db_r=dma((4,)),
        r1_s=dma((4, 4)),
        r1_r=dma((4, 4)),
        up_s=dma((4, 4)),
        up_r=dma((4, 4)),
        r2_s=dma((4, 2)),
        r2_r=dma((4, 2)),
        r3_s=dma((4,)),
        r3_r=dma((4,)),
        go_s=dma((8,)),
        go_r=dma((8,)),
        pe_s=dma((2, 4)),
        pe_r=dma((2, 4)),
        v1_s=dma((3,)),
        v1_r=dma((4,)),
        v2_s=dma((7,)),
        v2_r=dma((8,)),
        ret_s=dma((2, 2)),
        ret_r=dma((2, 2)),
    )
    return names


def fused(names, *all_refs):
    m = types.SimpleNamespace(**dict(zip(names, all_refs)))
    half, width = m.X.shape[2:]
    rows = 2 * half
    hid = m.HID.shape[1]
    rw = m.WOP.shape[1]
    fw = m.WD.shape[1]
    hd = width // HEADS
    two = 2 * hd
    scale = 1.0 / math.sqrt(hd)

    dp = lax.axis_index("dp")
    z = lax.axis_index("blk")
    yx = lax.div(dp, 2)
    y, x, c = lax.div(dp, 4), lax.rem(yx, 2), lax.rem(dp, 2)
    q, p = lax.div(z, 2), lax.rem(z, 2)
    t = p * 2 + c
    me = yx * 2 + q

    def dev(yy, xx, cc, zz):
        return ((yy * 2 + xx) * 2 + cc, zz)

    def mate(tt):
        return dev(y, x, lax.rem(tt, 2), q * 2 + lax.div(tt, 2))

    def peer(yy, xx, qq):
        return dev(yy, xx, c, qq * 2 + p)

    def at8(yy, xx, qq):
        return yy * 4 + xx * 2 + qq

    sib = dev(y, x, 1 - c, z)
    nbr = dev(y, x, c, q * 2 + 1 - p)
    over = {"q": peer(y, x, 1 - q), "x": peer(y, 1 - x, q), "y": peer(1 - y, x, q)}

    mine = (p, p + 2)
    theirs = (1 - p, 3 - p)

    sent = []

    def remote(src, dst, ssem, rsem, device):
        return pltpu.make_async_remote_copy(
            src_ref=src,
            dst_ref=dst,
            send_sem=ssem,
            recv_sem=rsem,
            device_id=device,
            device_id_type=MESH,
        )

    def push(src, dst, ssem, rsem, device, keep=True):
        copy = remote(src, dst, ssem, rsem, device)
        copy.start()
        if keep:
            sent.append(copy)
        return copy

    homes = []

    def push_if(cond, src, dst, ssem, rsem, device):
        copy = remote(src, dst, ssem, rsem, device)

        @pl.when(cond)
        def _():
            copy.start()

        homes.append((jnp.logical_not(cond), copy))

    def arrived(dst, rsem):
        pltpu.make_async_copy(dst, dst, rsem).wait()

    loads = [pltpu.make_async_copy(ref, m.PR1.at[k, 0, pl.ds(0, rw)], m.load.at[k]) for k, ref in enumerate((m.wq, m.wk, m.wv))]
    loads += [
        pltpu.make_async_copy(m.wup.at[:, pl.ds(k * width, width)], m.PR1.at[k, 1, pl.ds(0, rw)], m.load.at[3 + k])
        for k in range(4)
    ]
    for copy in loads:
        copy.start()
    m.st_in[...] = jnp.broadcast_to((z * rows - m.pos[0:1, 0:1]).astype(F32), (16, 128)).astype(BF16)
    for k, ref in enumerate((m.db, m.g1, m.b1, m.g2, m.b2)):
        m.SV[k : k + 1] = ref[...].astype(F32)
    m.SV[5:8] = jnp.zeros((3, rw), F32)
    spot = lax.broadcasted_iota(jnp.int32, (rw, width), 1) - (dp * 4 + z) * rw
    hot = jnp.where(spot == lax.broadcasted_iota(jnp.int32, (rw, width), 0), 1.0, 0.0).astype(BF16)
    m.VT[0:8] = dot_nn(m.SV[...].astype(BF16), hot)
    m.VT[8:16] = jnp.zeros((8, width), F32)
    m.VT[5:6, pl.ds(pl.multiple_of(me * fw, 128), fw)] = m.ub[...].astype(F32)
    m.vec[...] = m.VT[...].astype(BF16)

    barrier = pltpu.get_barrier_semaphore()
    flips = [(a, b, d) for a in range(2) for b in range(2) for d in range(2)]

    def flipped(a, b, d):
        return ((1 - y if a else y), (1 - x if b else x), (1 - q if d else q))

    others = [dev(y, x, lax.rem(c + a, 2), lax.rem(z + b, 4)) for a in range(2) for b in range(4) if a or b] + [
        peer(*flipped(*f)) for f in flips if f[0] or f[1]
    ]
    for device in others:
        pl.semaphore_signal(barrier, inc=1, device_id=device, device_id_type=MESH)
    pl.semaphore_wait(barrier, len(others))

    def half_rows(ref):
        return lambda k: ref.at[pl.ds(k * half, half)]

    streams = (
        (half_rows(m.x_in), m.X),
        (lambda k: m.st_in, m.ST),
        (half_rows(m.dz_in), m.DZ),
    )
    to_z = 2 * c + p

    def spread_home(k, stays):
        src, buf = streams[k]
        for cc in range(2):
            dst = buf.at[z, cc]
            rsem = m.sp_r.at[k, z, cc]
            copy = remote(src(cc), dst, m.sp_s.at[k, cc], rsem, dev(y, x, cc, to_z))
            if stays:

                @pl.when((q == c) & (c == cc))
                def _():
                    pltpu.make_async_copy(src(cc), dst, rsem).start()

                @pl.when((q == c) & (c != cc))
                def _():
                    copy.start()

                homes.append(((q == c) & (c == cc), copy))
            else:

                @pl.when(q != c)
                def _():
                    copy.start()

    held = (z, lax.rem(z + 2, 4))
    beside = (2 * q + 1 - p, lax.rem(2 * q + 3 - p, 4))

    def spread_own(k, far):
        _, buf = streams[k]
        i = held[far]
        arrived(buf.at[i, c], m.sp_r.at[k, i, c])
        push(buf.at[i, c], buf.at[i, c], m.sp_s.at[k, 2 + 2 * far], m.sp_r.at[k, i, c], nbr)
        push(buf.at[i, c], buf.at[i, c], m.sp_s.at[k, 3 + 2 * far], m.sp_r.at[k, i, c], sib)

    def spread_nbr(k, far):
        _, buf = streams[k]
        j = beside[far]
        arrived(buf.at[j, c], m.sp_r.at[k, j, c])
        push(buf.at[j, c], buf.at[j, c], m.sp_s.at[k, 6 + far], m.sp_r.at[k, j, c], sib)

    def spread_end(k):
        _, buf = streams[k]
        for i in held + beside:
            arrived(buf.at[i, 1 - c], m.sp_r.at[k, i, 1 - c])

    for k in range(2):
        spread_home(k, False)
        spread_home(k, True)
    spread_home(2, True)

    for copy in loads:
        copy.wait()
    for tt in range(4):
        at = 0
        for k in range(3):
            for j in range(2):
                m.PR0[tt, 1, 0:rw, at : at + hd] = m.PR1[k, 0, 0:rw, (j * 4 + tt) * hd : (j * 4 + tt + 1) * hd]
                at += hd
        for k in range(8):
            row, at = divmod(hidden_at(k, tt) * fw, width)
            m.PR0[tt, 0, 0:rw, k * fw : (k + 1) * fw] = m.PR1[row, 1, 0:rw, at : at + fw]
    cols = 3 * two

    def pre_src(n, tt):
        if n == 0:
            return m.PR0.at[tt, 1, pl.ds(0, rw), pl.ds(0, cols)]
        if n == 1:
            return m.vec
        return m.PR0.at[tt, 0, pl.ds(0, rw), pl.ds(0, hid)]

    def rank_rows(cc, pp):
        return (yx, cc, q, pl.ds(pl.multiple_of(pp * rw, rw), rw))

    def pre_dst(n, tt):
        if n == 1:
            return m.PV.at[tt]
        return (m.WA if n == 0 else m.WU).at[rank_rows(lax.rem(tt, 2), lax.div(tt, 2))]

    pre_sent = []

    def pre_send(n):
        for d in (1, 2, 3):
            tt = lax.rem(t + d, 4)
            pre_sent.append(
                push(pre_src(n, tt), pre_dst(n, t), m.pre_s.at[n, d - 1], m.pre_r.at[n, t], mate(tt), keep=False)
            )

    pre_send(1)
    pre_send(0)
    local_o = pltpu.make_async_copy(m.wo, m.WOP.at[me], m.loc.at[0])
    local_o.start()
    local_d = pltpu.make_async_copy(m.wdn, m.WD.at[me], m.loc.at[1])
    local_d.start()
    m.WA[rank_rows(c, p)] = m.PR0[t, 1, 0:rw, 0:cols]
    m.WU[rank_rows(c, p)] = m.PR0[t, 0, 0:rw, 0:hid]
    m.PV[t] = m.vec[...]

    def pre_wait(n):
        for d in (1, 2, 3):
            tt = lax.rem(t + d, 4)
            arrived(pre_dst(n, tt), m.pre_r.at[n, tt])

    def piece(n, yy, xx, qq):
        if n < 2:
            return m.WA.at[yy * 2 + xx, n, qq]
        if n == 4:
            return m.WU.at[yy * 2 + xx, :, qq]
        return {2: m.VEC, 3: m.WOP, 5: m.WD}[n].at[at8(yy, xx, qq)]

    def order(n):
        return "xy" if n in (0, 2, 4) else "yx"

    def beyond(first, qq):
        return (y, 1 - x, qq) if first == "x" else (1 - y, x, qq)

    def gather_send(n, spot, k, to):
        ref = piece(n, *spot)
        push(ref, ref, m.ag_s.at[n, k], m.ag_r.at[n, at8(*spot)], over[to])

    def gather_own(group, steps=(0, 1, 2)):
        for k in steps:
            for n in group:
                gather_send(n, (y, x, q), k, ("q" + order(n))[k])

    def gather_pass(group, k):
        for n in group:
            first, second = order(n)
            spot = (y, x, 1 - q) if k == 0 else beyond(first, q if k == 1 else 1 - q)
            arrived(piece(n, *spot), m.ag_r.at[n, at8(*spot)])
            if k == 0:
                gather_send(n, spot, 3, first)
                gather_send(n, spot, 4, second)
            else:
                gather_send(n, spot, 4 + k, second)

    def gather_end(group):
        for n in group:
            second = order(n)[1]
            for a in range(2):
                for qq in range(2):
                    spot = (1 - y, a, qq) if second == "y" else (a, 1 - x, qq)
                    arrived(piece(n, *spot), m.ag_r.at[n, at8(*spot)])

    VECS, ATT, WOUT, FFN = (2,), (0, 1), (3,), (4, 5)

    def norm_one(i, h):
        xhat, _ = norm_parts(m.X[i, h].astype(F32))
        at = pl.ds(pl.multiple_of(i * rows + h * half, half), half)
        m.N1[at, :] = (xhat * m.VF[1:2] + m.VF[2:3]).astype(BF16)

    def vec_own():
        pre_wait(1)
        total = sum((m.PV[a].astype(F32) for a in range(1, 4)), m.PV[0].astype(F32))
        line = lax.broadcasted_iota(jnp.int32, (16, width), 0)
        own_vec = jnp.where(line == 5, m.vec[...].astype(F32), total)
        m.VEC[me] = own_vec.astype(BF16)
        gather_own(VECS)

    def vec_end():
        gather_end(VECS)
        every = m.VEC[0].astype(F32)
        for a in range(1, 8):
            every = every + m.VEC[a].astype(F32)
        m.VF[...] = every[0:8]

    def swap_out():
        gather_end(WOUT)
        for yy in range(2):
            for qq in range(2):
                k = yy * 2 + qq
                push(
                    m.WOP.at[at8(yy, 1 - p, qq)], m.WO.at[yy, qq, p], m.sw_s.at[k], m.sw_r.at[k], nbr
                )
                m.WO[yy, qq, p] = m.WOP[at8(yy, p, qq)]

    def swap_end():
        for yy in range(2):
            for qq in range(2):
                arrived(m.WO.at[yy, qq, 1 - p], m.sw_r.at[yy * 2 + qq])

    spread_own(0, 0)
    spread_own(1, 0)
    vec_own()
    pre_wait(0)
    gather_own(ATT)
    pre_send(2)
    local_o.wait()
    local_d.wait()
    gather_pass(VECS, 0)
    gather_own(WOUT)
    gather_pass(VECS, 1)
    spread_nbr(0, 0)
    spread_nbr(1, 0)
    gather_pass(VECS, 2)
    pre_wait(2)
    for copy in pre_sent:
        copy.wait_send()
    vec_end()
    norm_one(held[0], c)
    norm_one(beside[0], c)
    gather_pass(ATT, 0)
    spread_own(0, 1)
    spread_own(1, 1)
    gather_own(FFN, (1, 2))
    norm_one(held[1], c)
    gather_pass(ATT, 1)
    gather_pass(WOUT, 0)
    spread_own(2, 0)
    gather_own(FFN, (0,))
    gather_pass(ATT, 2)
    spread_home(2, False)
    gather_pass(WOUT, 1)
    gather_pass(WOUT, 2)
    spread_nbr(0, 1)
    spread_nbr(1, 1)
    norm_one(beside[1], c)
    swap_out()
    spread_end(0)
    spread_end(1)
    for i in held + beside:
        norm_one(i, 1 - c)
    gather_end(ATT)

    def row_tile(i):
        return pl.ds(pl.multiple_of(i * rows, rows), rows)

    def col_tile(n, size=256):
        return pl.ds(pl.multiple_of(n * size, size), size)

    @pl.loop(0, 3)
    def _(n):
        w = m.WA[:, :, :, :, col_tile(n)].reshape(width, 256)

        @pl.loop(0, 4)
        def _(i):
            m.QKV[row_tile(i), col_tile(n)] = dot_nn(m.N1[row_tile(i), :], w).astype(BF16)

    EX = (
        (m.PR0, m.RBa, m.RXa),
        (m.PR1, m.RBb, m.RXb),
        (m.PR0, m.RBa, m.RXc),
        (m.PR1, m.RBc, m.RXd),
    )
    ex_open = {}
    ex_far = {1: [], 3: []}

    def ex_put(e, i, cols_at, value):
        pair = EX[e][0]
        low = value.astype(BF16)
        pair[i, 0, :, cols_at] = low[0:half]
        pair[i, 1, :, cols_at] = low[half:rows]

    def ex_send(e, i):
        pair, rb, _ = EX[e]
        ex_open[e, i] = [push(pair.at[i, 1 - c], rb.at[i], m.sib_s.at[e, i], m.sib_r.at[e, i], sib, keep=False)]

    def ex_mid(e, i):
        pair, rb, rx = EX[e]
        arrived(rb.at[i], m.sib_r.at[e, i])
        pair[i, c] = (pair[i, c].astype(F32) + rb[i].astype(F32)).astype(BF16)
        if e in (0, 2):
            ex_open[e, i].append(push(pair.at[i, c], rx.at[i], m.xs.at[e, i], m.xr.at[e, i], nbr, keep=False))
        else:
            copy = remote(pair.at[i, c], rx.at[i // 2], m.xs.at[e, i], m.xr.at[e, i // 2], nbr)
            far = p != i % 2

            @pl.when(far)
            def _():
                copy.start()

            ex_far[e].append((jnp.logical_not(far), copy))

    def ex_close(e, i):
        for copy in ex_open[e, i]:
            copy.wait_send()
        ex_open[e, i] = []

    def ex_total(e, i):
        pair, _, rx = EX[e]
        arrived(rx.at[i], m.xr.at[e, i])
        return pair[i, c].astype(F32) + rx[i].astype(F32)

    PS = (m.P0, m.P1, m.P2, m.P3)

    def attend(i):
        span = (i + 1) * rows
        r0 = i * rows
        start = m.ST[i, 0][0:1, 0:1].astype(F32)
        for j in range(2):
            q = m.QKV[r0 : r0 + rows, j * hd : (j + 1) * hd]
            k = m.QKV[0:span, two + j * hd : two + (j + 1) * hd]
            s = dot_nt(q, k) * scale
            row = lax.broadcasted_iota(jnp.int32, (rows, span), 0) + r0
            col = lax.broadcasted_iota(jnp.int32, (rows, span), 1)
            s = jnp.where((col <= row) & (col.astype(F32) >= start), s, masked_value)
            e = jnp.exp(s - jnp.max(s, axis=-1, keepdims=True))
            p = (e * (1.0 / jnp.sum(e, axis=-1, keepdims=True))).astype(BF16)
            PS[i][j] = p
            v = m.QKV[0:span, 2 * two + j * hd : 2 * two + (j + 1) * hd]
            m.MIX[r0 : r0 + rows, j * hd : (j + 1) * hd] = dot_nn(p, v).astype(BF16)

    def attend_out(i):
        r0 = i * rows

        @pl.loop(0, 4)
        def _(n):
            w = m.WO[:, :, :, :, col_tile(n)].reshape(two, 256)
            ex_put(0, i, col_tile(n), dot_nn(m.MIX[r0 : r0 + rows, :], w))

        ex_send(0, i)

    def second_norm(i):
        res = m.X[i, c].astype(F32) + ex_total(0, i)
        m.RES[i] = res
        xhat, _ = norm_parts(res)
        m.N2[i, c] = (xhat * m.VF[3:4] + m.VF[4:5]).astype(BF16)
        push(m.N2.at[i, c], m.N2.at[i, c], m.n2_s.at[i], m.n2_r.at[i], sib)

    m.VSUM[...] = jnp.zeros((8, width), F32)

    def feed(n):
        tile = col_tile(n)
        w_in = m.WU[:, :, :, :, tile].reshape(width, 256)
        w_back = m.WD[pl.ds(n * (256 // fw), 256 // fw)].reshape(256, width)

        @pl.loop(0, 4)
        def _(i):
            pre = dot_nn(m.N2[i].reshape(rows, width), w_in) + m.VF[5:6, tile]
            back = dot_nt(m.DZ[i].reshape(rows, width), w_back)
            sq = pre * pre
            th = jnp.tanh(GELU_K * pre * (1.0 + GELU_C * sq))
            m.HID[row_tile(i), tile] = (0.5 * pre * (1.0 + th)).astype(BF16)
            slope = 0.5 * (1.0 + th) + 0.5 * pre * (1.0 - th * th) * (GELU_K * (1.0 + 3.0 * GELU_C * sq))
            dpre = back * slope
            m.VSUM[5:6, tile] += jnp.sum(dpre, axis=0, keepdims=True)
            m.DP[row_tile(i), tile] = dpre.astype(BF16)

    def feed_two(i):
        r0 = i * rows
        ex_close(0, i)

        @pl.loop(0, width // 256)
        def _(n):
            w = m.WU[n].reshape(256, hid)
            ex_put(2, i, col_tile(n), dot_nt(m.DP[r0 : r0 + rows, :], w))

        ex_send(2, i)

    def feed_out(i):
        r0 = i * rows

        @pl.loop(0, width // 256)
        def _(n):
            w = m.WD[:, :, col_tile(n)].reshape(hid, 256)
            ex_put(1, i, col_tile(n), dot_nn(m.HID[r0 : r0 + rows, :], w))

        ex_send(1, i)

    def feed_back(i):
        xhat, rstd = norm_parts(m.RES[i])
        g = ex_total(2, i)
        a = 0.5 * jnp.sum(g * xhat, axis=0, keepdims=True)
        b = 0.5 * jnp.sum(g, axis=0, keepdims=True)
        m.VSUM[3:4] += a
        m.VSUM[4:5] += b

        @pl.when(p == i % 2)
        def _():
            m.KEEP[i // 2] = m.RES[i]

        dres = m.DZ[i, c].astype(F32) + norm_back(g, m.VF[3:4], xhat, rstd)
        m.RES[i] = dres
        m.DB[i, c] = dres.astype(BF16)
        push(m.DB.at[i, c], m.DB.at[i, c], m.db_s.at[i], m.db_r.at[i], sib)

    def lane(ref, at):
        return ref[:, pl.ds(pl.multiple_of(at * 128, 128), 128)]

    def lane_n2(at):
        return m.N2[:, :, :, pl.ds(pl.multiple_of(at * 128, 128), 128)].reshape(4 * rows, 128)

    def flip(parts):
        for a, part in enumerate(parts):
            m.TT[a * 128 : (a + 1) * 128, :] = part.T

    SEND = (m.YSF.at[0], m.YSF.at[1], m.YSQ.at[0], m.YSQ.at[1])
    GOT1 = (m.R1F.at[0], m.R1F.at[1], m.R1Q.at[0], m.R1Q.at[1])
    GOT2 = (m.R2F.at[0], m.R2F.at[1], m.R2Q.at[0], m.R2Q.at[1])
    GOT3 = (m.R3F.at[0], m.R3F.at[1], m.R3Q.at[0], m.R3Q.at[1])
    AXES = ("yx", "xy", "yx", "xy")
    open1 = {0: [], 1: [], 2: [], 3: []}
    fh = fw // 2

    def step1(w, slots):
        for k in slots:
            open1[w].append(
                push(SEND[w].at[k], GOT1[w].at[k], m.r1_s.at[w, k], m.r1_r.at[w, k], over[AXES[w][0]], keep=False)
            )

    def up_lhs(yy):
        flip([lane_n2((yy * 2 + a // 2) * 2 + a % 2) for a in range(4)])

    def up_parts(res):
        return [
            ((a // 2) * 2 + b, (a % 2) * fh, res[a * 128 + b * fh : a * 128 + (b + 1) * fh])
            for a in range(4)
            for b in range(2)
        ]

    def far_tile(k):
        return 2 * k + 1 - x if k < 2 else 2 * (k - 2) + x

    def up_far(k):
        s = col_tile(far_tile(k))
        for slot, at, part in up_parts(dot_nn(m.TT[...], m.DP[:, s])):
            m.YSF[0, slot, at : at + fh, s] = part.astype(BF16)
        for slot in range(4):
            src, dst = m.YSF.at[0, slot, :, s], m.R1F.at[0, slot, :, s]
            open1[0].append(push(src, dst, m.up_s.at[k, slot], m.up_r.at[k, slot], over["y"], keep=False))

    def down_far(k):
        for a in range(2):
            m.TU[a * 128 : (a + 1) * 128, :] = lane(m.HID, far_tile(k) * 2 + a).T

        @pl.loop(0, width // 256)
        def _(n):
            s = col_tile(n)
            res = dot_nn(m.TU[...], m.DZ[:, :, :, s].reshape(4 * rows, 256)).astype(BF16)
            m.YSF[1, 2 * k, :, s] = res[0:fw]
            m.YSF[1, 2 * k + 1, :, s] = res[fw : 2 * fw]

        step1(1, (2 * k, 2 * k + 1))

    def qkv_lhs(yy, xx):
        flip([lane(m.N1, (yy * 2 + a) * 2) for a in range(2)] + [lane(m.N1, (a * 2 + xx) * 2 + 1) for a in range(2)])

    def qkv_parts(res):
        return [
            (a // 2, (a % 2) * 2 + b, res[a * 128 + b * fh : a * 128 + (b + 1) * fh]) for a in range(4) for b in range(2)
        ]

    def qkv_far():
        qkv_lhs(1 - y, 1 - x)

        @pl.loop(0, 3)
        def _(n):
            s = col_tile(n)
            for e, slot, part in qkv_parts(dot_nn(m.TT[...], m.QKV[:, s])):
                m.YSQ[e, slot, :, s] = part.astype(BF16)

        step1(2, range(4))
        step1(3, range(4))

    def near_wait(w):
        for copy in open1[w]:
            copy.wait_send()
        for slot in range(4):
            if w:
                arrived(GOT1[w].at[slot], m.r1_r.at[w, slot])
            else:
                for k in range(4):
                    arrived(m.R1F.at[0, slot, :, col_tile(far_tile(k))], m.up_r.at[k, slot])

    def step2(w):
        first, second = AXES[w]
        there = 1 - (x if second == "x" else y)
        for qq in range(2):
            push(
                SEND[w].at[there * 2 + qq], GOT2[w].at[qq], m.r2_s.at[w, qq], m.r2_r.at[w, qq], over[second]
            )

    def up_near():
        up_lhs(y)
        near_wait(0)

        @pl.loop(0, hid // 256)
        def _(n):
            s = col_tile(n)
            for slot, at, part in up_parts(dot_nn(m.TT[...], m.DP[:, s])):
                to = slice(at, at + fh)
                m.YSF[0, slot, to, s] = (part + m.R1F[0, slot, to, s].astype(F32)).astype(BF16)

        step2(0)

    def down_near():
        near_wait(1)
        for k in range(2):
            for a in range(2):
                m.TU[a * 128 : (a + 1) * 128, :] = lane(m.HID, far_tile(k + 2) * 2 + a).T

            @pl.loop(0, width // 256)
            def _(n):
                s = col_tile(n)
                res = dot_nn(m.TU[...], m.DZ[:, :, :, s].reshape(4 * rows, 256))
                for b in range(2):
                    got = m.R1F[1, 2 * k + b, :, s].astype(F32)
                    m.YSF[1, 2 * k + b, :, s] = (res[b * fw : (b + 1) * fw] + got).astype(BF16)

        step2(1)

    def qkv_near():
        qkv_lhs(y, x)
        near_wait(2)
        near_wait(3)

        @pl.loop(0, 3)
        def _(n):
            s = col_tile(n)
            for e, slot, part in qkv_parts(dot_nn(m.TT[...], m.QKV[:, s])):
                m.YSQ[e, slot, :, s] = (part + m.R1Q[e, slot, :, s].astype(F32)).astype(BF16)

        step2(2)
        step2(3)

    def here(w):
        return x if AXES[w][1] == "x" else y

    def grad_mid(w):
        for qq in range(2):
            arrived(GOT2[w].at[qq], m.r2_r.at[w, qq])
            slot = here(w) * 2 + qq
            SEND[w][slot] = (SEND[w][slot].astype(F32) + GOT2[w][qq].astype(F32)).astype(BF16)
        push(SEND[w].at[here(w) * 2 + 1 - q], GOT3[w], m.r3_s.at[w], m.r3_r.at[w], over["q"])

    def grad_sum(w):
        arrived(GOT3[w], m.r3_r.at[w])
        return SEND[w][here(w) * 2 + q].astype(F32) + GOT3[w][...].astype(F32)

    def out_first():
        flip([lane(m.MIX, a) for a in range(2)])

        @pl.loop(0, width // 256)
        def _(n):
            s = col_tile(n)
            res = dot_nn(m.TT[0:two, :], m.DB[:, :, :, s].reshape(4 * rows, 256)).astype(BF16)
            m.GOB[:, :, :, :, s] = res.reshape(2, 2, 2, rw, 256)

        for yy in range(2):
            for qq in range(2):
                k = yy * 2 + qq
                push(m.GOB.at[yy, qq, 1 - p], m.GOR.at[yy, qq], m.sw_s2.at[k], m.sw_r2.at[k], nbr)

    def out_second():
        for yy in range(2):
            for qq in range(2):
                k = yy * 2 + qq
                arrived(m.GOR.at[yy, qq], m.sw_r2.at[k])
                m.GOS[at8(yy, p, qq)] = m.GOB[yy, qq, p]
                m.GOS[at8(yy, 1 - p, qq)] = m.GOR[yy, qq]
        for yy in range(2):
            for qq in range(2):
                k = yy * 2 + qq
                push(m.GOS.at[at8(yy, 1 - x, qq)], m.GOT.at[k], m.go_s.at[k], m.go_r.at[k], over["x"])

    def out_add(at, k):
        arrived(m.GOT.at[k], m.go_r.at[k])
        m.GOS[at] = (m.GOS[at].astype(F32) + m.GOT[k].astype(F32)).astype(BF16)

    def out_third():
        for yy in range(2):
            for qq in range(2):
                out_add(at8(yy, x, qq), yy * 2 + qq)
        for qq in range(2):
            push(m.GOS.at[at8(1 - y, x, qq)], m.GOT.at[4 + qq], m.go_s.at[4 + qq], m.go_r.at[4 + qq], over["y"])

    def out_fourth():
        for qq in range(2):
            out_add(at8(y, x, qq), 4 + qq)
        push(m.GOS.at[at8(y, x, 1 - q)], m.GOT.at[6], m.go_s.at[6], m.go_r.at[6], over["q"])

    def out_sum():
        arrived(m.GOT.at[6], m.go_r.at[6])
        m.OO[...] = m.GOS[me].astype(F32) + m.GOT[6].astype(F32)

    def give(e, src_of, dst):
        pltpu.make_async_copy(src_of(c, p), dst.at[t], m.pe_r.at[e, t]).start()
        for d in (1, 2, 3):
            tt = lax.rem(t + d, 4)
            push(src_of(lax.rem(tt, 2), lax.div(tt, 2)), dst.at[t], m.pe_s.at[e, d - 1], m.pe_r.at[e, t], mate(tt))

    def give_end():
        for e, dst in ((0, m.peu), (1, m.peq)):
            for tt in range(4):
                arrived(dst.at[tt], m.pe_r.at[e, tt])

    attend(0)
    swap_end()
    attend_out(0)
    gather_pass(FFN, 0)
    attend(1)
    attend_out(1)
    ex_mid(0, 0)
    attend(2)
    attend_out(2)
    gather_pass(FFN, 1)
    ex_mid(0, 1)
    second_norm(0)
    attend(3)
    attend_out(3)
    ex_mid(0, 2)
    gather_pass(FFN, 2)
    second_norm(1)
    ex_mid(0, 3)
    spread_nbr(2, 0)
    spread_own(2, 1)
    second_norm(2)
    second_norm(3)
    spread_nbr(2, 1)
    for i in range(4):
        arrived(m.N2.at[i, 1 - c], m.n2_r.at[i])
    up_lhs(1 - y)
    spread_end(2)
    gather_end(FFN)
    for k in range(4):
        feed(far_tile(k))
        if k < 2:
            down_far(k)
            up_far(k)
    feed_two(0)
    up_far(2)
    feed_two(1)
    ex_mid(2, 0)
    up_far(3)
    feed_two(2)
    ex_mid(2, 1)
    feed_two(3)
    ex_mid(2, 2)
    feed_out(0)
    ex_mid(2, 3)
    for i in (1, 2, 3):
        feed_out(i)
    feed_back(0)
    feed_back(1)
    down_near()
    up_near()

    def db_end(i):
        arrived(m.DB.at[i, 1 - c], m.db_r.at[i])

    def attend_back(i):
        span = (i + 1) * rows
        r0 = i * rows
        m.DMIX[...] = dot_nt(m.DB[i].reshape(rows, width), m.WO[...].reshape(two, width)).astype(BF16)
        for j in range(2):
            k0, v0 = two + j * hd, 2 * two + j * hd
            do = m.DMIX[:, j * hd : (j + 1) * hd]
            p = PS[i][j]
            pf = p.astype(F32)
            g = dot_nt(do, m.QKV[0:span, v0 : v0 + hd])
            delta = jnp.sum(pf * g, axis=-1, keepdims=True)
            ds = (pf * (g - delta) * scale).astype(BF16)
            q = m.QKV[r0 : r0 + rows, j * hd : (j + 1) * hd]
            dk = dot_tn(ds, q)
            dv = dot_tn(p, do)
            dq = dot_nn(ds, m.QKV[0:span, k0 : k0 + hd])
            ka, va = slice(j * hd, (j + 1) * hd), slice(two + j * hd, two + (j + 1) * hd)
            if i:
                m.ACC[0:r0, ka] += dk[0:r0]
                m.ACC[0:r0, va] += dv[0:r0]
            m.ACC[r0:span, ka] = dk[r0:span]
            m.ACC[r0:span, va] = dv[r0:span]
            m.QKV[r0 : r0 + rows, j * hd : (j + 1) * hd] = dq.astype(BF16)

    def give_back(k, kk, buf, dst):
        i = mine[kk]
        near = (q == c) & (i == z)
        to = dst.at[pl.ds(pl.multiple_of(c * half, half), half)]
        rsem = m.ret_r.at[k, c]

        @pl.when(near)
        def _():
            pltpu.make_async_copy(buf.at[kk], to, rsem).start()

        copy = remote(buf.at[kk], to, m.ret_s.at[k, kk], rsem, dev(y, x, q, i))

        @pl.when(jnp.logical_not(near))
        def _():
            copy.start()

        homes.append((near, copy))

    def far_close(e):
        for near, copy in ex_far.pop(e):

            @pl.when(jnp.logical_not(near))
            def _():
                copy.wait_send()

    def finish_out(kk):
        i = mine[kk]
        arrived(m.RXb.at[kk], m.xr.at[1, kk])
        value = m.KEEP[kk] + m.PR1[i, c].astype(F32) + m.RXb[kk].astype(F32) + m.VF[0:1]
        m.OUTB[kk] = value.astype(BF16)
        give_back(0, kk, m.OUTB, m.out)

    def first_back(i):
        r0 = i * rows

        @pl.loop(0, width // 256)
        def _(n):
            w = m.WA[n].reshape(256, cols)
            ex_put(3, i, col_tile(n), dot_nt(m.QKV[r0 : r0 + rows, :], w))

        ex_send(3, i)

    def finish_in(kk):
        i = mine[kk]
        arrived(m.RXd.at[kk], m.xr.at[3, kk])
        g = m.PR1[i, c].astype(F32) + m.RXd[kk].astype(F32)
        xhat, rstd = norm_parts(m.X[i, c].astype(F32))
        parts = (
            jnp.sum(m.DZ[i, c].astype(F32), axis=0, keepdims=True),
            jnp.sum(g * xhat, axis=0, keepdims=True),
            jnp.sum(g, axis=0, keepdims=True),
        )
        for k, part in enumerate(parts):
            m.VSUM[k : k + 1] += part
        m.IGB[kk] = (m.RES[i] + norm_back(g, m.VF[1:2], xhat, rstd)).astype(BF16)
        give_back(1, kk, m.IGB, m.ig)

    db_end(0)
    attend_back(0)
    feed_back(2)
    db_end(1)
    attend_back(1)
    feed_back(3)
    for i in range(4):
        ex_mid(1, i)
    db_end(2)
    attend_back(2)
    db_end(3)
    out_first()
    grad_mid(1)
    attend_back(3)

    @pl.loop(0, 4)
    def _(i):
        m.QKV[row_tile(i), two : 3 * two] = m.ACC[row_tile(i), :].astype(BF16)

    qkv_far()
    grad_mid(0)
    finish_out(0)
    finish_out(1)
    out_second()
    far_close(1)
    for i in range(4):
        ex_close(1, i)
    for i in range(4):
        first_back(i)
        if i:
            ex_mid(3, i - 1)
    ex_mid(3, 3)
    out_third()
    qkv_near()
    out_fourth()
    grad_mid(2)
    grad_mid(3)
    finish_in(0)
    finish_in(1)

    for d in (1, 2, 3):
        tt = lax.rem(t + d, 4)
        push(m.VSUM, m.VR1.at[t], m.v1_s.at[d - 1], m.v1_r.at[t], mate(tt))
    rest = m.VSUM[...]
    for d in (1, 2, 3):
        tt = lax.rem(t + d, 4)
        arrived(m.VR1.at[tt], m.v1_r.at[tt])
        rest = rest + m.VR1[tt]
    row8 = lax.broadcasted_iota(jnp.int32, (8, width), 0)
    m.VMID[...] = jnp.where(row8 == 5, m.VSUM[...], rest)
    for k, f in enumerate(flips):
        if k:
            push(m.VMID, m.VR2.at[me], m.v2_s.at[k - 1], m.v2_r.at[me], peer(*flipped(*f)))
    m.OD[...] = grad_sum(1)
    keep_down = pltpu.make_async_copy(m.OD, m.gdn, m.loc.at[2])
    keep_down.start()
    m.FIU[...] = grad_sum(0).astype(BF16)
    give(0, lambda cc, pp: m.FIU.at[pl.ds(pl.multiple_of((cc * 2 + pp) * rw, rw), rw)], m.peu)
    out_sum()
    keep_out = pltpu.make_async_copy(m.OO, m.go, m.loc.at[3])
    keep_out.start()
    for e in range(2):
        m.FIN[e] = grad_sum(2 + e).astype(BF16)
    give(1, lambda cc, pp: m.FIN.at[cc, pl.ds(pl.multiple_of(pp * rw, rw), rw)], m.peq)

    final = m.VMID[...]
    for k, f in enumerate(flips):
        if k:
            at = at8(*flipped(*f))
            arrived(m.VR2.at[at], m.v2_r.at[at])
            final = final + m.VR2[at]
    m.gvec[...] = final

    for k, dst in enumerate((m.out, m.ig)):
        for cc in range(2):
            arrived(dst.at[pl.ds(cc * half, half)], m.ret_r.at[k, cc])
    give_end()
    keep_down.wait()
    keep_out.wait()
    for copy in sent:
        copy.wait_send()
    for e, i in ex_open:
        ex_close(e, i)
    far_close(3)
    for near, copy in homes:

        @pl.when(jnp.logical_not(near))
        def _():
            copy.wait_send()


def place_outputs(out_i, ig_i, peq, peu, go_i, gdn_i, out, ig, gq, gk, gv, go, gup, gdn, PQ, PU, GQ, GU, A, B, GO, GD, sem):
    pairs = ((peq, PQ), (peu, PU), (out_i, A), (ig_i, B), (go_i, GO), (gdn_i, GD))
    moves = [pltpu.make_async_copy(src, dst, sem.at[k]) for k, (src, dst) in enumerate(pairs)]
    for move in moves:
        move.start()
    results = ((A, out), (B, ig), (GO, go), (GD, gdn), (GQ.at[0], gq), (GQ.at[1], gk), (GQ.at[2], gv), (GU, gup))
    last = [pltpu.make_async_copy(src, dst, sem.at[6 + k]) for k, (src, dst) in enumerate(results)]
    hd = PQ.shape[2] // 6
    fw = PU.shape[2] // 8
    moves[0].wait()
    moves[1].wait()
    for tt in range(RANKS):
        for j in range(2):
            a = (j * RANKS + tt) * hd
            for n in range(3):
                GQ[n, :, a : a + hd] = PQ[tt, :, (n * 2 + j) * hd : (n * 2 + j + 1) * hd].astype(F32)
        for k in range(8):
            a = hidden_at(k, tt) * fw
            GU[:, a : a + fw] = PU[tt, :, k * fw : (k + 1) * fw].astype(F32)
    for k in range(4):
        last[4 + k].start()
    for k in range(4):
        moves[2 + k].wait()
        last[k].start()
    for move in last:
        move.wait()


def call_fused(inputs, positions, w_query, w_key, w_value, w_out, w_up, w_down, up_bias, down_bias,
               ln1_gain, ln1_bias, ln2_gain, ln2_bias, cotangent):
    rows, width = inputs.shape
    hid = w_up.shape[1] // RANKS
    rw, fw = w_query.shape[0], w_down.shape[0]
    shapes = scratch_of(rows, width, hid, rw, fw)
    dp, blk = lax.axis_index("dp"), lax.axis_index("blk")
    n_blk = lax.axis_size("blk")
    place = dp * n_blk + blk
    at_up = dp // 2 * 2 + blk // 2
    small_in = [v.reshape(1, -1) for v in (down_bias, ln1_gain, ln1_bias, ln2_gain, ln2_bias, up_bias)]
    names = IN_NAMES + OUT_NAMES + tuple(shapes)
    any_, vm = pl.BlockSpec(memory_space=pl.ANY), pl.BlockSpec(memory_space=pltpu.VMEM)
    S = jax.ShapeDtypeStruct
    cols = 3 * 2 * (width // HEADS)
    tokens, wide = S((rows, width), BF16), S((rw, width), F32)
    moved = (S((RANKS, rw, cols), BF16), S((RANKS, rw, hid), BF16))
    out, ig, peq, peu, go, gdn, gvec = pl.pallas_call(
        functools.partial(fused, names),
        out_shape=(tokens, tokens) + moved + (wide, S(w_down.shape, F32), S((8, width), F32)),
        in_specs=[any_, any_, vm] + [any_] * 6 + [vm] * 6,
        out_specs=[any_] * 6 + [vm],
        scratch_shapes=list(shapes.values()),
        compiler_params=pltpu.CompilerParams(
            collective_id=0, has_side_effects=True, vmem_limit_bytes=VMEM_BYTES
        ),
        cost_estimate=pl.CostEstimate(flops=23 * 10**9, bytes_accessed=10**7, transcendentals=10**6),
    )(inputs, cotangent, positions.reshape(2, -1), w_query, w_key, w_value, w_out, w_up, w_down, *small_in)
    out, ig, gq, gk, gv, go, gup, gdn = pl.pallas_call(
        place_outputs,
        out_shape=(tokens, tokens, wide, wide, wide, wide, S(w_up.shape, F32), S(w_down.shape, F32)),
        in_specs=[any_] * 6,
        out_specs=[any_] * 8,
        scratch_shapes=[
            pltpu.VMEM(moved[0].shape, BF16),
            pltpu.VMEM(moved[1].shape, BF16),
            pltpu.VMEM((3, rw, width), F32),
            pltpu.VMEM(w_up.shape, F32),
            pltpu.VMEM((rows, width), BF16),
            pltpu.VMEM((rows, width), BF16),
            pltpu.VMEM((rw, width), F32),
            pltpu.VMEM(w_down.shape, F32),
            pltpu.SemaphoreType.DMA((14,)),
        ],
        compiler_params=pltpu.CompilerParams(vmem_limit_bytes=VMEM_BYTES),
    )(out, ig, peq, peu, go, gdn)
    small = lax.dynamic_slice(gvec, (0, place * rw), (5, rw))
    gup_bias = lax.dynamic_slice(gvec, (5, at_up * fw), (1, fw))[0]
    return (out, ig, gq, gk, gv, go, gup, gdn, gup_bias, small[0], small[1], small[2], small[3], small[4])


def layer_norm(values, gain, offset):
    centre = jnp.mean(values, axis=-1, keepdims=True)
    centred = values - centre
    variance = jnp.mean(centred * centred, axis=-1, keepdims=True)
    return centred * lax.rsqrt(variance + eps) * gain + offset


def smooth_gate(values):
    return jax.nn.gelu(values, approximate=True)


def keep_same(carry):
    return carry


def local(
    inputs,
    positions,
    w_query,
    w_key,
    w_value,
    w_out,
    w_up,
    w_down,
    up_bias,
    down_bias,
    ln1_gain,
    ln1_bias,
    ln2_gain,
    ln2_bias,
    cotangent,
):
    attn_full = (
        lax.all_gather(w_query, ("dp", "blk"), axis=0, tiled=True),
        lax.all_gather(w_key, ("dp", "blk"), axis=0, tiled=True),
        lax.all_gather(w_value, ("dp", "blk"), axis=0, tiled=True),
        lax.all_gather(w_out, ("dp", "blk"), axis=0, tiled=True),
        lax.all_gather(ln1_gain, ("dp", "blk"), axis=0, tiled=True),
        lax.all_gather(ln1_bias, ("dp", "blk"), axis=0, tiled=True),
    )
    ffn_full = (
        lax.all_gather(w_up, ("dp", "blk"), axis=0, tiled=True),
        lax.all_gather(w_down, ("dp", "blk"), axis=0, tiled=True),
        lax.all_gather(up_bias, ("dp", "blk"), axis=0, tiled=True),
        lax.all_gather(down_bias, ("dp", "blk"), axis=0, tiled=True),
        lax.all_gather(ln2_gain, ("dp", "blk"), axis=0, tiled=True),
        lax.all_gather(ln2_bias, ("dp", "blk"), axis=0, tiled=True),
    )
    token_rows = inputs.astype(jnp.float32)
    local_rows, model_width = token_rows.shape
    head_count = HEADS
    head_size = model_width // head_count
    score_scale = 1.0 / math.sqrt(head_size)
    normed_first, first_pull = jax.vjp(
        layer_norm, token_rows, attn_full[4].astype(jnp.float32), attn_full[5].astype(jnp.float32)
    )
    normed_low = normed_first.astype(jnp.bfloat16)
    query_low = jnp.dot(normed_low, attn_full[0], preferred_element_type=jnp.float32).astype(
        jnp.bfloat16
    )
    key_low = jnp.dot(normed_low, attn_full[1], preferred_element_type=jnp.float32).astype(
        jnp.bfloat16
    )
    value_low = jnp.dot(normed_low, attn_full[2], preferred_element_type=jnp.float32).astype(
        jnp.bfloat16
    )
    keys_all, values_all = (
        lax.all_gather(key_low, "blk", axis=0, tiled=True),
        lax.all_gather(value_low, "blk", axis=0, tiled=True),
    )
    group_rows = keys_all.shape[0]
    key_rows = max(min(512, group_rows), local_rows)
    block_count = group_rows // key_rows
    first_row = lax.axis_index("blk") * local_rows
    query_index = first_row + jnp.arange(local_rows, dtype=jnp.int32)
    seq_start = query_index - positions
    earliest = jnp.min(seq_start)
    query_heads = query_low.reshape(local_rows, head_count, head_size)
    key_parts = []
    for which in range(block_count):
        begin = which * key_rows
        key_part = keys_all[begin : begin + key_rows].reshape(key_rows, head_count, head_size)
        value_part = values_all[begin : begin + key_rows].reshape(key_rows, head_count, head_size)
        key_index = begin + jnp.arange(key_rows, dtype=jnp.int32)
        allowed = (key_index[None, :] <= query_index[:, None]) & (
            key_index[None, :] >= seq_start[:, None]
        )
        needed = (begin <= first_row + local_rows - 1) & (begin + key_rows - 1 >= earliest)
        key_parts.append((key_part, value_part, allowed, needed))

    def scores_of(key_part, allowed):
        scores = (
            jnp.einsum("qhd,khd->hqk", query_heads, key_part, preferred_element_type=jnp.float32)
            * score_scale
        )
        return jnp.where(allowed[None], scores, masked_value)

    running_max = jnp.full((head_count, local_rows), masked_value, jnp.float32)
    running_sum = jnp.zeros((head_count, local_rows), jnp.float32)
    for key_part, value_part, allowed, needed in key_parts:

        def extend(carry):
            old_max, old_sum = carry
            scores = scores_of(key_part, allowed)
            new_max = jnp.maximum(old_max, jnp.max(scores, axis=-1))
            terms = jnp.where(allowed[None], jnp.exp(scores - new_max[..., None]), 0.0)
            return (new_max, old_sum * jnp.exp(old_max - new_max) + jnp.sum(terms, axis=-1))

        running_max, running_sum = lax.cond(needed, extend, keep_same, (running_max, running_sum))
    log_total = running_max + jnp.log(running_sum)

    def probs_of(key_part, allowed):
        scores = scores_of(key_part, allowed)
        return jnp.where(allowed[None], jnp.exp(scores - log_total[..., None]), 0.0)

    attended = jnp.zeros((local_rows, head_count, head_size), jnp.float32)
    for key_part, value_part, allowed, needed in key_parts:

        def gather_values(total):
            weights_low = probs_of(key_part, allowed).astype(jnp.bfloat16)
            return total + jnp.einsum(
                "hqk,khd->qhd", weights_low, value_part, preferred_element_type=jnp.float32
            )

        attended = lax.cond(needed, gather_values, keep_same, attended)
    mixed_low = attended.reshape(local_rows, model_width).astype(jnp.bfloat16)
    residual = token_rows + jnp.dot(mixed_low, attn_full[3], preferred_element_type=jnp.float32)
    normed_second, second_pull = jax.vjp(
        layer_norm, residual, ffn_full[4].astype(jnp.float32), ffn_full[5].astype(jnp.float32)
    )
    normed_two = normed_second.astype(jnp.bfloat16)
    preact = jnp.dot(normed_two, ffn_full[0], preferred_element_type=jnp.float32) + ffn_full[
        2
    ].astype(jnp.float32)
    gated, gate_pull = jax.vjp(smooth_gate, preact)
    hidden = gated.astype(jnp.bfloat16)
    output = (
        residual
        + jnp.dot(hidden, ffn_full[1], preferred_element_type=jnp.float32)
        + ffn_full[3].astype(jnp.float32)
    ).astype(jnp.bfloat16)
    up_back, down_back = (ffn_full[0], ffn_full[1])
    grad_final = cotangent.astype(jnp.float32)
    grad_down_w = jnp.einsum("tf,td->fd", hidden, cotangent, preferred_element_type=jnp.float32)
    grad_down_shift = jnp.sum(grad_final, axis=0)
    grad_hidden = jnp.einsum("td,fd->tf", cotangent, down_back, preferred_element_type=jnp.float32)
    grad_preact = gate_pull(grad_hidden)[0].astype(jnp.bfloat16)
    grad_up_shift = jnp.sum(grad_preact.astype(jnp.float32), axis=0)
    grad_up_w = jnp.einsum("td,tf->df", normed_two, grad_preact, preferred_element_type=jnp.float32)
    grad_normed_two = jnp.einsum(
        "tf,df->td", grad_preact, up_back, preferred_element_type=jnp.float32
    )
    grad_resid_two, grad_gain_two, grad_shift_two = second_pull(grad_normed_two)
    grad_residual = grad_final + grad_resid_two
    query_back, key_back, value_back, out_back = (
        attn_full[0],
        attn_full[1],
        attn_full[2],
        attn_full[3],
    )
    grad_branch = grad_residual.astype(jnp.bfloat16)
    grad_out_w = jnp.einsum("te,td->ed", mixed_low, grad_branch, preferred_element_type=jnp.float32)
    grad_mixed = jnp.einsum(
        "td,ed->te", grad_branch, out_back, preferred_element_type=jnp.float32
    ).astype(jnp.bfloat16)
    grad_heads = grad_mixed.reshape(local_rows, head_count, head_size)
    delta = jnp.zeros((head_count, local_rows), jnp.float32)
    for key_part, value_part, allowed, needed in key_parts:

        def add_delta(total):
            probs = probs_of(key_part, allowed)
            grad_probs = jnp.einsum(
                "qhd,khd->hqk", grad_heads, value_part, preferred_element_type=jnp.float32
            )
            return total + jnp.sum(probs * grad_probs, axis=-1)

        delta = lax.cond(needed, add_delta, keep_same, delta)
    grad_query_sum = jnp.zeros((local_rows, head_count, head_size), jnp.float32)
    kv_terms = []
    for key_part, value_part, allowed, needed in key_parts:

        def backward_part(total):
            probs = probs_of(key_part, allowed)
            grad_probs = jnp.einsum(
                "qhd,khd->hqk", grad_heads, value_part, preferred_element_type=jnp.float32
            )
            grad_scores = (probs * (grad_probs - delta[..., None]) * score_scale).astype(
                jnp.bfloat16
            )
            new_total = total + jnp.einsum(
                "hqk,khd->qhd", grad_scores, key_part, preferred_element_type=jnp.float32
            )
            grad_keys = jnp.einsum(
                "hqk,qhd->khd", grad_scores, query_heads, preferred_element_type=jnp.float32
            ).reshape(key_rows, model_width)
            grad_values = jnp.einsum(
                "hqk,qhd->khd",
                probs.astype(jnp.bfloat16),
                grad_heads,
                preferred_element_type=jnp.float32,
            ).reshape(key_rows, model_width)
            return (new_total, jnp.concatenate([grad_keys, grad_values], axis=1))

        def skip_part(total):
            return (total, jnp.zeros((key_rows, 2 * model_width), jnp.float32))

        grad_query_sum, kv_term = lax.cond(needed, backward_part, skip_part, grad_query_sum)
        kv_terms.append(kv_term)
    kv_shares = lax.psum_scatter(
        jnp.concatenate(kv_terms, axis=0).astype(jnp.bfloat16),
        "blk",
        scatter_dimension=0,
        tiled=True,
    ).astype(jnp.float32)
    grad_key_low = kv_shares[:, :model_width].astype(jnp.bfloat16)
    grad_value_low = kv_shares[:, model_width:].astype(jnp.bfloat16)
    grad_query_low = grad_query_sum.reshape(local_rows, model_width).astype(jnp.bfloat16)
    grad_query_w = jnp.einsum(
        "td,te->de", normed_low, grad_query_low, preferred_element_type=jnp.float32
    )
    grad_key_w = jnp.einsum(
        "td,te->de", normed_low, grad_key_low, preferred_element_type=jnp.float32
    )
    grad_value_w = jnp.einsum(
        "td,te->de", normed_low, grad_value_low, preferred_element_type=jnp.float32
    )
    grad_normed = (
        jnp.einsum("te,de->td", grad_query_low, query_back, preferred_element_type=jnp.float32)
        + jnp.einsum("te,de->td", grad_key_low, key_back, preferred_element_type=jnp.float32)
        + jnp.einsum("te,de->td", grad_value_low, value_back, preferred_element_type=jnp.float32)
    )
    grad_rows_one, grad_gain_one, grad_shift_one = first_pull(grad_normed)
    input_grad = (grad_residual + grad_rows_one).astype(jnp.bfloat16)
    shares = (
        lax.psum_scatter(grad_query_w, ("dp", "blk"), scatter_dimension=0, tiled=True),
        lax.psum_scatter(grad_key_w, ("dp", "blk"), scatter_dimension=0, tiled=True),
        lax.psum_scatter(grad_value_w, ("dp", "blk"), scatter_dimension=0, tiled=True),
        lax.psum_scatter(grad_out_w, ("dp", "blk"), scatter_dimension=0, tiled=True),
        lax.psum_scatter(grad_up_w, ("dp", "blk"), scatter_dimension=0, tiled=True),
        lax.psum_scatter(grad_down_w, ("dp", "blk"), scatter_dimension=0, tiled=True),
        lax.psum_scatter(grad_up_shift, ("dp", "blk"), scatter_dimension=0, tiled=True),
        lax.psum_scatter(grad_down_shift, ("dp", "blk"), scatter_dimension=0, tiled=True),
        lax.psum_scatter(grad_gain_one, ("dp", "blk"), scatter_dimension=0, tiled=True),
        lax.psum_scatter(grad_shift_one, ("dp", "blk"), scatter_dimension=0, tiled=True),
        lax.psum_scatter(grad_gain_two, ("dp", "blk"), scatter_dimension=0, tiled=True),
        lax.psum_scatter(grad_shift_two, ("dp", "blk"), scatter_dimension=0, tiled=True),
    )
    return (
        output,
        input_grad,
        shares[0],
        shares[1],
        shares[2],
        shares[3],
        shares[4],
        shares[5],
        shares[6],
        shares[7],
        shares[8],
        shares[9],
        shares[10],
        shares[11],
    )


def solution(mesh):
    in_specs = (
        P(("dp", "blk"), None),
        P(("dp", "blk")),
        P(("dp", "blk"), None),
        P(("dp", "blk"), None),
        P(("dp", "blk"), None),
        P(("dp", "blk"), None),
        P(("dp", "blk"), None),
        P(("dp", "blk"), None),
        P(("dp", "blk")),
        P(("dp", "blk")),
        P(("dp", "blk")),
        P(("dp", "blk")),
        P(("dp", "blk")),
        P(("dp", "blk")),
        P(("dp", "blk"), None),
    )
    out_specs = (
        P(("dp", "blk"), None),
        P(("dp", "blk"), None),
        P(("dp", "blk"), None),
        P(("dp", "blk"), None),
        P(("dp", "blk"), None),
        P(("dp", "blk"), None),
        P(("dp", "blk"), None),
        P(("dp", "blk"), None),
        P(("dp", "blk")),
        P(("dp", "blk")),
        P(("dp", "blk")),
        P(("dp", "blk")),
        P(("dp", "blk")),
        P(("dp", "blk")),
    )
    n_dp, n_blk = mesh.shape["dp"], mesh.shape["blk"]

    def layer(*args):
        fits = n_blk == RANKS and n_dp == 2 * RANKS and args[2].shape[0] // (n_dp * n_blk) % 16 == 0
        call = jax.shard_map(
            call_fused if fits else local, mesh=mesh, in_specs=in_specs, out_specs=out_specs, check_vma=False
        )
        return call(*args)

    return layer
```

```python
import functools
import math
import types

import jax
import jax.numpy as jnp
from jax import lax
from jax.experimental import pallas as pl
from jax.experimental.pallas import tpu as pltpu
from jax.sharding import PartitionSpec as P

MESH = pl.DeviceIdType.MESH
F32 = jnp.float32
BF16 = jnp.bfloat16
HEADS = 8
VMEM_BYTES = 60 * 2**20
RANKS = 4
eps = 1e-05
masked_value = -1e30
GELU_K = math.sqrt(2.0 / math.pi)
GELU_C = 0.044715


def dot_nn(a, b):
    return lax.dot_general(a, b, (((1,), (0,)), ((), ())), preferred_element_type=F32)


def dot_nt(a, b):
    return lax.dot_general(a, b, (((1,), (1,)), ((), ())), preferred_element_type=F32)


def dot_tn(a, b):
    return lax.dot_general(a, b, (((0,), (0,)), ((), ())), preferred_element_type=F32)


def norm_parts(v):
    centre = jnp.mean(v, axis=-1, keepdims=True)
    centred = v - centre
    variance = jnp.mean(centred * centred, axis=-1, keepdims=True)
    rstd = lax.rsqrt(variance + eps)
    return centred * rstd, rstd


def norm_back(g, gain, xhat, rstd):
    e = g * gain
    return rstd * (
        e
        - jnp.mean(e, axis=-1, keepdims=True)
        - xhat * jnp.mean(e * xhat, axis=-1, keepdims=True)
    )


def hidden_at(k, tt):
    return ((k // 2) * 2 + tt % 2) * 4 + (k % 2) * 2 + tt // 2


IN_NAMES = ("x_in", "dz_in", "pos", "wq", "wk", "wv", "wo", "wup", "wdn", "db", "g1", "b1", "g2", "b2", "ub")
OUT_NAMES = ("out", "ig", "peq", "peu", "go", "gdn", "gvec")


def scratch_of(rows, width, hid, rw, fw):
    half = rows // 2
    hd = width // HEADS
    cols = 3 * 2 * hd
    dma = pltpu.SemaphoreType.DMA
    V = pltpu.VMEM
    names = dict(
        X=V((4, 2, half, width), BF16),
        DZ=V((4, 2, half, width), BF16),
        ST=V((4, 2, 16, 128), BF16),
        WA=V((4, 2, 2, 2 * rw, cols), BF16),
        WOP=V((8, rw, width), BF16),
        WO=V((2, 2, 2, rw, width), BF16),
        VEC=V((8, 16, width), BF16),
        WU=V((4, 2, 2, 2 * rw, hid), BF16),
        WD=V((8, fw, width), BF16),
        PV=V((4, 16, width), BF16),
        VF=V((8, width), F32),
        SV=V((8, rw), F32),
        VT=V((16, width), F32),
        vec=V((16, width), BF16),
        st_in=V((16, 128), BF16),
        TU=V((256, 4 * rows), BF16),
        N1=V((4 * rows, width), BF16),
        QKV=V((4 * rows, cols), BF16),
        P0=V((2, rows, rows), BF16),
        P1=V((2, rows, 2 * rows), BF16),
        P2=V((2, rows, 3 * rows), BF16),
        P3=V((2, rows, 4 * rows), BF16),
        MIX=V((4 * rows, 2 * hd), BF16),
        DMIX=V((rows, 2 * hd), BF16),
        PR0=V((4, 2, half, width), BF16),
        PR1=V((4, 2, half, width), BF16),
        RBa=V((4, half, width), BF16),
        RBb=V((4, half, width), BF16),
        RBc=V((4, half, width), BF16),
        RXa=V((4, half, width), BF16),
        RXb=V((2, half, width), BF16),
        RXc=V((4, half, width), BF16),
        RXd=V((2, half, width), BF16),
        RES=V((4, half, width), F32),
        KEEP=V((2, half, width), F32),
        N2=V((4, 2, half, width), BF16),
        HID=V((4 * rows, hid), BF16),
        DP=V((4 * rows, hid), BF16),
        DB=V((4, 2, half, width), BF16),
        ACC=V((4 * rows, 4 * hd), F32),
        TT=V((width // 2, 4 * rows), BF16),
        YSF=V((2, 4, fw, width), BF16),
        R1F=V((2, 4, fw, width), BF16),
        R2F=V((2, 2, fw, width), BF16),
        R3F=V((2, fw, width), BF16),
        YSQ=V((2, 4, 2 * rw, cols), BF16),
        R1Q=V((2, 4, 2 * rw, cols), BF16),
        R2Q=V((2, 2, 2 * rw, cols), BF16),
        R3Q=V((2, 2 * rw, cols), BF16),
        GOB=V((2, 2, 2, rw, width), BF16),
        GOR=V((2, 2, rw, width), BF16),
        GOS=V((8, rw, width), BF16),
        GOT=V((8, rw, width), BF16),
        OD=V((fw, width), F32),
        OO=V((rw, width), F32),
        OUTB=V((2, half, width), BF16),
        IGB=V((2, half, width), BF16),
        VSUM=V((8, width), F32),
        VMID=V((8, width), F32),
        VR1=V((4, 8, width), F32),
        VR2=V((8, 2, 8, 128), F32),
        sp_s=dma((3, 8)),
        sp_r=dma((3, 4, 2)),
        loc=dma((4,)),
        load=dma((7,)),
        pre_s=dma((3, 3)),
        pre_r=dma((3, 4)),
        ag_s=dma((6, 7)),
        ag_r=dma((6, 8)),
        sw_s=dma((4,)),
        sw_r=dma((4,)),
        sw_s2=dma((4,)),
        sw_r2=dma((4,)),
        FIN=V((2, 2 * rw, cols), BF16),
        FIU=V((fw, hid), BF16),
        sib_s=dma((4, 4)),
        sib_r=dma((4, 4)),
        xs=dma((4, 4)),
        xr=dma((4, 4)),
        n2_s=dma((4,)),
        n2_r=dma((4,)),
        db_s=dma((4,)),
        db_r=dma((4,)),
        r1_s=dma((4, 4)),
        r1_r=dma((4, 4)),
        up_s=dma((4, 4)),
        up_r=dma((4, 4)),
        r2_s=dma((4, 2)),
        r2_r=dma((4, 2)),
        r3_s=dma((4,)),
        r3_r=dma((4,)),
        go_s=dma((8,)),
        go_r=dma((8,)),
        pe_s=dma((2, 4)),
        pe_r=dma((2, 4)),
        v1_s=dma((3,)),
        v1_r=dma((4,)),
        v2_s=dma((7, 2)),
        v2_r=dma((8, 2)),
        ret_s=dma((2, 2)),
        ret_r=dma((2, 2)),
    )
    return names


def fused(names, *all_refs):
    m = types.SimpleNamespace(**dict(zip(names, all_refs)))
    half, width = m.X.shape[2:]
    rows = 2 * half
    hid = m.HID.shape[1]
    rw = m.WOP.shape[1]
    fw = m.WD.shape[1]
    hd = width // HEADS
    two = 2 * hd
    scale = 1.0 / math.sqrt(hd)

    dp = lax.axis_index("dp")
    z = lax.axis_index("blk")
    yx = lax.div(dp, 2)
    y, x, c = lax.div(dp, 4), lax.rem(yx, 2), lax.rem(dp, 2)
    q, p = lax.div(z, 2), lax.rem(z, 2)
    t = p * 2 + c
    me = yx * 2 + q

    def dev(yy, xx, cc, zz):
        return ((yy * 2 + xx) * 2 + cc, zz)

    def mate(tt):
        return dev(y, x, lax.rem(tt, 2), q * 2 + lax.div(tt, 2))

    def peer(yy, xx, qq):
        return dev(yy, xx, c, qq * 2 + p)

    def at8(yy, xx, qq):
        return yy * 4 + xx * 2 + qq

    sib = dev(y, x, 1 - c, z)
    nbr = dev(y, x, c, q * 2 + 1 - p)
    over = {"q": peer(y, x, 1 - q), "x": peer(y, 1 - x, q), "y": peer(1 - y, x, q)}

    mine = (p, p + 2)
    theirs = (1 - p, 3 - p)

    sent = []

    def remote(src, dst, ssem, rsem, device):
        return pltpu.make_async_remote_copy(
            src_ref=src,
            dst_ref=dst,
            send_sem=ssem,
            recv_sem=rsem,
            device_id=device,
            device_id_type=MESH,
        )

    def push(src, dst, ssem, rsem, device, keep=True):
        copy = remote(src, dst, ssem, rsem, device)
        copy.start()
        if keep:
            sent.append(copy)
        return copy

    homes = []

    def push_if(cond, src, dst, ssem, rsem, device):
        copy = remote(src, dst, ssem, rsem, device)

        @pl.when(cond)
        def _():
            copy.start()

        homes.append((jnp.logical_not(cond), copy))

    def arrived(dst, rsem):
        pltpu.make_async_copy(dst, dst, rsem).wait()

    loads = [pltpu.make_async_copy(ref, m.PR1.at[k, 0, pl.ds(0, rw)], m.load.at[k]) for k, ref in enumerate((m.wq, m.wk, m.wv))]
    loads += [
        pltpu.make_async_copy(m.wup.at[:, pl.ds(k * width, width)], m.PR1.at[k, 1, pl.ds(0, rw)], m.load.at[3 + k])
        for k in range(4)
    ]
    for copy in loads:
        copy.start()
    m.st_in[...] = jnp.broadcast_to((z * rows - m.pos[0:1, 0:1]).astype(F32), (16, 128)).astype(BF16)
    for k, ref in enumerate((m.db, m.g1, m.b1, m.g2, m.b2)):
        m.SV[k : k + 1] = ref[...].astype(F32)
    m.SV[5:8] = jnp.zeros((3, rw), F32)
    spot = lax.broadcasted_iota(jnp.int32, (rw, width), 1) - (dp * 4 + z) * rw
    hot = jnp.where(spot == lax.broadcasted_iota(jnp.int32, (rw, width), 0), 1.0, 0.0).astype(BF16)
    m.VT[0:8] = dot_nn(m.SV[...].astype(BF16), hot)
    m.VT[8:16] = jnp.zeros((8, width), F32)
    m.VT[5:6, pl.ds(pl.multiple_of(me * fw, 128), fw)] = m.ub[...].astype(F32)
    m.vec[...] = m.VT[...].astype(BF16)

    barrier = pltpu.get_barrier_semaphore()
    flips = [(a, b, d) for a in range(2) for b in range(2) for d in range(2)]

    def flipped(a, b, d):
        return ((1 - y if a else y), (1 - x if b else x), (1 - q if d else q))

    others = [dev(y, x, lax.rem(c + a, 2), lax.rem(z + b, 4)) for a in range(2) for b in range(4) if a or b] + [
        peer(*flipped(*f)) for f in flips if f[0] or f[1]
    ]
    for device in others:
        pl.semaphore_signal(barrier, inc=1, device_id=device, device_id_type=MESH)
    pl.semaphore_wait(barrier, len(others))

    def half_rows(ref):
        return lambda k: ref.at[pl.ds(k * half, half)]

    streams = (
        (half_rows(m.x_in), m.X),
        (lambda k: m.st_in, m.ST),
        (half_rows(m.dz_in), m.DZ),
    )
    to_z = 2 * c + p

    def spread_home(k, stays):
        src, buf = streams[k]
        for cc in range(2):
            dst = buf.at[z, cc]
            rsem = m.sp_r.at[k, z, cc]
            copy = remote(src(cc), dst, m.sp_s.at[k, cc], rsem, dev(y, x, cc, to_z))
            if stays:

                @pl.when((q == c) & (c == cc))
                def _():
                    pltpu.make_async_copy(src(cc), dst, rsem).start()

                @pl.when((q == c) & (c != cc))
                def _():
                    copy.start()

                homes.append(((q == c) & (c == cc), copy))
            else:

                @pl.when(q != c)
                def _():
                    copy.start()

    held = (z, lax.rem(z + 2, 4))
    beside = (2 * q + 1 - p, lax.rem(2 * q + 3 - p, 4))

    def spread_own(k, far):
        _, buf = streams[k]
        i = held[far]
        arrived(buf.at[i, c], m.sp_r.at[k, i, c])
        push(buf.at[i, c], buf.at[i, c], m.sp_s.at[k, 2 + 2 * far], m.sp_r.at[k, i, c], nbr)
        push(buf.at[i, c], buf.at[i, c], m.sp_s.at[k, 3 + 2 * far], m.sp_r.at[k, i, c], sib)

    def spread_nbr(k, far):
        _, buf = streams[k]
        j = beside[far]
        arrived(buf.at[j, c], m.sp_r.at[k, j, c])
        push(buf.at[j, c], buf.at[j, c], m.sp_s.at[k, 6 + far], m.sp_r.at[k, j, c], sib)

    def spread_end(k):
        _, buf = streams[k]
        for i in held + beside:
            arrived(buf.at[i, 1 - c], m.sp_r.at[k, i, 1 - c])

    for k in range(2):
        spread_home(k, False)
        spread_home(k, True)
    spread_home(2, True)

    for copy in loads:
        copy.wait()
    for tt in range(4):
        at = 0
        for k in range(3):
            for j in range(2):
                m.PR0[tt, 1, 0:rw, at : at + hd] = m.PR1[k, 0, 0:rw, (j * 4 + tt) * hd : (j * 4 + tt + 1) * hd]
                at += hd
        for k in range(8):
            row, at = divmod(hidden_at(k, tt) * fw, width)
            m.PR0[tt, 0, 0:rw, k * fw : (k + 1) * fw] = m.PR1[row, 1, 0:rw, at : at + fw]
    cols = 3 * two

    def pre_src(n, tt):
        if n == 0:
            return m.PR0.at[tt, 1, pl.ds(0, rw), pl.ds(0, cols)]
        if n == 1:
            return m.vec
        return m.PR0.at[tt, 0, pl.ds(0, rw), pl.ds(0, hid)]

    def rank_rows(cc, pp):
        return (yx, cc, q, pl.ds(pl.multiple_of(pp * rw, rw), rw))

    def pre_dst(n, tt):
        if n == 1:
            return m.PV.at[tt]
        return (m.WA if n == 0 else m.WU).at[rank_rows(lax.rem(tt, 2), lax.div(tt, 2))]

    pre_sent = []

    def pre_send(n):
        for d in (1, 2, 3):
            tt = lax.rem(t + d, 4)
            pre_sent.append(
                push(pre_src(n, tt), pre_dst(n, t), m.pre_s.at[n, d - 1], m.pre_r.at[n, t], mate(tt), keep=False)
            )

    pre_send(1)
    pre_send(0)
    local_o = pltpu.make_async_copy(m.wo, m.WOP.at[me], m.loc.at[0])
    local_o.start()
    local_d = pltpu.make_async_copy(m.wdn, m.WD.at[me], m.loc.at[1])
    local_d.start()
    m.WA[rank_rows(c, p)] = m.PR0[t, 1, 0:rw, 0:cols]
    m.WU[rank_rows(c, p)] = m.PR0[t, 0, 0:rw, 0:hid]
    m.PV[t] = m.vec[...]

    def pre_wait(n):
        for d in (1, 2, 3):
            tt = lax.rem(t + d, 4)
            arrived(pre_dst(n, tt), m.pre_r.at[n, tt])

    def piece(n, yy, xx, qq):
        if n < 2:
            return m.WA.at[yy * 2 + xx, n, qq]
        if n == 4:
            return m.WU.at[yy * 2 + xx, :, qq]
        return {2: m.VEC, 3: m.WOP, 5: m.WD}[n].at[at8(yy, xx, qq)]

    def order(n):
        return "xy" if n in (0, 2, 4) else "yx"

    def beyond(first, qq):
        return (y, 1 - x, qq) if first == "x" else (1 - y, x, qq)

    def gather_send(n, spot, k, to):
        ref = piece(n, *spot)
        push(ref, ref, m.ag_s.at[n, k], m.ag_r.at[n, at8(*spot)], over[to])

    def gather_own(group, steps=(0, 1, 2)):
        for k in steps:
            for n in group:
                gather_send(n, (y, x, q), k, ("q" + order(n))[k])

    def gather_pass(group, k):
        for n in group:
            first, second = order(n)
            spot = (y, x, 1 - q) if k == 0 else beyond(first, q if k == 1 else 1 - q)
            arrived(piece(n, *spot), m.ag_r.at[n, at8(*spot)])
            if k == 0:
                gather_send(n, spot, 3, first)
                gather_send(n, spot, 4, second)
            else:
                gather_send(n, spot, 4 + k, second)

    def gather_end(group):
        for n in group:
            second = order(n)[1]
            for a in range(2):
                for qq in range(2):
                    spot = (1 - y, a, qq) if second == "y" else (a, 1 - x, qq)
                    arrived(piece(n, *spot), m.ag_r.at[n, at8(*spot)])

    VECS, ATT, WOUT, FFN = (2,), (0, 1), (3,), (4, 5)

    def norm_one(i, h):
        xhat, _ = norm_parts(m.X[i, h].astype(F32))
        at = pl.ds(pl.multiple_of(i * rows + h * half, half), half)
        m.N1[at, :] = (xhat * m.VF[1:2] + m.VF[2:3]).astype(BF16)

    def vec_own():
        pre_wait(1)
        total = sum((m.PV[a].astype(F32) for a in range(1, 4)), m.PV[0].astype(F32))
        line = lax.broadcasted_iota(jnp.int32, (16, width), 0)
        own_vec = jnp.where(line == 5, m.vec[...].astype(F32), total)
        m.VEC[me] = own_vec.astype(BF16)
        gather_own(VECS)

    def vec_end():
        gather_end(VECS)
        every = m.VEC[0].astype(F32)
        for a in range(1, 8):
            every = every + m.VEC[a].astype(F32)
        m.VF[...] = every[0:8]

    def swap_out():
        gather_end(WOUT)
        for yy in range(2):
            for qq in range(2):
                k = yy * 2 + qq
                push(
                    m.WOP.at[at8(yy, 1 - p, qq)], m.WO.at[yy, qq, p], m.sw_s.at[k], m.sw_r.at[k], nbr
                )
                m.WO[yy, qq, p] = m.WOP[at8(yy, p, qq)]

    def swap_end():
        for yy in range(2):
            for qq in range(2):
                arrived(m.WO.at[yy, qq, 1 - p], m.sw_r.at[yy * 2 + qq])

    spread_own(0, 0)
    spread_own(1, 0)
    vec_own()
    pre_wait(0)
    gather_own(ATT)
    pre_send(2)
    local_o.wait()
    local_d.wait()
    gather_pass(VECS, 0)
    gather_own(WOUT)
    gather_pass(VECS, 1)
    spread_nbr(0, 0)
    spread_nbr(1, 0)
    gather_pass(VECS, 2)
    pre_wait(2)
    for copy in pre_sent:
        copy.wait_send()
    vec_end()
    norm_one(held[0], c)
    norm_one(beside[0], c)
    gather_pass(ATT, 0)
    spread_own(0, 1)
    spread_own(1, 1)
    gather_own(FFN, (1, 2))
    gather_own(FFN, (0,))
    norm_one(held[1], c)
    gather_pass(ATT, 1)
    gather_pass(WOUT, 0)
    spread_own(2, 0)
    gather_pass(ATT, 2)
    spread_home(2, False)
    gather_pass(WOUT, 1)
    gather_pass(WOUT, 2)
    spread_nbr(0, 1)
    spread_nbr(1, 1)
    norm_one(beside[1], c)
    swap_out()
    spread_end(0)
    spread_end(1)
    for i in held + beside:
        norm_one(i, 1 - c)
    gather_end(ATT)

    def row_tile(i):
        return pl.ds(pl.multiple_of(i * rows, rows), rows)

    def col_tile(n, size=256):
        return pl.ds(pl.multiple_of(n * size, size), size)

    @pl.loop(0, 3)
    def _(n):
        w = m.WA[:, :, :, :, col_tile(n)].reshape(width, 256)

        for i in range(2):
            at = slice(2 * i * rows, (2 * i + 2) * rows)
            m.QKV[at, col_tile(n)] = dot_nn(m.N1[at, :], w).astype(BF16)

    EX = (
        (m.PR0, m.RBa, m.RXa),
        (m.PR1, m.RBb, m.RXb),
        (m.PR0, m.RBa, m.RXc),
        (m.PR0, m.RBc, m.RXd),
    )
    ex_open = {}
    ex_far = {1: [], 3: []}

    def ex_put(e, i, cols_at, value):
        pair = EX[e][0]
        low = value.astype(BF16)
        pair[i, 0, :, cols_at] = low[0:half]
        pair[i, 1, :, cols_at] = low[half:rows]

    def ex_send(e, i):
        pair, rb, _ = EX[e]
        ex_open[e, i] = [push(pair.at[i, 1 - c], rb.at[i], m.sib_s.at[e, i], m.sib_r.at[e, i], sib, keep=False)]

    def ex_mid(e, i):
        pair, rb, rx = EX[e]
        arrived(rb.at[i], m.sib_r.at[e, i])
        pair[i, c] = (pair[i, c].astype(F32) + rb[i].astype(F32)).astype(BF16)
        if e in (0, 2):
            ex_open[e, i].append(push(pair.at[i, c], rx.at[i], m.xs.at[e, i], m.xr.at[e, i], nbr, keep=False))
        else:
            copy = remote(pair.at[i, c], rx.at[i // 2], m.xs.at[e, i], m.xr.at[e, i // 2], nbr)
            far = p != i % 2

            @pl.when(far)
            def _():
                copy.start()

            ex_far[e].append((jnp.logical_not(far), copy))

    def ex_close(e, i):
        for copy in ex_open[e, i]:
            copy.wait_send()
        ex_open[e, i] = []

    def ex_total(e, i):
        pair, _, rx = EX[e]
        arrived(rx.at[i], m.xr.at[e, i])
        return pair[i, c].astype(F32) + rx[i].astype(F32)

    PS = (m.P0, m.P1, m.P2, m.P3)

    def attend(i):
        span = (i + 1) * rows
        r0 = i * rows
        start = m.ST[i, 0][0:1, 0:1].astype(F32)
        for j in range(2):
            q = m.QKV[r0 : r0 + rows, j * hd : (j + 1) * hd]
            k = m.QKV[0:span, two + j * hd : two + (j + 1) * hd]
            s = dot_nt(q, k) * scale
            row = lax.broadcasted_iota(jnp.int32, (rows, span), 0) + r0
            col = lax.broadcasted_iota(jnp.int32, (rows, span), 1)
            s = jnp.where((col <= row) & (col.astype(F32) >= start), s, masked_value)
            e = jnp.exp(s - jnp.max(s, axis=-1, keepdims=True))
            p = (e * (1.0 / jnp.sum(e, axis=-1, keepdims=True))).astype(BF16)
            PS[i][j] = p
            v = m.QKV[0:span, 2 * two + j * hd : 2 * two + (j + 1) * hd]
            m.MIX[r0 : r0 + rows, j * hd : (j + 1) * hd] = dot_nn(p, v).astype(BF16)

    def attend_out(i):
        r0 = i * rows

        @pl.loop(0, 4)
        def _(n):
            w = m.WO[:, :, :, :, col_tile(n)].reshape(two, 256)
            ex_put(0, i, col_tile(n), dot_nn(m.MIX[r0 : r0 + rows, :], w))

        ex_send(0, i)

    def second_norm(i):
        res = m.X[i, c].astype(F32) + ex_total(0, i)
        m.RES[i] = res
        xhat, _ = norm_parts(res)
        m.N2[i, c] = (xhat * m.VF[3:4] + m.VF[4:5]).astype(BF16)
        push(m.N2.at[i, c], m.N2.at[i, c], m.n2_s.at[i], m.n2_r.at[i], sib)

    m.VSUM[...] = jnp.zeros((8, width), F32)

    def feed(n):
        tile = col_tile(n)
        w_in = m.WU[:, :, :, :, tile].reshape(width, 256)
        w_back = m.WD[pl.ds(n * (256 // fw), 256 // fw)].reshape(256, width)

        @pl.loop(0, 4)
        def _(i):
            pre = dot_nn(m.N2[i].reshape(rows, width), w_in) + m.VF[5:6, tile]
            back = dot_nt(m.DZ[i].reshape(rows, width), w_back)
            sq = pre * pre
            th = jnp.tanh(GELU_K * pre * (1.0 + GELU_C * sq))
            m.HID[row_tile(i), tile] = (0.5 * pre * (1.0 + th)).astype(BF16)
            slope = 0.5 * (1.0 + th) + 0.5 * pre * (1.0 - th * th) * (GELU_K * (1.0 + 3.0 * GELU_C * sq))
            dpre = back * slope
            m.VSUM[5:6, tile] += jnp.sum(dpre, axis=0, keepdims=True)
            m.DP[row_tile(i), tile] = dpre.astype(BF16)

    def feed_two(i):
        r0 = i * rows
        ex_close(0, i)

        @pl.loop(0, width // 256)
        def _(n):
            w = m.WU[n].reshape(256, hid)
            ex_put(2, i, col_tile(n), dot_nt(m.DP[r0 : r0 + rows, :], w))

        ex_send(2, i)

    def feed_out(i):
        r0 = i * rows

        @pl.loop(0, width // 256)
        def _(n):
            w = m.WD[:, :, col_tile(n)].reshape(hid, 256)
            low = dot_nn(m.HID[r0 : r0 + 2 * rows, :], w).astype(BF16)
            for b in range(2):
                ex_put(1, i + b, col_tile(n), low[b * rows : (b + 1) * rows])

        ex_send(1, i)
        ex_send(1, i + 1)

    def feed_back(i):
        xhat, rstd = norm_parts(m.RES[i])
        g = ex_total(2, i)
        a = 0.5 * jnp.sum(g * xhat, axis=0, keepdims=True)
        b = 0.5 * jnp.sum(g, axis=0, keepdims=True)
        m.VSUM[3:4] += a
        m.VSUM[4:5] += b

        @pl.when(p == i % 2)
        def _():
            m.KEEP[i // 2] = m.RES[i]

        dres = m.DZ[i, c].astype(F32) + norm_back(g, m.VF[3:4], xhat, rstd)
        m.RES[i] = dres
        m.DB[i, c] = dres.astype(BF16)
        push(m.DB.at[i, c], m.DB.at[i, c], m.db_s.at[i], m.db_r.at[i], sib)

    def lane(ref, at):
        return ref[:, pl.ds(pl.multiple_of(at * 128, 128), 128)]

    def lane_n2(at):
        return m.N2[:, :, :, pl.ds(pl.multiple_of(at * 128, 128), 128)].reshape(4 * rows, 128)

    def flip(parts):
        for a, part in enumerate(parts):
            m.TT[a * 128 : (a + 1) * 128, :] = part.T

    SEND = (m.YSF.at[0], m.YSF.at[1], m.YSQ.at[0], m.YSQ.at[1])
    GOT1 = (m.R1F.at[0], m.R1F.at[1], m.R1Q.at[0], m.R1Q.at[1])
    GOT2 = (m.R2F.at[0], m.R2F.at[1], m.R2Q.at[0], m.R2Q.at[1])
    GOT3 = (m.R3F.at[0], m.R3F.at[1], m.R3Q.at[0], m.R3Q.at[1])
    AXES = ("yx", "xy", "yx", "xy")
    open1 = {0: [], 1: [], 2: [], 3: []}
    fh = fw // 2

    def step1(w, slots):
        for k in slots:
            open1[w].append(
                push(SEND[w].at[k], GOT1[w].at[k], m.r1_s.at[w, k], m.r1_r.at[w, k], over[AXES[w][0]], keep=False)
            )

    def up_lhs(yy):
        flip([lane_n2((yy * 2 + a // 2) * 2 + a % 2) for a in range(4)])

    def up_parts(res):
        return [
            ((a // 2) * 2 + b, (a % 2) * fh, res[a * 128 + b * fh : a * 128 + (b + 1) * fh])
            for a in range(4)
            for b in range(2)
        ]

    def far_tile(k):
        return 2 * k + 1 - x if k < 2 else 2 * (k - 2) + x

    def up_far(k):
        s = col_tile(far_tile(k))
        for slot, at, part in up_parts(dot_nn(m.TT[...], m.DP[:, s])):
            m.YSF[0, slot, at : at + fh, s] = part.astype(BF16)
        for slot in range(4):
            src, dst = m.YSF.at[0, slot, :, s], m.R1F.at[0, slot, :, s]
            open1[0].append(push(src, dst, m.up_s.at[k, slot], m.up_r.at[k, slot], over["y"], keep=False))

    def down_far(k):
        for a in range(2):
            m.TU[a * 128 : (a + 1) * 128, :] = lane(m.HID, far_tile(k) * 2 + a).T

        @pl.loop(0, width // 256)
        def _(n):
            s = col_tile(n)
            res = dot_nn(m.TU[...], m.DZ[:, :, :, s].reshape(4 * rows, 256)).astype(BF16)
            m.YSF[1, 2 * k, :, s] = res[0:fw]
            m.YSF[1, 2 * k + 1, :, s] = res[fw : 2 * fw]

        step1(1, (2 * k, 2 * k + 1))

    def qkv_lhs(yy, xx):
        flip([lane(m.N1, (yy * 2 + a) * 2) for a in range(2)] + [lane(m.N1, (a * 2 + xx) * 2 + 1) for a in range(2)])

    def qkv_parts(res):
        return [
            (a // 2, (a % 2) * 2 + b, res[a * 128 + b * fh : a * 128 + (b + 1) * fh]) for a in range(4) for b in range(2)
        ]

    def qkv_far():
        qkv_lhs(1 - y, 1 - x)

        @pl.loop(0, 3)
        def _(n):
            s = col_tile(n)
            for e, slot, part in qkv_parts(dot_nn(m.TT[...], m.QKV[:, s])):
                m.YSQ[e, slot, :, s] = part.astype(BF16)

        step1(2, range(4))
        step1(3, range(4))

    def near_wait(w):
        for copy in open1[w]:
            copy.wait_send()
        for slot in range(4):
            if w:
                arrived(GOT1[w].at[slot], m.r1_r.at[w, slot])
            else:
                for k in range(4):
                    arrived(m.R1F.at[0, slot, :, col_tile(far_tile(k))], m.up_r.at[k, slot])

    def step2(w):
        first, second = AXES[w]
        there = 1 - (x if second == "x" else y)
        for qq in range(2):
            push(
                SEND[w].at[there * 2 + qq], GOT2[w].at[qq], m.r2_s.at[w, qq], m.r2_r.at[w, qq], over[second]
            )

    def up_near():
        up_lhs(y)
        near_wait(0)

        @pl.loop(0, hid // 256)
        def _(n):
            s = col_tile(n)
            for slot, at, part in up_parts(dot_nn(m.TT[...], m.DP[:, s])):
                to = slice(at, at + fh)
                m.YSF[0, slot, to, s] = (part + m.R1F[0, slot, to, s].astype(F32)).astype(BF16)

        step2(0)

    def down_near():
        near_wait(1)
        for k in range(2):
            for a in range(2):
                m.TU[a * 128 : (a + 1) * 128, :] = lane(m.HID, far_tile(k + 2) * 2 + a).T

            @pl.loop(0, width // 256)
            def _(n):
                s = col_tile(n)
                res = dot_nn(m.TU[...], m.DZ[:, :, :, s].reshape(4 * rows, 256))
                for b in range(2):
                    got = m.R1F[1, 2 * k + b, :, s].astype(F32)
                    m.YSF[1, 2 * k + b, :, s] = (res[b * fw : (b + 1) * fw] + got).astype(BF16)

        step2(1)

    def qkv_near():
        qkv_lhs(y, x)
        near_wait(2)
        near_wait(3)

        @pl.loop(0, 3)
        def _(n):
            s = col_tile(n)
            for e, slot, part in qkv_parts(dot_nn(m.TT[...], m.QKV[:, s])):
                m.YSQ[e, slot, :, s] = (part + m.R1Q[e, slot, :, s].astype(F32)).astype(BF16)

        step2(2)
        step2(3)

    def here(w):
        return x if AXES[w][1] == "x" else y

    def grad_mid(w):
        for qq in range(2):
            arrived(GOT2[w].at[qq], m.r2_r.at[w, qq])
            slot = here(w) * 2 + qq
            SEND[w][slot] = (SEND[w][slot].astype(F32) + GOT2[w][qq].astype(F32)).astype(BF16)
        push(SEND[w].at[here(w) * 2 + 1 - q], GOT3[w], m.r3_s.at[w], m.r3_r.at[w], over["q"])

    def grad_sum(w):
        arrived(GOT3[w], m.r3_r.at[w])
        return SEND[w][here(w) * 2 + q].astype(F32) + GOT3[w][...].astype(F32)

    def out_first():
        flip([lane(m.MIX, a) for a in range(2)])

        @pl.loop(0, width // 256)
        def _(n):
            s = col_tile(n)
            res = dot_nn(m.TT[0:two, :], m.DB[:, :, :, s].reshape(4 * rows, 256)).astype(BF16)
            m.GOB[:, :, :, :, s] = res.reshape(2, 2, 2, rw, 256)

        for yy in range(2):
            for qq in range(2):
                k = yy * 2 + qq
                push(m.GOB.at[yy, qq, 1 - p], m.GOR.at[yy, qq], m.sw_s2.at[k], m.sw_r2.at[k], nbr)

    def out_second():
        for yy in range(2):
            for qq in range(2):
                k = yy * 2 + qq
                arrived(m.GOR.at[yy, qq], m.sw_r2.at[k])
                m.GOS[at8(yy, p, qq)] = m.GOB[yy, qq, p]
                m.GOS[at8(yy, 1 - p, qq)] = m.GOR[yy, qq]
        for yy in range(2):
            for qq in range(2):
                k = yy * 2 + qq
                push(m.GOS.at[at8(yy, 1 - x, qq)], m.GOT.at[k], m.go_s.at[k], m.go_r.at[k], over["x"])

    def out_add(at, k):
        arrived(m.GOT.at[k], m.go_r.at[k])
        m.GOS[at] = (m.GOS[at].astype(F32) + m.GOT[k].astype(F32)).astype(BF16)

    def out_third():
        for yy in range(2):
            for qq in range(2):
                out_add(at8(yy, x, qq), yy * 2 + qq)
        for qq in range(2):
            push(m.GOS.at[at8(1 - y, x, qq)], m.GOT.at[4 + qq], m.go_s.at[4 + qq], m.go_r.at[4 + qq], over["y"])

    def out_fourth():
        for qq in range(2):
            out_add(at8(y, x, qq), 4 + qq)
        push(m.GOS.at[at8(y, x, 1 - q)], m.GOT.at[6], m.go_s.at[6], m.go_r.at[6], over["q"])

    def out_sum():
        arrived(m.GOT.at[6], m.go_r.at[6])
        m.OO[...] = m.GOS[me].astype(F32) + m.GOT[6].astype(F32)

    def give(e, src_of, dst):
        pltpu.make_async_copy(src_of(c, p), dst.at[t], m.pe_r.at[e, t]).start()
        for d in (1, 2, 3):
            tt = lax.rem(t + d, 4)
            push(src_of(lax.rem(tt, 2), lax.div(tt, 2)), dst.at[t], m.pe_s.at[e, d - 1], m.pe_r.at[e, t], mate(tt))

    def give_end():
        for e, dst in ((0, m.peu), (1, m.peq)):
            for tt in range(4):
                arrived(dst.at[tt], m.pe_r.at[e, tt])

    attend(0)
    swap_end()
    attend_out(0)
    gather_pass(FFN, 0)
    attend(1)
    attend_out(1)
    ex_mid(0, 0)
    attend(2)
    attend_out(2)
    gather_pass(FFN, 1)
    ex_mid(0, 1)
    second_norm(0)
    attend(3)
    attend_out(3)
    ex_mid(0, 2)
    gather_pass(FFN, 2)
    second_norm(1)
    ex_mid(0, 3)
    spread_nbr(2, 0)
    spread_own(2, 1)
    second_norm(2)
    second_norm(3)
    spread_nbr(2, 1)
    for i in range(4):
        arrived(m.N2.at[i, 1 - c], m.n2_r.at[i])
    up_lhs(1 - y)
    spread_end(2)
    gather_end(FFN)
    for k in range(4):
        feed(far_tile(k))
        if k < 2:
            down_far(k)
            up_far(k)
    feed_two(0)
    up_far(2)
    feed_two(1)
    ex_mid(2, 0)
    up_far(3)
    feed_two(2)
    ex_mid(2, 1)
    feed_two(3)
    ex_mid(2, 2)
    ex_mid(2, 3)
    feed_out(0)
    feed_out(2)
    feed_back(0)
    feed_back(1)
    down_near()
    up_near()

    def db_end(i):
        arrived(m.DB.at[i, 1 - c], m.db_r.at[i])

    def attend_back(i):
        span = (i + 1) * rows
        r0 = i * rows
        m.DMIX[...] = dot_nt(m.DB[i].reshape(rows, width), m.WO[...].reshape(two, width)).astype(BF16)
        for j in range(2):
            k0, v0 = two + j * hd, 2 * two + j * hd
            do = m.DMIX[:, j * hd : (j + 1) * hd]
            p = PS[i][j]
            pf = p.astype(F32)
            g = dot_nt(do, m.QKV[0:span, v0 : v0 + hd])
            delta = jnp.sum(pf * g, axis=-1, keepdims=True)
            ds = (pf * (g - delta) * scale).astype(BF16)
            q = m.QKV[r0 : r0 + rows, j * hd : (j + 1) * hd]
            dk = dot_tn(ds, q)
            dv = dot_tn(p, do)
            dq = dot_nn(ds, m.QKV[0:span, k0 : k0 + hd])
            ka, va = slice(j * hd, (j + 1) * hd), slice(two + j * hd, two + (j + 1) * hd)
            if i:
                m.ACC[0:r0, ka] += dk[0:r0]
                m.ACC[0:r0, va] += dv[0:r0]
            m.ACC[r0:span, ka] = dk[r0:span]
            m.ACC[r0:span, va] = dv[r0:span]
            m.QKV[r0 : r0 + rows, j * hd : (j + 1) * hd] = dq.astype(BF16)

    def give_back(k, kk, buf, dst):
        i = mine[kk]
        near = (q == c) & (i == z)
        to = dst.at[pl.ds(pl.multiple_of(c * half, half), half)]
        rsem = m.ret_r.at[k, c]

        @pl.when(near)
        def _():
            pltpu.make_async_copy(buf.at[kk], to, rsem).start()

        copy = remote(buf.at[kk], to, m.ret_s.at[k, kk], rsem, dev(y, x, q, i))

        @pl.when(jnp.logical_not(near))
        def _():
            copy.start()

        homes.append((near, copy))

    def far_close(e):
        for near, copy in ex_far.pop(e):

            @pl.when(jnp.logical_not(near))
            def _():
                copy.wait_send()

    def finish_out(kk):
        i = mine[kk]
        arrived(m.RXb.at[kk], m.xr.at[1, kk])
        value = m.KEEP[kk] + m.PR1[i, c].astype(F32) + m.RXb[kk].astype(F32) + m.VF[0:1]
        m.OUTB[kk] = value.astype(BF16)
        give_back(0, kk, m.OUTB, m.out)

    def first_back(i):
        r0 = i * rows
        ex_close(2, i)

        @pl.loop(0, width // 256)
        def _(n):
            w = m.WA[n].reshape(256, cols)
            ex_put(3, i, col_tile(n), dot_nt(m.QKV[r0 : r0 + rows, :], w))

        ex_send(3, i)

    def finish_in(kk):
        i = mine[kk]
        arrived(m.RXd.at[kk], m.xr.at[3, kk])
        g = m.PR0[i, c].astype(F32) + m.RXd[kk].astype(F32)
        xhat, rstd = norm_parts(m.X[i, c].astype(F32))
        parts = (
            jnp.sum(m.DZ[i, c].astype(F32), axis=0, keepdims=True),
            jnp.sum(g * xhat, axis=0, keepdims=True),
            jnp.sum(g, axis=0, keepdims=True),
        )
        for k, part in enumerate(parts):
            m.VSUM[k : k + 1] += part
        m.IGB[kk] = (m.RES[i] + norm_back(g, m.VF[1:2], xhat, rstd)).astype(BF16)
        give_back(1, kk, m.IGB, m.ig)

    db_end(0)
    attend_back(0)
    feed_back(2)
    db_end(1)
    attend_back(1)
    feed_back(3)
    for i in range(4):
        ex_mid(1, i)
    db_end(2)
    attend_back(2)
    db_end(3)
    out_first()
    grad_mid(1)
    attend_back(3)

    @pl.loop(0, 4)
    def _(i):
        m.QKV[row_tile(i), two : 3 * two] = m.ACC[row_tile(i), :].astype(BF16)

    qkv_far()
    grad_mid(0)
    finish_out(0)
    finish_out(1)
    out_second()
    for i in range(4):
        first_back(i)
        if i:
            ex_mid(3, i - 1)
    ex_mid(3, 3)
    out_third()
    qkv_near()
    out_fourth()
    grad_mid(2)
    grad_mid(3)
    finish_in(0)
    finish_in(1)

    for d in (1, 2, 3):
        tt = lax.rem(t + d, 4)
        push(m.VSUM, m.VR1.at[t], m.v1_s.at[d - 1], m.v1_r.at[t], mate(tt))
    m.OD[...] = grad_sum(1)
    keep_down = pltpu.make_async_copy(m.OD, m.gdn, m.loc.at[2])
    keep_down.start()
    m.FIU[...] = grad_sum(0).astype(BF16)
    give(0, lambda cc, pp: m.FIU.at[pl.ds(pl.multiple_of((cc * 2 + pp) * rw, rw), rw)], m.peu)
    rest = m.VSUM[...]
    for d in (1, 2, 3):
        tt = lax.rem(t + d, 4)
        arrived(m.VR1.at[tt], m.v1_r.at[tt])
        rest = rest + m.VR1[tt]
    row8 = lax.broadcasted_iota(jnp.int32, (8, width), 0)
    m.VMID[...] = jnp.where(row8 == 5, m.VSUM[...], rest)
    def vec_parts(yy, xx, qq):
        return [
            m.VMID.at[:, pl.ds(pl.multiple_of(at * 128, 128), 128)]
            for at in ((yy * 2 + xx) * 2 + c, at8(yy, xx, qq))
        ]

    for k, f in enumerate(flips):
        if k:
            spot = flipped(*f)
            for e, part in enumerate(vec_parts(*spot)):
                push(part, m.VR2.at[me, e], m.v2_s.at[k - 1, e], m.v2_r.at[me, e], peer(*spot))
    out_sum()
    keep_out = pltpu.make_async_copy(m.OO, m.go, m.loc.at[3])
    keep_out.start()
    for e in range(2):
        m.FIN[e] = grad_sum(2 + e).astype(BF16)
    give(1, lambda cc, pp: m.FIN.at[cc, pl.ds(pl.multiple_of(pp * rw, rw), rw)], m.peq)

    for e, part in enumerate(vec_parts(y, x, q)):
        final = part[...]
        for k, f in enumerate(flips):
            if k:
                at = at8(*flipped(*f))
                arrived(m.VR2.at[at, e], m.v2_r.at[at, e])
                final = final + m.VR2[at, e]
        m.gvec[e] = final

    for k, dst in enumerate((m.out, m.ig)):
        for cc in range(2):
            arrived(dst.at[pl.ds(cc * half, half)], m.ret_r.at[k, cc])
    give_end()
    keep_down.wait()
    keep_out.wait()
    for copy in sent:
        copy.wait_send()
    for e, i in ex_open:
        ex_close(e, i)
    far_close(1)
    far_close(3)
    for near, copy in homes:

        @pl.when(jnp.logical_not(near))
        def _():
            copy.wait_send()


def place_outputs(out_i, ig_i, peq, peu, go_i, gdn_i, out, ig, gq, gk, gv, go, gup, gdn, PQ, PU, GQ, GU, A, B, GO, GD, sem):
    pairs = ((peq, PQ), (peu, PU), (out_i, A), (ig_i, B), (go_i, GO), (gdn_i, GD))
    moves = [pltpu.make_async_copy(src, dst, sem.at[k]) for k, (src, dst) in enumerate(pairs)]
    for move in moves:
        move.start()
    results = ((A, out), (B, ig), (GO, go), (GD, gdn), (GQ.at[0], gq), (GQ.at[1], gk), (GQ.at[2], gv), (GU, gup))
    last = [pltpu.make_async_copy(src, dst, sem.at[6 + k]) for k, (src, dst) in enumerate(results)]
    hd = PQ.shape[2] // 6
    fw = PU.shape[2] // 8
    moves[0].wait()
    moves[1].wait()
    for tt in range(RANKS):
        for j in range(2):
            a = (j * RANKS + tt) * hd
            for n in range(3):
                GQ[n, :, a : a + hd] = PQ[tt, :, (n * 2 + j) * hd : (n * 2 + j + 1) * hd].astype(F32)
        for k in range(8):
            a = hidden_at(k, tt) * fw
            GU[:, a : a + fw] = PU[tt, :, k * fw : (k + 1) * fw].astype(F32)
    for k in range(4):
        last[4 + k].start()
    for k in range(4):
        moves[2 + k].wait()
        last[k].start()
    for move in last:
        move.wait()


def call_fused(inputs, positions, w_query, w_key, w_value, w_out, w_up, w_down, up_bias, down_bias,
               ln1_gain, ln1_bias, ln2_gain, ln2_bias, cotangent):
    rows, width = inputs.shape
    hid = w_up.shape[1] // RANKS
    rw, fw = w_query.shape[0], w_down.shape[0]
    shapes = scratch_of(rows, width, hid, rw, fw)
    blk = lax.axis_index("blk")
    small_in = [v.reshape(1, -1) for v in (down_bias, ln1_gain, ln1_bias, ln2_gain, ln2_bias, up_bias)]
    names = IN_NAMES + OUT_NAMES + tuple(shapes)
    any_, vm = pl.BlockSpec(memory_space=pl.ANY), pl.BlockSpec(memory_space=pltpu.VMEM)
    S = jax.ShapeDtypeStruct
    cols = 3 * 2 * (width // HEADS)
    tokens, wide = S((rows, width), BF16), S((rw, width), F32)
    moved = (S((RANKS, rw, cols), BF16), S((RANKS, rw, hid), BF16))
    out, ig, peq, peu, go, gdn, gvec = pl.pallas_call(
        functools.partial(fused, names),
        out_shape=(tokens, tokens) + moved + (wide, S(w_down.shape, F32), S((2, 8, 128), F32)),
        in_specs=[any_, any_, vm] + [any_] * 6 + [vm] * 6,
        out_specs=[any_] * 6 + [vm],
        scratch_shapes=list(shapes.values()),
        compiler_params=pltpu.CompilerParams(
            collective_id=0, has_side_effects=True, vmem_limit_bytes=VMEM_BYTES
        ),
        cost_estimate=pl.CostEstimate(flops=23 * 10**9, bytes_accessed=10**7, transcendentals=10**6),
    )(inputs, cotangent, positions.reshape(2, -1), w_query, w_key, w_value, w_out, w_up, w_down, *small_in)
    out, ig, gq, gk, gv, go, gup, gdn = pl.pallas_call(
        place_outputs,
        out_shape=(tokens, tokens, wide, wide, wide, wide, S(w_up.shape, F32), S(w_down.shape, F32)),
        in_specs=[any_] * 6,
        out_specs=[any_] * 8,
        scratch_shapes=[
            pltpu.VMEM(moved[0].shape, BF16),
            pltpu.VMEM(moved[1].shape, BF16),
            pltpu.VMEM((3, rw, width), F32),
            pltpu.VMEM(w_up.shape, F32),
            pltpu.VMEM((rows, width), BF16),
            pltpu.VMEM((rows, width), BF16),
            pltpu.VMEM((rw, width), F32),
            pltpu.VMEM(w_down.shape, F32),
            pltpu.SemaphoreType.DMA((14,)),
        ],
        compiler_params=pltpu.CompilerParams(vmem_limit_bytes=VMEM_BYTES),
    )(out, ig, peq, peu, go, gdn)
    small = lax.dynamic_slice(gvec[0], (0, blk * rw), (5, rw))
    gup_bias = gvec[1, 5]
    return (out, ig, gq, gk, gv, go, gup, gdn, gup_bias, small[0], small[1], small[2], small[3], small[4])


def layer_norm(values, gain, offset):
    centre = jnp.mean(values, axis=-1, keepdims=True)
    centred = values - centre
    variance = jnp.mean(centred * centred, axis=-1, keepdims=True)
    return centred * lax.rsqrt(variance + eps) * gain + offset


def smooth_gate(values):
    return jax.nn.gelu(values, approximate=True)


def keep_same(carry):
    return carry


def local(
    inputs,
    positions,
    w_query,
    w_key,
    w_value,
    w_out,
    w_up,
    w_down,
    up_bias,
    down_bias,
    ln1_gain,
    ln1_bias,
    ln2_gain,
    ln2_bias,
    cotangent,
):
    attn_full = (
        lax.all_gather(w_query, ("dp", "blk"), axis=0, tiled=True),
        lax.all_gather(w_key, ("dp", "blk"), axis=0, tiled=True),
        lax.all_gather(w_value, ("dp", "blk"), axis=0, tiled=True),
        lax.all_gather(w_out, ("dp", "blk"), axis=0, tiled=True),
        lax.all_gather(ln1_gain, ("dp", "blk"), axis=0, tiled=True),
        lax.all_gather(ln1_bias, ("dp", "blk"), axis=0, tiled=True),
    )
    ffn_full = (
        lax.all_gather(w_up, ("dp", "blk"), axis=0, tiled=True),
        lax.all_gather(w_down, ("dp", "blk"), axis=0, tiled=True),
        lax.all_gather(up_bias, ("dp", "blk"), axis=0, tiled=True),
        lax.all_gather(down_bias, ("dp", "blk"), axis=0, tiled=True),
        lax.all_gather(ln2_gain, ("dp", "blk"), axis=0, tiled=True),
        lax.all_gather(ln2_bias, ("dp", "blk"), axis=0, tiled=True),
    )
    token_rows = inputs.astype(jnp.float32)
    local_rows, model_width = token_rows.shape
    head_count = HEADS
    head_size = model_width // head_count
    score_scale = 1.0 / math.sqrt(head_size)
    normed_first, first_pull = jax.vjp(
        layer_norm, token_rows, attn_full[4].astype(jnp.float32), attn_full[5].astype(jnp.float32)
    )
    normed_low = normed_first.astype(jnp.bfloat16)
    query_low = jnp.dot(normed_low, attn_full[0], preferred_element_type=jnp.float32).astype(
        jnp.bfloat16
    )
    key_low = jnp.dot(normed_low, attn_full[1], preferred_element_type=jnp.float32).astype(
        jnp.bfloat16
    )
    value_low = jnp.dot(normed_low, attn_full[2], preferred_element_type=jnp.float32).astype(
        jnp.bfloat16
    )
    keys_all, values_all = (
        lax.all_gather(key_low, "blk", axis=0, tiled=True),
        lax.all_gather(value_low, "blk", axis=0, tiled=True),
    )
    group_rows = keys_all.shape[0]
    key_rows = max(min(512, group_rows), local_rows)
    block_count = group_rows // key_rows
    first_row = lax.axis_index("blk") * local_rows
    query_index = first_row + jnp.arange(local_rows, dtype=jnp.int32)
    seq_start = query_index - positions
    earliest = jnp.min(seq_start)
    query_heads = query_low.reshape(local_rows, head_count, head_size)
    key_parts = []
    for which in range(block_count):
        begin = which * key_rows
        key_part = keys_all[begin : begin + key_rows].reshape(key_rows, head_count, head_size)
        value_part = values_all[begin : begin + key_rows].reshape(key_rows, head_count, head_size)
        key_index = begin + jnp.arange(key_rows, dtype=jnp.int32)
        allowed = (key_index[None, :] <= query_index[:, None]) & (
            key_index[None, :] >= seq_start[:, None]
        )
        needed = (begin <= first_row + local_rows - 1) & (begin + key_rows - 1 >= earliest)
        key_parts.append((key_part, value_part, allowed, needed))

    def scores_of(key_part, allowed):
        scores = (
            jnp.einsum("qhd,khd->hqk", query_heads, key_part, preferred_element_type=jnp.float32)
            * score_scale
        )
        return jnp.where(allowed[None], scores, masked_value)

    running_max = jnp.full((head_count, local_rows), masked_value, jnp.float32)
    running_sum = jnp.zeros((head_count, local_rows), jnp.float32)
    for key_part, value_part, allowed, needed in key_parts:

        def extend(carry):
            old_max, old_sum = carry
            scores = scores_of(key_part, allowed)
            new_max = jnp.maximum(old_max, jnp.max(scores, axis=-1))
            terms = jnp.where(allowed[None], jnp.exp(scores - new_max[..., None]), 0.0)
            return (new_max, old_sum * jnp.exp(old_max - new_max) + jnp.sum(terms, axis=-1))

        running_max, running_sum = lax.cond(needed, extend, keep_same, (running_max, running_sum))
    log_total = running_max + jnp.log(running_sum)

    def probs_of(key_part, allowed):
        scores = scores_of(key_part, allowed)
        return jnp.where(allowed[None], jnp.exp(scores - log_total[..., None]), 0.0)

    attended = jnp.zeros((local_rows, head_count, head_size), jnp.float32)
    for key_part, value_part, allowed, needed in key_parts:

        def gather_values(total):
            weights_low = probs_of(key_part, allowed).astype(jnp.bfloat16)
            return total + jnp.einsum(
                "hqk,khd->qhd", weights_low, value_part, preferred_element_type=jnp.float32
            )

        attended = lax.cond(needed, gather_values, keep_same, attended)
    mixed_low = attended.reshape(local_rows, model_width).astype(jnp.bfloat16)
    residual = token_rows + jnp.dot(mixed_low, attn_full[3], preferred_element_type=jnp.float32)
    normed_second, second_pull = jax.vjp(
        layer_norm, residual, ffn_full[4].astype(jnp.float32), ffn_full[5].astype(jnp.float32)
    )
    normed_two = normed_second.astype(jnp.bfloat16)
    preact = jnp.dot(normed_two, ffn_full[0], preferred_element_type=jnp.float32) + ffn_full[
        2
    ].astype(jnp.float32)
    gated, gate_pull = jax.vjp(smooth_gate, preact)
    hidden = gated.astype(jnp.bfloat16)
    output = (
        residual
        + jnp.dot(hidden, ffn_full[1], preferred_element_type=jnp.float32)
        + ffn_full[3].astype(jnp.float32)
    ).astype(jnp.bfloat16)
    up_back, down_back = (ffn_full[0], ffn_full[1])
    grad_final = cotangent.astype(jnp.float32)
    grad_down_w = jnp.einsum("tf,td->fd", hidden, cotangent, preferred_element_type=jnp.float32)
    grad_down_shift = jnp.sum(grad_final, axis=0)
    grad_hidden = jnp.einsum("td,fd->tf", cotangent, down_back, preferred_element_type=jnp.float32)
    grad_preact = gate_pull(grad_hidden)[0].astype(jnp.bfloat16)
    grad_up_shift = jnp.sum(grad_preact.astype(jnp.float32), axis=0)
    grad_up_w = jnp.einsum("td,tf->df", normed_two, grad_preact, preferred_element_type=jnp.float32)
    grad_normed_two = jnp.einsum(
        "tf,df->td", grad_preact, up_back, preferred_element_type=jnp.float32
    )
    grad_resid_two, grad_gain_two, grad_shift_two = second_pull(grad_normed_two)
    grad_residual = grad_final + grad_resid_two
    query_back, key_back, value_back, out_back = (
        attn_full[0],
        attn_full[1],
        attn_full[2],
        attn_full[3],
    )
    grad_branch = grad_residual.astype(jnp.bfloat16)
    grad_out_w = jnp.einsum("te,td->ed", mixed_low, grad_branch, preferred_element_type=jnp.float32)
    grad_mixed = jnp.einsum(
        "td,ed->te", grad_branch, out_back, preferred_element_type=jnp.float32
    ).astype(jnp.bfloat16)
    grad_heads = grad_mixed.reshape(local_rows, head_count, head_size)
    delta = jnp.zeros((head_count, local_rows), jnp.float32)
    for key_part, value_part, allowed, needed in key_parts:

        def add_delta(total):
            probs = probs_of(key_part, allowed)
            grad_probs = jnp.einsum(
                "qhd,khd->hqk", grad_heads, value_part, preferred_element_type=jnp.float32
            )
            return total + jnp.sum(probs * grad_probs, axis=-1)

        delta = lax.cond(needed, add_delta, keep_same, delta)
    grad_query_sum = jnp.zeros((local_rows, head_count, head_size), jnp.float32)
    kv_terms = []
    for key_part, value_part, allowed, needed in key_parts:

        def backward_part(total):
            probs = probs_of(key_part, allowed)
            grad_probs = jnp.einsum(
                "qhd,khd->hqk", grad_heads, value_part, preferred_element_type=jnp.float32
            )
            grad_scores = (probs * (grad_probs - delta[..., None]) * score_scale).astype(
                jnp.bfloat16
            )
            new_total = total + jnp.einsum(
                "hqk,khd->qhd", grad_scores, key_part, preferred_element_type=jnp.float32
            )
            grad_keys = jnp.einsum(
                "hqk,qhd->khd", grad_scores, query_heads, preferred_element_type=jnp.float32
            ).reshape(key_rows, model_width)
            grad_values = jnp.einsum(
                "hqk,qhd->khd",
                probs.astype(jnp.bfloat16),
                grad_heads,
                preferred_element_type=jnp.float32,
            ).reshape(key_rows, model_width)
            return (new_total, jnp.concatenate([grad_keys, grad_values], axis=1))

        def skip_part(total):
            return (total, jnp.zeros((key_rows, 2 * model_width), jnp.float32))

        grad_query_sum, kv_term = lax.cond(needed, backward_part, skip_part, grad_query_sum)
        kv_terms.append(kv_term)
    kv_shares = lax.psum_scatter(
        jnp.concatenate(kv_terms, axis=0).astype(jnp.bfloat16),
        "blk",
        scatter_dimension=0,
        tiled=True,
    ).astype(jnp.float32)
    grad_key_low = kv_shares[:, :model_width].astype(jnp.bfloat16)
    grad_value_low = kv_shares[:, model_width:].astype(jnp.bfloat16)
    grad_query_low = grad_query_sum.reshape(local_rows, model_width).astype(jnp.bfloat16)
    grad_query_w = jnp.einsum(
        "td,te->de", normed_low, grad_query_low, preferred_element_type=jnp.float32
    )
    grad_key_w = jnp.einsum(
        "td,te->de", normed_low, grad_key_low, preferred_element_type=jnp.float32
    )
    grad_value_w = jnp.einsum(
        "td,te->de", normed_low, grad_value_low, preferred_element_type=jnp.float32
    )
    grad_normed = (
        jnp.einsum("te,de->td", grad_query_low, query_back, preferred_element_type=jnp.float32)
        + jnp.einsum("te,de->td", grad_key_low, key_back, preferred_element_type=jnp.float32)
        + jnp.einsum("te,de->td", grad_value_low, value_back, preferred_element_type=jnp.float32)
    )
    grad_rows_one, grad_gain_one, grad_shift_one = first_pull(grad_normed)
    input_grad = (grad_residual + grad_rows_one).astype(jnp.bfloat16)
    shares = (
        lax.psum_scatter(grad_query_w, ("dp", "blk"), scatter_dimension=0, tiled=True),
        lax.psum_scatter(grad_key_w, ("dp", "blk"), scatter_dimension=0, tiled=True),
        lax.psum_scatter(grad_value_w, ("dp", "blk"), scatter_dimension=0, tiled=True),
        lax.psum_scatter(grad_out_w, ("dp", "blk"), scatter_dimension=0, tiled=True),
        lax.psum_scatter(grad_up_w, ("dp", "blk"), scatter_dimension=0, tiled=True),
        lax.psum_scatter(grad_down_w, ("dp", "blk"), scatter_dimension=0, tiled=True),
        lax.psum_scatter(grad_up_shift, ("dp", "blk"), scatter_dimension=0, tiled=True),
        lax.psum_scatter(grad_down_shift, ("dp", "blk"), scatter_dimension=0, tiled=True),
        lax.psum_scatter(grad_gain_one, ("dp", "blk"), scatter_dimension=0, tiled=True),
        lax.psum_scatter(grad_shift_one, ("dp", "blk"), scatter_dimension=0, tiled=True),
        lax.psum_scatter(grad_gain_two, ("dp", "blk"), scatter_dimension=0, tiled=True),
        lax.psum_scatter(grad_shift_two, ("dp", "blk"), scatter_dimension=0, tiled=True),
    )
    return (
        output,
        input_grad,
        shares[0],
        shares[1],
        shares[2],
        shares[3],
        shares[4],
        shares[5],
        shares[6],
        shares[7],
        shares[8],
        shares[9],
        shares[10],
        shares[11],
    )


def solution(mesh):
    in_specs = (
        P(("dp", "blk"), None),
        P(("dp", "blk")),
        P(("dp", "blk"), None),
        P(("dp", "blk"), None),
        P(("dp", "blk"), None),
        P(("dp", "blk"), None),
        P(("dp", "blk"), None),
        P(("dp", "blk"), None),
        P(("dp", "blk")),
        P(("dp", "blk")),
        P(("dp", "blk")),
        P(("dp", "blk")),
        P(("dp", "blk")),
        P(("dp", "blk")),
        P(("dp", "blk"), None),
    )
    out_specs = (
        P(("dp", "blk"), None),
        P(("dp", "blk"), None),
        P(("dp", "blk"), None),
        P(("dp", "blk"), None),
        P(("dp", "blk"), None),
        P(("dp", "blk"), None),
        P(("dp", "blk"), None),
        P(("dp", "blk"), None),
        P(("dp", "blk")),
        P(("dp", "blk")),
        P(("dp", "blk")),
        P(("dp", "blk")),
        P(("dp", "blk")),
        P(("dp", "blk")),
    )
    n_dp, n_blk = mesh.shape["dp"], mesh.shape["blk"]

    def layer(*args):
        fits = n_blk == RANKS and n_dp == 2 * RANKS and args[2].shape[0] // (n_dp * n_blk) % 16 == 0
        call = jax.shard_map(
            call_fused if fits else local, mesh=mesh, in_specs=in_specs, out_specs=out_specs, check_vma=False
        )
        return call(*args)

    return layer
```

```python
import functools
import math
import types

import jax
import jax.numpy as jnp
from jax import lax
from jax.experimental import pallas as pl
from jax.experimental.pallas import tpu as pltpu
from jax.sharding import PartitionSpec as P

MESH = pl.DeviceIdType.MESH
F32 = jnp.float32
BF16 = jnp.bfloat16
HEADS = 8
VMEM_BYTES = 60 * 2**20
RANKS = 4
eps = 1e-05
masked_value = -1e30
GELU_K = math.sqrt(2.0 / math.pi)
GELU_C = 0.044715


def dot_nn(a, b):
    return lax.dot_general(a, b, (((1,), (0,)), ((), ())), preferred_element_type=F32)


def dot_nt(a, b):
    return lax.dot_general(a, b, (((1,), (1,)), ((), ())), preferred_element_type=F32)


def dot_tn(a, b):
    return lax.dot_general(a, b, (((0,), (0,)), ((), ())), preferred_element_type=F32)


def norm_parts(v):
    centre = jnp.mean(v, axis=-1, keepdims=True)
    centred = v - centre
    variance = jnp.mean(centred * centred, axis=-1, keepdims=True)
    rstd = lax.rsqrt(variance + eps)
    return centred * rstd, rstd


def norm_back(g, gain, xhat, rstd):
    e = g * gain
    return rstd * (
        e
        - jnp.mean(e, axis=-1, keepdims=True)
        - xhat * jnp.mean(e * xhat, axis=-1, keepdims=True)
    )


def hidden_at(k, tt):
    return ((k // 2) * 2 + tt % 2) * 4 + (k % 2) * 2 + tt // 2


IN_NAMES = ("x_in", "dz_in", "pos", "wq", "wk", "wv", "wo", "wup", "wdn", "db", "g1", "b1", "g2", "b2", "ub")
OUT_NAMES = ("out", "ig", "peq", "peu", "go", "gdn", "gvec")


def scratch_of(rows, width, hid, rw, fw):
    half = rows // 2
    hd = width // HEADS
    cols = 3 * 2 * hd
    dma = pltpu.SemaphoreType.DMA
    V = pltpu.VMEM
    names = dict(
        X=V((4, 2, half, width), BF16),
        DZ=V((4, 2, half, width), BF16),
        ST=V((4, 2, 16, 128), BF16),
        WA=V((4, 2, 2, 2 * rw, cols), BF16),
        WOP=V((8, rw, width), BF16),
        WO=V((2, 2, 2, rw, width), BF16),
        VEC=V((8, 16, width), BF16),
        WU=V((4, 2, 2, 2 * rw, hid), BF16),
        WD=V((8, fw, width), BF16),
        PV=V((4, 16, width), BF16),
        VF=V((8, width), F32),
        SV=V((8, rw), F32),
        VT=V((16, width), F32),
        vec=V((16, width), BF16),
        st_in=V((16, 128), BF16),
        TU=V((256, 4 * rows), BF16),
        N1=V((4 * rows, width), BF16),
        QKV=V((4 * rows, cols), BF16),
        P0=V((2, rows, rows), BF16),
        P1=V((2, rows, 2 * rows), BF16),
        P2=V((2, rows, 3 * rows), BF16),
        P3=V((2, rows, 4 * rows), BF16),
        MIX=V((4 * rows, 2 * hd), BF16),
        DMIX=V((rows, 2 * hd), BF16),
        PR0=V((4, 2, half, width), BF16),
        PR1=V((4, 2, half, width), BF16),
        RBa=V((4, half, width), BF16),
        RBb=V((4, half, width), BF16),
        RBc=V((4, half, width), BF16),
        RXa=V((4, half, width), BF16),
        RXb=V((2, half, width), BF16),
        RXc=V((4, half, width), BF16),
        RXd=V((2, half, width), BF16),
        RES=V((4, half, width), F32),
        KEEP=V((2, half, width), F32),
        N2=V((4, 2, half, width), BF16),
        HID=V((4 * rows, hid), BF16),
        DP=V((4 * rows, hid), BF16),
        DB=V((4, 2, half, width), BF16),
        ACC=V((4 * rows, 4 * hd), F32),
        TT=V((width // 2, 4 * rows), BF16),
        YSF=V((2, 4, fw, width), BF16),
        R1F=V((2, 4, fw, width), BF16),
        R2F=V((2, 2, fw, width), BF16),
        R3F=V((2, fw, width), BF16),
        YSQ=V((2, 4, 2 * rw, cols), BF16),
        R1Q=V((2, 4, 2 * rw, cols), BF16),
        R2Q=V((2, 2, 2 * rw, cols), BF16),
        R3Q=V((2, 2 * rw, cols), BF16),
        GOB=V((2, 2, 2, rw, width), BF16),
        GOR=V((2, 2, rw, width), BF16),
        GOS=V((8, rw, width), BF16),
        GOT=V((8, rw, width), BF16),
        OD=V((fw, width), F32),
        OO=V((rw, width), F32),
        OUTB=V((2, half, width), BF16),
        IGB=V((2, half, width), BF16),
        VSUM=V((8, width), F32),
        VMID=V((8, width), F32),
        VR1=V((4, 8, width), F32),
        VR2=V((8, 2, 8, 128), F32),
        sp_s=dma((3, 8)),
        sp_r=dma((3, 4, 2)),
        loc=dma((4,)),
        load=dma((7,)),
        pre_s=dma((3, 3)),
        pre_r=dma((3, 4)),
        ag_s=dma((6, 7)),
        ag_r=dma((6, 8)),
        sw_s=dma((4,)),
        sw_r=dma((4,)),
        sw_s2=dma((4,)),
        sw_r2=dma((4,)),
        FIN=V((2, 2 * rw, cols), BF16),
        FIU=V((fw, hid), BF16),
        sib_s=dma((4, 4)),
        sib_r=dma((4, 4)),
        xs=dma((4, 4)),
        xr=dma((4, 4)),
        n2_s=dma((4,)),
        n2_r=dma((4,)),
        db_s=dma((4,)),
        db_r=dma((4,)),
        r1_s=dma((4, 4)),
        r1_r=dma((4, 4)),
        up_s=dma((4, 4)),
        up_r=dma((4, 4)),
        r2_s=dma((4, 2)),
        r2_r=dma((4, 2)),
        r3_s=dma((4,)),
        r3_r=dma((4,)),
        go_s=dma((8,)),
        go_r=dma((8,)),
        pe_s=dma((2, 4)),
        pe_r=dma((2, 4)),
        v1_s=dma((3,)),
        v1_r=dma((4,)),
        v2_s=dma((7, 2)),
        v2_r=dma((8, 2)),
        ret_s=dma((2, 2)),
        ret_r=dma((2, 2)),
    )
    return names


def fused(names, *all_refs):
    m = types.SimpleNamespace(**dict(zip(names, all_refs)))
    half, width = m.X.shape[2:]
    rows = 2 * half
    hid = m.HID.shape[1]
    rw = m.WOP.shape[1]
    fw = m.WD.shape[1]
    hd = width // HEADS
    two = 2 * hd
    scale = 1.0 / math.sqrt(hd)

    dp = lax.axis_index("dp")
    z = lax.axis_index("blk")
    yx = lax.div(dp, 2)
    y, x, c = lax.div(dp, 4), lax.rem(yx, 2), lax.rem(dp, 2)
    q, p = lax.div(z, 2), lax.rem(z, 2)
    t = p * 2 + c
    me = yx * 2 + q

    def dev(yy, xx, cc, zz):
        return ((yy * 2 + xx) * 2 + cc, zz)

    def mate(tt):
        return dev(y, x, lax.rem(tt, 2), q * 2 + lax.div(tt, 2))

    def peer(yy, xx, qq):
        return dev(yy, xx, c, qq * 2 + p)

    def at8(yy, xx, qq):
        return yy * 4 + xx * 2 + qq

    sib = dev(y, x, 1 - c, z)
    nbr = dev(y, x, c, q * 2 + 1 - p)
    over = {"q": peer(y, x, 1 - q), "x": peer(y, 1 - x, q), "y": peer(1 - y, x, q)}

    mine = (p, p + 2)
    theirs = (1 - p, 3 - p)

    sent = []

    def remote(src, dst, ssem, rsem, device):
        return pltpu.make_async_remote_copy(
            src_ref=src,
            dst_ref=dst,
            send_sem=ssem,
            recv_sem=rsem,
            device_id=device,
            device_id_type=MESH,
        )

    def push(src, dst, ssem, rsem, device, keep=True):
        copy = remote(src, dst, ssem, rsem, device)
        copy.start()
        if keep:
            sent.append(copy)
        return copy

    homes = []

    def push_if(cond, src, dst, ssem, rsem, device):
        copy = remote(src, dst, ssem, rsem, device)

        @pl.when(cond)
        def _():
            copy.start()

        homes.append((jnp.logical_not(cond), copy))

    def arrived(dst, rsem):
        pltpu.make_async_copy(dst, dst, rsem).wait()

    loads = [pltpu.make_async_copy(ref, m.PR1.at[k, 0, pl.ds(0, rw)], m.load.at[k]) for k, ref in enumerate((m.wq, m.wk, m.wv))]
    loads += [
        pltpu.make_async_copy(m.wup.at[:, pl.ds(k * width, width)], m.PR1.at[k, 1, pl.ds(0, rw)], m.load.at[3 + k])
        for k in range(4)
    ]
    for copy in loads:
        copy.start()
    m.st_in[...] = jnp.broadcast_to((z * rows - m.pos[0:1, 0:1]).astype(F32), (16, 128)).astype(BF16)
    for k, ref in enumerate((m.db, m.g1, m.b1, m.g2, m.b2)):
        m.SV[k : k + 1] = ref[...].astype(F32)
    m.SV[5:8] = jnp.zeros((3, rw), F32)
    spot = lax.broadcasted_iota(jnp.int32, (rw, width), 1) - (dp * 4 + z) * rw
    hot = jnp.where(spot == lax.broadcasted_iota(jnp.int32, (rw, width), 0), 1.0, 0.0).astype(BF16)
    m.VT[0:8] = dot_nn(m.SV[...].astype(BF16), hot)
    m.VT[8:16] = jnp.zeros((8, width), F32)
    m.VT[5:6, pl.ds(pl.multiple_of(me * fw, 128), fw)] = m.ub[...].astype(F32)
    m.vec[...] = m.VT[...].astype(BF16)

    barrier = pltpu.get_barrier_semaphore()
    flips = [(a, b, d) for a in range(2) for b in range(2) for d in range(2)]

    def flipped(a, b, d):
        return ((1 - y if a else y), (1 - x if b else x), (1 - q if d else q))

    others = [dev(y, x, lax.rem(c + a, 2), lax.rem(z + b, 4)) for a in range(2) for b in range(4) if a or b] + [
        peer(*flipped(*f)) for f in flips if f[0] or f[1]
    ]
    for device in others:
        pl.semaphore_signal(barrier, inc=1, device_id=device, device_id_type=MESH)
    pl.semaphore_wait(barrier, len(others))

    def half_rows(ref):
        return lambda k: ref.at[pl.ds(k * half, half)]

    streams = (
        (half_rows(m.x_in), m.X),
        (lambda k: m.st_in, m.ST),
        (half_rows(m.dz_in), m.DZ),
    )
    to_z = 2 * c + p

    def spread_home(k, stays):
        src, buf = streams[k]
        for cc in range(2):
            dst = buf.at[z, cc]
            rsem = m.sp_r.at[k, z, cc]
            copy = remote(src(cc), dst, m.sp_s.at[k, cc], rsem, dev(y, x, cc, to_z))
            if stays:

                @pl.when((q == c) & (c == cc))
                def _():
                    pltpu.make_async_copy(src(cc), dst, rsem).start()

                @pl.when((q == c) & (c != cc))
                def _():
                    copy.start()

                homes.append(((q == c) & (c == cc), copy))
            else:

                @pl.when(q != c)
                def _():
                    copy.start()

    held = (z, lax.rem(z + 2, 4))
    beside = (2 * q + 1 - p, lax.rem(2 * q + 3 - p, 4))

    def spread_own(k, far):
        _, buf = streams[k]
        i = held[far]
        arrived(buf.at[i, c], m.sp_r.at[k, i, c])
        push(buf.at[i, c], buf.at[i, c], m.sp_s.at[k, 2 + 2 * far], m.sp_r.at[k, i, c], nbr)
        push(buf.at[i, c], buf.at[i, c], m.sp_s.at[k, 3 + 2 * far], m.sp_r.at[k, i, c], sib)

    def spread_nbr(k, far):
        _, buf = streams[k]
        j = beside[far]
        arrived(buf.at[j, c], m.sp_r.at[k, j, c])
        push(buf.at[j, c], buf.at[j, c], m.sp_s.at[k, 6 + far], m.sp_r.at[k, j, c], sib)

    def spread_end(k):
        _, buf = streams[k]
        for i in held + beside:
            arrived(buf.at[i, 1 - c], m.sp_r.at[k, i, 1 - c])

    for k in range(2):
        spread_home(k, False)
        spread_home(k, True)
    spread_home(2, True)

    for copy in loads:
        copy.wait()
    for tt in range(4):
        at = 0
        for k in range(3):
            for j in range(2):
                m.PR0[tt, 1, 0:rw, at : at + hd] = m.PR1[k, 0, 0:rw, (j * 4 + tt) * hd : (j * 4 + tt + 1) * hd]
                at += hd
        for k in range(8):
            row, at = divmod(hidden_at(k, tt) * fw, width)
            m.PR0[tt, 0, 0:rw, k * fw : (k + 1) * fw] = m.PR1[row, 1, 0:rw, at : at + fw]
    cols = 3 * two

    def pre_src(n, tt):
        if n == 0:
            return m.PR0.at[tt, 1, pl.ds(0, rw), pl.ds(0, cols)]
        if n == 1:
            return m.vec
        return m.PR0.at[tt, 0, pl.ds(0, rw), pl.ds(0, hid)]

    def rank_rows(cc, pp):
        return (yx, cc, q, pl.ds(pl.multiple_of(pp * rw, rw), rw))

    def pre_dst(n, tt):
        if n == 1:
            return m.PV.at[tt]
        return (m.WA if n == 0 else m.WU).at[rank_rows(lax.rem(tt, 2), lax.div(tt, 2))]

    pre_sent = []

    def pre_send(n):
        for d in (1, 2, 3):
            tt = lax.rem(t + d, 4)
            pre_sent.append(
                push(pre_src(n, tt), pre_dst(n, t), m.pre_s.at[n, d - 1], m.pre_r.at[n, t], mate(tt), keep=False)
            )

    pre_send(1)
    pre_send(0)
    local_o = pltpu.make_async_copy(m.wo, m.WOP.at[me], m.loc.at[0])
    local_o.start()
    local_d = pltpu.make_async_copy(m.wdn, m.WD.at[me], m.loc.at[1])
    local_d.start()
    m.WA[rank_rows(c, p)] = m.PR0[t, 1, 0:rw, 0:cols]
    m.WU[rank_rows(c, p)] = m.PR0[t, 0, 0:rw, 0:hid]
    m.PV[t] = m.vec[...]

    def pre_wait(n):
        for d in (1, 2, 3):
            tt = lax.rem(t + d, 4)
            arrived(pre_dst(n, tt), m.pre_r.at[n, tt])

    def piece(n, yy, xx, qq):
        if n < 2:
            return m.WA.at[yy * 2 + xx, n, qq]
        if n == 4:
            return m.WU.at[yy * 2 + xx, :, qq]
        return {2: m.VEC, 3: m.WOP, 5: m.WD}[n].at[at8(yy, xx, qq)]

    def order(n):
        return "xy" if n in (0, 2, 4) else "yx"

    def beyond(first, qq):
        return (y, 1 - x, qq) if first == "x" else (1 - y, x, qq)

    def gather_send(n, spot, k, to):
        ref = piece(n, *spot)
        push(ref, ref, m.ag_s.at[n, k], m.ag_r.at[n, at8(*spot)], over[to])

    def gather_own(group, steps=(0, 1, 2)):
        for k in steps:
            for n in group:
                gather_send(n, (y, x, q), k, ("q" + order(n))[k])

    def gather_pass(group, k):
        for n in group:
            first, second = order(n)
            spot = (y, x, 1 - q) if k == 0 else beyond(first, q if k == 1 else 1 - q)
            arrived(piece(n, *spot), m.ag_r.at[n, at8(*spot)])
            if k == 0:
                gather_send(n, spot, 3, first)
                gather_send(n, spot, 4, second)
            else:
                gather_send(n, spot, 4 + k, second)

    def gather_end(group):
        for n in group:
            second = order(n)[1]
            for a in range(2):
                for qq in range(2):
                    spot = (1 - y, a, qq) if second == "y" else (a, 1 - x, qq)
                    arrived(piece(n, *spot), m.ag_r.at[n, at8(*spot)])

    VECS, ATT, WOUT, FFN = (2,), (0, 1), (3,), (4, 5)

    def norm_one(i, h):
        xhat, _ = norm_parts(m.X[i, h].astype(F32))
        at = pl.ds(pl.multiple_of(i * rows + h * half, half), half)
        m.N1[at, :] = (xhat * m.VF[1:2] + m.VF[2:3]).astype(BF16)

    def vec_own():
        pre_wait(1)
        total = sum((m.PV[a].astype(F32) for a in range(1, 4)), m.PV[0].astype(F32))
        line = lax.broadcasted_iota(jnp.int32, (16, width), 0)
        own_vec = jnp.where(line == 5, m.vec[...].astype(F32), total)
        m.VEC[me] = own_vec.astype(BF16)
        gather_own(VECS)

    def vec_end():
        gather_end(VECS)
        every = m.VEC[0].astype(F32)
        for a in range(1, 8):
            every = every + m.VEC[a].astype(F32)
        m.VF[...] = every[0:8]

    def swap_out():
        gather_end(WOUT)
        for yy in range(2):
            for qq in range(2):
                k = yy * 2 + qq
                push(
                    m.WOP.at[at8(yy, 1 - p, qq)], m.WO.at[yy, qq, p], m.sw_s.at[k], m.sw_r.at[k], nbr
                )
                m.WO[yy, qq, p] = m.WOP[at8(yy, p, qq)]

    def swap_end():
        for yy in range(2):
            for qq in range(2):
                arrived(m.WO.at[yy, qq, 1 - p], m.sw_r.at[yy * 2 + qq])

    spread_own(0, 0)
    spread_own(1, 0)
    vec_own()
    pre_wait(0)
    gather_own(ATT)
    pre_send(2)
    local_o.wait()
    local_d.wait()
    gather_pass(VECS, 0)
    gather_own(WOUT)
    gather_pass(VECS, 1)
    spread_nbr(0, 0)
    spread_nbr(1, 0)
    gather_pass(VECS, 2)
    pre_wait(2)
    for copy in pre_sent:
        copy.wait_send()
    vec_end()
    norm_one(held[0], c)
    norm_one(beside[0], c)
    gather_pass(ATT, 0)
    spread_own(0, 1)
    spread_own(1, 1)
    gather_own(FFN, (1, 2))
    gather_own(FFN, (0,))
    norm_one(held[1], c)
    gather_pass(ATT, 1)
    gather_pass(WOUT, 0)
    spread_own(2, 0)
    gather_pass(ATT, 2)
    spread_home(2, False)
    gather_pass(WOUT, 1)
    gather_pass(WOUT, 2)
    spread_nbr(0, 1)
    spread_nbr(1, 1)
    norm_one(beside[1], c)
    swap_out()
    spread_end(0)
    spread_end(1)
    for i in held + beside:
        norm_one(i, 1 - c)
    gather_end(ATT)

    def row_tile(i):
        return pl.ds(pl.multiple_of(i * rows, rows), rows)

    def col_tile(n, size=256):
        return pl.ds(pl.multiple_of(n * size, size), size)

    @pl.loop(0, 3)
    def _(n):
        w = m.WA[:, :, :, :, col_tile(n)].reshape(width, 256)

        for i in range(2):
            at = slice(2 * i * rows, (2 * i + 2) * rows)
            m.QKV[at, col_tile(n)] = dot_nn(m.N1[at, :], w).astype(BF16)

    EX = (
        (m.PR0, m.RBa, m.RXa),
        (m.PR1, m.RBb, m.RXb),
        (m.PR0, m.RBa, m.RXc),
        (m.PR0, m.RBc, m.RXd),
    )
    ex_open = {}
    ex_far = {1: [], 3: []}

    def ex_put(e, i, cols_at, value):
        pair = EX[e][0]
        low = value.astype(BF16)
        pair[i, 0, :, cols_at] = low[0:half]
        pair[i, 1, :, cols_at] = low[half:rows]

    def ex_send(e, i):
        pair, rb, _ = EX[e]
        ex_open[e, i] = [push(pair.at[i, 1 - c], rb.at[i], m.sib_s.at[e, i], m.sib_r.at[e, i], sib, keep=False)]

    def ex_mid(e, i):
        pair, rb, rx = EX[e]
        arrived(rb.at[i], m.sib_r.at[e, i])
        pair[i, c] = (pair[i, c].astype(F32) + rb[i].astype(F32)).astype(BF16)
        if e in (0, 2):
            ex_open[e, i].append(push(pair.at[i, c], rx.at[i], m.xs.at[e, i], m.xr.at[e, i], nbr, keep=False))
        else:
            copy = remote(pair.at[i, c], rx.at[i // 2], m.xs.at[e, i], m.xr.at[e, i // 2], nbr)
            far = p != i % 2

            @pl.when(far)
            def _():
                copy.start()

            ex_far[e].append((jnp.logical_not(far), copy))

    def ex_close(e, i):
        for copy in ex_open[e, i]:
            copy.wait_send()
        ex_open[e, i] = []

    def ex_total(e, i):
        pair, _, rx = EX[e]
        arrived(rx.at[i], m.xr.at[e, i])
        return pair[i, c].astype(F32) + rx[i].astype(F32)

    PS = (m.P0, m.P1, m.P2, m.P3)

    def attend(i):
        span = (i + 1) * rows
        r0 = i * rows
        start = m.ST[i, 0][0:1, 0:1].astype(F32)
        for j in range(2):
            q = m.QKV[r0 : r0 + rows, j * hd : (j + 1) * hd]
            k = m.QKV[0:span, two + j * hd : two + (j + 1) * hd]
            s = dot_nt(q, k) * scale
            row = lax.broadcasted_iota(jnp.int32, (rows, span), 0) + r0
            col = lax.broadcasted_iota(jnp.int32, (rows, span), 1)
            s = jnp.where((col <= row) & (col.astype(F32) >= start), s, masked_value)
            e = jnp.exp(s - jnp.max(s, axis=-1, keepdims=True))
            p = (e * (1.0 / jnp.sum(e, axis=-1, keepdims=True))).astype(BF16)
            PS[i][j] = p
            v = m.QKV[0:span, 2 * two + j * hd : 2 * two + (j + 1) * hd]
            m.MIX[r0 : r0 + rows, j * hd : (j + 1) * hd] = dot_nn(p, v).astype(BF16)

    def attend_out(i):
        r0 = i * rows

        @pl.loop(0, 4)
        def _(n):
            w = m.WO[:, :, :, :, col_tile(n)].reshape(two, 256)
            ex_put(0, i, col_tile(n), dot_nn(m.MIX[r0 : r0 + rows, :], w))

        ex_send(0, i)

    def second_norm(i):
        res = m.X[i, c].astype(F32) + ex_total(0, i)
        m.RES[i] = res
        xhat, _ = norm_parts(res)
        m.N2[i, c] = (xhat * m.VF[3:4] + m.VF[4:5]).astype(BF16)
        push(m.N2.at[i, c], m.N2.at[i, c], m.n2_s.at[i], m.n2_r.at[i], sib)

    m.VSUM[...] = jnp.zeros((8, width), F32)

    def feed(n):
        tile = col_tile(n)
        w_in = m.WU[:, :, :, :, tile].reshape(width, 256)
        w_back = m.WD[pl.ds(n * (256 // fw), 256 // fw)].reshape(256, width)

        @pl.loop(0, 4)
        def _(i):
            pre = dot_nn(m.N2[i].reshape(rows, width), w_in) + m.VF[5:6, tile]
            back = dot_nt(m.DZ[i].reshape(rows, width), w_back)
            sq = pre * pre
            th = jnp.tanh(GELU_K * pre * (1.0 + GELU_C * sq))
            m.HID[row_tile(i), tile] = (0.5 * pre * (1.0 + th)).astype(BF16)
            slope = 0.5 * (1.0 + th) + 0.5 * pre * (1.0 - th * th) * (GELU_K * (1.0 + 3.0 * GELU_C * sq))
            dpre = back * slope
            m.VSUM[5:6, tile] += jnp.sum(dpre, axis=0, keepdims=True)
            m.DP[row_tile(i), tile] = dpre.astype(BF16)

    def feed_two(i):
        r0 = i * rows
        ex_close(0, i)

        @pl.loop(0, width // 256)
        def _(n):
            w = m.WU[n].reshape(256, hid)
            ex_put(2, i, col_tile(n), dot_nt(m.DP[r0 : r0 + rows, :], w))

        ex_send(2, i)

    def feed_out(i):
        r0 = i * rows

        @pl.loop(0, width // 256)
        def _(n):
            w = m.WD[:, :, col_tile(n)].reshape(hid, 256)
            low = dot_nn(m.HID[r0 : r0 + 2 * rows, :], w).astype(BF16)
            for b in range(2):
                ex_put(1, i + b, col_tile(n), low[b * rows : (b + 1) * rows])

        ex_send(1, i)
        ex_send(1, i + 1)

    def feed_back(i):
        xhat, rstd = norm_parts(m.RES[i])
        g = ex_total(2, i)
        a = 0.5 * jnp.sum(g * xhat, axis=0, keepdims=True)
        b = 0.5 * jnp.sum(g, axis=0, keepdims=True)
        m.VSUM[3:4] += a
        m.VSUM[4:5] += b

        @pl.when(p == i % 2)
        def _():
            m.KEEP[i // 2] = m.RES[i]

        dres = m.DZ[i, c].astype(F32) + norm_back(g, m.VF[3:4], xhat, rstd)
        m.RES[i] = dres
        m.DB[i, c] = dres.astype(BF16)
        push(m.DB.at[i, c], m.DB.at[i, c], m.db_s.at[i], m.db_r.at[i], sib)

    def lane(ref, at):
        return ref[:, pl.ds(pl.multiple_of(at * 128, 128), 128)]

    def lane_n2(at):
        return m.N2[:, :, :, pl.ds(pl.multiple_of(at * 128, 128), 128)].reshape(4 * rows, 128)

    def flip(parts):
        for a, part in enumerate(parts):
            m.TT[a * 128 : (a + 1) * 128, :] = part.T

    SEND = (m.YSF.at[0], m.YSF.at[1], m.YSQ.at[0], m.YSQ.at[1])
    GOT1 = (m.R1F.at[0], m.R1F.at[1], m.R1Q.at[0], m.R1Q.at[1])
    GOT2 = (m.R2F.at[0], m.R2F.at[1], m.R2Q.at[0], m.R2Q.at[1])
    GOT3 = (m.R3F.at[0], m.R3F.at[1], m.R3Q.at[0], m.R3Q.at[1])
    AXES = ("yx", "xy", "yx", "xy")
    open1 = {0: [], 1: [], 2: [], 3: []}
    fh = fw // 2

    def step1(w, slots):
        for k in slots:
            open1[w].append(
                push(SEND[w].at[k], GOT1[w].at[k], m.r1_s.at[w, k], m.r1_r.at[w, k], over[AXES[w][0]], keep=False)
            )

    def up_lhs(yy):
        flip([lane_n2((yy * 2 + a // 2) * 2 + a % 2) for a in range(4)])

    def up_parts(res):
        return [
            ((a // 2) * 2 + b, (a % 2) * fh, res[a * 128 + b * fh : a * 128 + (b + 1) * fh])
            for a in range(4)
            for b in range(2)
        ]

    def far_tile(k):
        return 2 * k + 1 - x if k < 2 else 2 * (k - 2) + x

    def up_far(k):
        s = col_tile(far_tile(k))
        for slot, at, part in up_parts(dot_nn(m.TT[...], m.DP[:, s])):
            m.YSF[0, slot, at : at + fh, s] = part.astype(BF16)
        for slot in range(4):
            src, dst = m.YSF.at[0, slot, :, s], m.R1F.at[0, slot, :, s]
            open1[0].append(push(src, dst, m.up_s.at[k, slot], m.up_r.at[k, slot], over["y"], keep=False))

    def down_far(k):
        for a in range(2):
            m.TU[a * 128 : (a + 1) * 128, :] = lane(m.HID, far_tile(k) * 2 + a).T

        @pl.loop(0, width // 256)
        def _(n):
            s = col_tile(n)
            res = dot_nn(m.TU[...], m.DZ[:, :, :, s].reshape(4 * rows, 256)).astype(BF16)
            m.YSF[1, 2 * k, :, s] = res[0:fw]
            m.YSF[1, 2 * k + 1, :, s] = res[fw : 2 * fw]

        step1(1, (2 * k, 2 * k + 1))

    def qkv_lhs(yy, xx):
        flip([lane(m.N1, (yy * 2 + a) * 2) for a in range(2)] + [lane(m.N1, (a * 2 + xx) * 2 + 1) for a in range(2)])

    def qkv_parts(res):
        return [
            (a // 2, (a % 2) * 2 + b, res[a * 128 + b * fh : a * 128 + (b + 1) * fh]) for a in range(4) for b in range(2)
        ]

    def qkv_far():
        qkv_lhs(1 - y, 1 - x)

        @pl.loop(0, 3)
        def _(n):
            s = col_tile(n)
            for e, slot, part in qkv_parts(dot_nn(m.TT[...], m.QKV[:, s])):
                m.YSQ[e, slot, :, s] = part.astype(BF16)

        step1(2, range(4))
        step1(3, range(4))

    def near_wait(w):
        for copy in open1[w]:
            copy.wait_send()
        for slot in range(4):
            if w:
                arrived(GOT1[w].at[slot], m.r1_r.at[w, slot])
            else:
                for k in range(4):
                    arrived(m.R1F.at[0, slot, :, col_tile(far_tile(k))], m.up_r.at[k, slot])

    def step2(w):
        first, second = AXES[w]
        there = 1 - (x if second == "x" else y)
        for qq in range(2):
            push(
                SEND[w].at[there * 2 + qq], GOT2[w].at[qq], m.r2_s.at[w, qq], m.r2_r.at[w, qq], over[second]
            )

    def up_near():
        up_lhs(y)
        near_wait(0)

        @pl.loop(0, hid // 256)
        def _(n):
            s = col_tile(n)
            for slot, at, part in up_parts(dot_nn(m.TT[...], m.DP[:, s])):
                to = slice(at, at + fh)
                m.YSF[0, slot, to, s] = (part + m.R1F[0, slot, to, s].astype(F32)).astype(BF16)

        step2(0)

    def down_near():
        near_wait(1)
        for k in range(2):
            for a in range(2):
                m.TU[a * 128 : (a + 1) * 128, :] = lane(m.HID, far_tile(k + 2) * 2 + a).T

            @pl.loop(0, width // 256)
            def _(n):
                s = col_tile(n)
                res = dot_nn(m.TU[...], m.DZ[:, :, :, s].reshape(4 * rows, 256))
                for b in range(2):
                    got = m.R1F[1, 2 * k + b, :, s].astype(F32)
                    m.YSF[1, 2 * k + b, :, s] = (res[b * fw : (b + 1) * fw] + got).astype(BF16)

        step2(1)

    def qkv_near():
        qkv_lhs(y, x)
        near_wait(2)
        near_wait(3)

        @pl.loop(0, 3)
        def _(n):
            s = col_tile(n)
            for e, slot, part in qkv_parts(dot_nn(m.TT[...], m.QKV[:, s])):
                m.YSQ[e, slot, :, s] = (part + m.R1Q[e, slot, :, s].astype(F32)).astype(BF16)

        step2(2)
        step2(3)

    def here(w):
        return x if AXES[w][1] == "x" else y

    def grad_mid(w):
        for qq in range(2):
            arrived(GOT2[w].at[qq], m.r2_r.at[w, qq])
            slot = here(w) * 2 + qq
            SEND[w][slot] = (SEND[w][slot].astype(F32) + GOT2[w][qq].astype(F32)).astype(BF16)
        push(SEND[w].at[here(w) * 2 + 1 - q], GOT3[w], m.r3_s.at[w], m.r3_r.at[w], over["q"])

    def grad_sum(w):
        arrived(GOT3[w], m.r3_r.at[w])
        return SEND[w][here(w) * 2 + q].astype(F32) + GOT3[w][...].astype(F32)

    def out_first():
        flip([lane(m.MIX, a) for a in range(2)])

        @pl.loop(0, width // 256)
        def _(n):
            s = col_tile(n)
            res = dot_nn(m.TT[0:two, :], m.DB[:, :, :, s].reshape(4 * rows, 256)).astype(BF16)
            m.GOB[:, :, :, :, s] = res.reshape(2, 2, 2, rw, 256)

        for yy in range(2):
            for qq in range(2):
                k = yy * 2 + qq
                push(m.GOB.at[yy, qq, 1 - p], m.GOR.at[yy, qq], m.sw_s2.at[k], m.sw_r2.at[k], nbr)

    def out_second():
        for yy in range(2):
            for qq in range(2):
                k = yy * 2 + qq
                arrived(m.GOR.at[yy, qq], m.sw_r2.at[k])
                m.GOS[at8(yy, p, qq)] = m.GOB[yy, qq, p]
                m.GOS[at8(yy, 1 - p, qq)] = m.GOR[yy, qq]
        for yy in range(2):
            for qq in range(2):
                k = yy * 2 + qq
                push(m.GOS.at[at8(yy, 1 - x, qq)], m.GOT.at[k], m.go_s.at[k], m.go_r.at[k], over["x"])

    def out_add(at, k):
        arrived(m.GOT.at[k], m.go_r.at[k])
        m.GOS[at] = (m.GOS[at].astype(F32) + m.GOT[k].astype(F32)).astype(BF16)

    def out_third():
        for yy in range(2):
            for qq in range(2):
                out_add(at8(yy, x, qq), yy * 2 + qq)
        for qq in range(2):
            push(m.GOS.at[at8(1 - y, x, qq)], m.GOT.at[4 + qq], m.go_s.at[4 + qq], m.go_r.at[4 + qq], over["y"])

    def out_fourth():
        for qq in range(2):
            out_add(at8(y, x, qq), 4 + qq)
        push(m.GOS.at[at8(y, x, 1 - q)], m.GOT.at[6], m.go_s.at[6], m.go_r.at[6], over["q"])

    def out_sum():
        arrived(m.GOT.at[6], m.go_r.at[6])
        m.OO[...] = m.GOS[me].astype(F32) + m.GOT[6].astype(F32)

    def give(e, src_of, dst):
        pltpu.make_async_copy(src_of(c, p), dst.at[t], m.pe_r.at[e, t]).start()
        for d in (1, 2, 3):
            tt = lax.rem(t + d, 4)
            push(src_of(lax.rem(tt, 2), lax.div(tt, 2)), dst.at[t], m.pe_s.at[e, d - 1], m.pe_r.at[e, t], mate(tt))

    def give_end():
        for e, dst in ((0, m.peu), (1, m.peq)):
            for tt in range(4):
                arrived(dst.at[tt], m.pe_r.at[e, tt])

    attend(0)
    swap_end()
    attend_out(0)
    gather_pass(FFN, 0)
    attend(1)
    attend_out(1)
    ex_mid(0, 0)
    attend(2)
    attend_out(2)
    gather_pass(FFN, 1)
    ex_mid(0, 1)
    second_norm(0)
    attend(3)
    attend_out(3)
    ex_mid(0, 2)
    gather_pass(FFN, 2)
    second_norm(1)
    ex_mid(0, 3)
    spread_nbr(2, 0)
    spread_own(2, 1)
    second_norm(2)
    second_norm(3)
    spread_nbr(2, 1)
    for i in range(4):
        arrived(m.N2.at[i, 1 - c], m.n2_r.at[i])
    up_lhs(1 - y)
    spread_end(2)
    gather_end(FFN)
    for k in range(4):
        feed(far_tile(k))
        if k < 2:
            down_far(k)
            up_far(k)
    feed_two(0)
    up_far(2)
    feed_two(1)
    ex_mid(2, 0)
    up_far(3)
    feed_two(2)
    ex_mid(2, 1)
    feed_two(3)
    ex_mid(2, 2)
    ex_mid(2, 3)
    feed_out(0)
    feed_out(2)
    feed_back(0)
    feed_back(1)
    down_near()
    up_near()

    def db_end(i):
        arrived(m.DB.at[i, 1 - c], m.db_r.at[i])

    def attend_back(i):
        span = (i + 1) * rows
        r0 = i * rows
        m.DMIX[...] = dot_nt(m.DB[i].reshape(rows, width), m.WO[...].reshape(two, width)).astype(BF16)
        for j in range(2):
            k0, v0 = two + j * hd, 2 * two + j * hd
            do = m.DMIX[:, j * hd : (j + 1) * hd]
            p = PS[i][j]
            pf = p.astype(F32)
            g = dot_nt(do, m.QKV[0:span, v0 : v0 + hd])
            delta = jnp.sum(pf * g, axis=-1, keepdims=True)
            ds = (pf * (g - delta) * scale).astype(BF16)
            q = m.QKV[r0 : r0 + rows, j * hd : (j + 1) * hd]
            dk = dot_tn(ds, q)
            dv = dot_tn(p, do)
            dq = dot_nn(ds, m.QKV[0:span, k0 : k0 + hd])
            ka, va = slice(j * hd, (j + 1) * hd), slice(two + j * hd, two + (j + 1) * hd)
            if i:
                m.ACC[0:r0, ka] += dk[0:r0]
                m.ACC[0:r0, va] += dv[0:r0]
            m.ACC[r0:span, ka] = dk[r0:span]
            m.ACC[r0:span, va] = dv[r0:span]
            m.QKV[r0 : r0 + rows, j * hd : (j + 1) * hd] = dq.astype(BF16)

    def give_back(k, kk, buf, dst):
        i = mine[kk]
        near = (q == c) & (i == z)
        to = dst.at[pl.ds(pl.multiple_of(c * half, half), half)]
        rsem = m.ret_r.at[k, c]

        @pl.when(near)
        def _():
            pltpu.make_async_copy(buf.at[kk], to, rsem).start()

        copy = remote(buf.at[kk], to, m.ret_s.at[k, kk], rsem, dev(y, x, q, i))

        @pl.when(jnp.logical_not(near))
        def _():
            copy.start()

        homes.append((near, copy))

    def far_close(e):
        for near, copy in ex_far.pop(e):

            @pl.when(jnp.logical_not(near))
            def _():
                copy.wait_send()

    def finish_out(kk):
        i = mine[kk]
        arrived(m.RXb.at[kk], m.xr.at[1, kk])
        value = m.KEEP[kk] + m.PR1[i, c].astype(F32) + m.RXb[kk].astype(F32) + m.VF[0:1]
        m.OUTB[kk] = value.astype(BF16)
        give_back(0, kk, m.OUTB, m.out)

    def first_back(i):
        r0 = i * rows
        ex_close(2, i)
        ex_close(2, i + 1)

        @pl.loop(0, width // 256)
        def _(n):
            low = dot_nt(m.QKV[r0 : r0 + 2 * rows, :], m.WA[n].reshape(256, cols)).astype(BF16)
            for b in range(2):
                ex_put(3, i + b, col_tile(n), low[b * rows : (b + 1) * rows])

        ex_send(3, i)
        ex_send(3, i + 1)

    def finish_in(kk):
        i = mine[kk]
        arrived(m.RXd.at[kk], m.xr.at[3, kk])
        g = m.PR0[i, c].astype(F32) + m.RXd[kk].astype(F32)
        xhat, rstd = norm_parts(m.X[i, c].astype(F32))
        parts = (
            jnp.sum(m.DZ[i, c].astype(F32), axis=0, keepdims=True),
            jnp.sum(g * xhat, axis=0, keepdims=True),
            jnp.sum(g, axis=0, keepdims=True),
        )
        for k, part in enumerate(parts):
            m.VSUM[k : k + 1] += part
        m.IGB[kk] = (m.RES[i] + norm_back(g, m.VF[1:2], xhat, rstd)).astype(BF16)
        give_back(1, kk, m.IGB, m.ig)

    db_end(0)
    attend_back(0)
    feed_back(2)
    db_end(1)
    attend_back(1)
    feed_back(3)
    for i in range(4):
        ex_mid(1, i)
    db_end(2)
    attend_back(2)
    db_end(3)
    out_first()
    grad_mid(1)
    attend_back(3)

    @pl.loop(0, 4)
    def _(i):
        m.QKV[row_tile(i), two : 3 * two] = m.ACC[row_tile(i), :].astype(BF16)

    qkv_far()
    grad_mid(0)
    finish_out(0)
    finish_out(1)
    out_second()
    first_back(0)
    first_back(2)
    for i in range(4):
        ex_mid(3, i)
    out_third()
    qkv_near()
    out_fourth()
    grad_mid(2)
    grad_mid(3)
    finish_in(0)
    finish_in(1)

    for d in (1, 2, 3):
        tt = lax.rem(t + d, 4)
        push(m.VSUM, m.VR1.at[t], m.v1_s.at[d - 1], m.v1_r.at[t], mate(tt))
    m.FIU[...] = grad_sum(0).astype(BF16)
    give(0, lambda cc, pp: m.FIU.at[pl.ds(pl.multiple_of((cc * 2 + pp) * rw, rw), rw)], m.peu)
    m.OD[...] = grad_sum(1)
    keep_down = pltpu.make_async_copy(m.OD, m.gdn, m.loc.at[2])
    keep_down.start()
    rest = m.VSUM[...]
    for d in (1, 2, 3):
        tt = lax.rem(t + d, 4)
        arrived(m.VR1.at[tt], m.v1_r.at[tt])
        rest = rest + m.VR1[tt]
    row8 = lax.broadcasted_iota(jnp.int32, (8, width), 0)
    m.VMID[...] = jnp.where(row8 == 5, m.VSUM[...], rest)
    def vec_parts(yy, xx, qq):
        return [
            m.VMID.at[:, pl.ds(pl.multiple_of(at * 128, 128), 128)]
            for at in ((yy * 2 + xx) * 2 + c, at8(yy, xx, qq))
        ]

    for k, f in enumerate(flips):
        if k:
            spot = flipped(*f)
            for e, part in enumerate(vec_parts(*spot)):
                push(part, m.VR2.at[me, e], m.v2_s.at[k - 1, e], m.v2_r.at[me, e], peer(*spot))
    out_sum()
    keep_out = pltpu.make_async_copy(m.OO, m.go, m.loc.at[3])
    keep_out.start()
    for e in range(2):
        m.FIN[e] = grad_sum(2 + e).astype(BF16)
    give(1, lambda cc, pp: m.FIN.at[cc, pl.ds(pl.multiple_of(pp * rw, rw), rw)], m.peq)

    for e, part in enumerate(vec_parts(y, x, q)):
        final = part[...]
        for k, f in enumerate(flips):
            if k:
                at = at8(*flipped(*f))
                arrived(m.VR2.at[at, e], m.v2_r.at[at, e])
                final = final + m.VR2[at, e]
        m.gvec[e] = final

    for k, dst in enumerate((m.out, m.ig)):
        for cc in range(2):
            arrived(dst.at[pl.ds(cc * half, half)], m.ret_r.at[k, cc])
    give_end()
    keep_down.wait()
    keep_out.wait()
    for copy in sent:
        copy.wait_send()
    for e, i in ex_open:
        ex_close(e, i)
    far_close(1)
    far_close(3)
    for near, copy in homes:

        @pl.when(jnp.logical_not(near))
        def _():
            copy.wait_send()


def place_outputs(out_i, ig_i, peq, peu, go_i, gdn_i, out, ig, gq, gk, gv, go, gup, gdn, PQ, PU, GQ, GU, A, B, GO, GD, sem):
    pairs = ((peq, PQ), (peu, PU), (out_i, A), (ig_i, B), (go_i, GO), (gdn_i, GD))
    moves = [pltpu.make_async_copy(src, dst, sem.at[k]) for k, (src, dst) in enumerate(pairs)]
    for move in moves:
        move.start()
    results = ((A, out), (B, ig), (GO, go), (GD, gdn), (GQ.at[0], gq), (GQ.at[1], gk), (GQ.at[2], gv), (GU, gup))
    last = [pltpu.make_async_copy(src, dst, sem.at[6 + k]) for k, (src, dst) in enumerate(results)]
    hd = PQ.shape[2] // 6
    fw = PU.shape[2] // 8
    moves[0].wait()
    moves[1].wait()
    for tt in range(RANKS):
        for j in range(2):
            a = (j * RANKS + tt) * hd
            for n in range(3):
                GQ[n, :, a : a + hd] = PQ[tt, :, (n * 2 + j) * hd : (n * 2 + j + 1) * hd].astype(F32)
        for k in range(8):
            a = hidden_at(k, tt) * fw
            GU[:, a : a + fw] = PU[tt, :, k * fw : (k + 1) * fw].astype(F32)
    for k in range(4):
        last[4 + k].start()
    for k in range(4):
        moves[2 + k].wait()
        last[k].start()
    for move in last:
        move.wait()


def call_fused(inputs, positions, w_query, w_key, w_value, w_out, w_up, w_down, up_bias, down_bias,
               ln1_gain, ln1_bias, ln2_gain, ln2_bias, cotangent):
    rows, width = inputs.shape
    hid = w_up.shape[1] // RANKS
    rw, fw = w_query.shape[0], w_down.shape[0]
    shapes = scratch_of(rows, width, hid, rw, fw)
    blk = lax.axis_index("blk")
    small_in = [v.reshape(1, -1) for v in (down_bias, ln1_gain, ln1_bias, ln2_gain, ln2_bias, up_bias)]
    names = IN_NAMES + OUT_NAMES + tuple(shapes)
    any_, vm = pl.BlockSpec(memory_space=pl.ANY), pl.BlockSpec(memory_space=pltpu.VMEM)
    S = jax.ShapeDtypeStruct
    cols = 3 * 2 * (width // HEADS)
    tokens, wide = S((rows, width), BF16), S((rw, width), F32)
    moved = (S((RANKS, rw, cols), BF16), S((RANKS, rw, hid), BF16))
    out, ig, peq, peu, go, gdn, gvec = pl.pallas_call(
        functools.partial(fused, names),
        out_shape=(tokens, tokens) + moved + (wide, S(w_down.shape, F32), S((2, 8, 128), F32)),
        in_specs=[any_, any_, vm] + [any_] * 6 + [vm] * 6,
        out_specs=[any_] * 6 + [vm],
        scratch_shapes=list(shapes.values()),
        compiler_params=pltpu.CompilerParams(
            collective_id=0, has_side_effects=True, vmem_limit_bytes=VMEM_BYTES
        ),
        cost_estimate=pl.CostEstimate(flops=23 * 10**9, bytes_accessed=10**7, transcendentals=10**6),
    )(inputs, cotangent, positions.reshape(2, -1), w_query, w_key, w_value, w_out, w_up, w_down, *small_in)
    out, ig, gq, gk, gv, go, gup, gdn = pl.pallas_call(
        place_outputs,
        out_shape=(tokens, tokens, wide, wide, wide, wide, S(w_up.shape, F32), S(w_down.shape, F32)),
        in_specs=[any_] * 6,
        out_specs=[any_] * 8,
        scratch_shapes=[
            pltpu.VMEM(moved[0].shape, BF16),
            pltpu.VMEM(moved[1].shape, BF16),
            pltpu.VMEM((3, rw, width), F32),
            pltpu.VMEM(w_up.shape, F32),
            pltpu.VMEM((rows, width), BF16),
            pltpu.VMEM((rows, width), BF16),
            pltpu.VMEM((rw, width), F32),
            pltpu.VMEM(w_down.shape, F32),
            pltpu.SemaphoreType.DMA((14,)),
        ],
        compiler_params=pltpu.CompilerParams(vmem_limit_bytes=VMEM_BYTES),
    )(out, ig, peq, peu, go, gdn)
    small = lax.dynamic_slice(gvec[0], (0, blk * rw), (5, rw))
    gup_bias = gvec[1, 5]
    return (out, ig, gq, gk, gv, go, gup, gdn, gup_bias, small[0], small[1], small[2], small[3], small[4])


def layer_norm(values, gain, offset):
    centre = jnp.mean(values, axis=-1, keepdims=True)
    centred = values - centre
    variance = jnp.mean(centred * centred, axis=-1, keepdims=True)
    return centred * lax.rsqrt(variance + eps) * gain + offset


def smooth_gate(values):
    return jax.nn.gelu(values, approximate=True)


def keep_same(carry):
    return carry


def local(
    inputs,
    positions,
    w_query,
    w_key,
    w_value,
    w_out,
    w_up,
    w_down,
    up_bias,
    down_bias,
    ln1_gain,
    ln1_bias,
    ln2_gain,
    ln2_bias,
    cotangent,
):
    attn_full = (
        lax.all_gather(w_query, ("dp", "blk"), axis=0, tiled=True),
        lax.all_gather(w_key, ("dp", "blk"), axis=0, tiled=True),
        lax.all_gather(w_value, ("dp", "blk"), axis=0, tiled=True),
        lax.all_gather(w_out, ("dp", "blk"), axis=0, tiled=True),
        lax.all_gather(ln1_gain, ("dp", "blk"), axis=0, tiled=True),
        lax.all_gather(ln1_bias, ("dp", "blk"), axis=0, tiled=True),
    )
    ffn_full = (
        lax.all_gather(w_up, ("dp", "blk"), axis=0, tiled=True),
        lax.all_gather(w_down, ("dp", "blk"), axis=0, tiled=True),
        lax.all_gather(up_bias, ("dp", "blk"), axis=0, tiled=True),
        lax.all_gather(down_bias, ("dp", "blk"), axis=0, tiled=True),
        lax.all_gather(ln2_gain, ("dp", "blk"), axis=0, tiled=True),
        lax.all_gather(ln2_bias, ("dp", "blk"), axis=0, tiled=True),
    )
    token_rows = inputs.astype(jnp.float32)
    local_rows, model_width = token_rows.shape
    head_count = HEADS
    head_size = model_width // head_count
    score_scale = 1.0 / math.sqrt(head_size)
    normed_first, first_pull = jax.vjp(
        layer_norm, token_rows, attn_full[4].astype(jnp.float32), attn_full[5].astype(jnp.float32)
    )
    normed_low = normed_first.astype(jnp.bfloat16)
    query_low = jnp.dot(normed_low, attn_full[0], preferred_element_type=jnp.float32).astype(
        jnp.bfloat16
    )
    key_low = jnp.dot(normed_low, attn_full[1], preferred_element_type=jnp.float32).astype(
        jnp.bfloat16
    )
    value_low = jnp.dot(normed_low, attn_full[2], preferred_element_type=jnp.float32).astype(
        jnp.bfloat16
    )
    keys_all, values_all = (
        lax.all_gather(key_low, "blk", axis=0, tiled=True),
        lax.all_gather(value_low, "blk", axis=0, tiled=True),
    )
    group_rows = keys_all.shape[0]
    key_rows = max(min(512, group_rows), local_rows)
    block_count = group_rows // key_rows
    first_row = lax.axis_index("blk") * local_rows
    query_index = first_row + jnp.arange(local_rows, dtype=jnp.int32)
    seq_start = query_index - positions
    earliest = jnp.min(seq_start)
    query_heads = query_low.reshape(local_rows, head_count, head_size)
    key_parts = []
    for which in range(block_count):
        begin = which * key_rows
        key_part = keys_all[begin : begin + key_rows].reshape(key_rows, head_count, head_size)
        value_part = values_all[begin : begin + key_rows].reshape(key_rows, head_count, head_size)
        key_index = begin + jnp.arange(key_rows, dtype=jnp.int32)
        allowed = (key_index[None, :] <= query_index[:, None]) & (
            key_index[None, :] >= seq_start[:, None]
        )
        needed = (begin <= first_row + local_rows - 1) & (begin + key_rows - 1 >= earliest)
        key_parts.append((key_part, value_part, allowed, needed))

    def scores_of(key_part, allowed):
        scores = (
            jnp.einsum("qhd,khd->hqk", query_heads, key_part, preferred_element_type=jnp.float32)
            * score_scale
        )
        return jnp.where(allowed[None], scores, masked_value)

    running_max = jnp.full((head_count, local_rows), masked_value, jnp.float32)
    running_sum = jnp.zeros((head_count, local_rows), jnp.float32)
    for key_part, value_part, allowed, needed in key_parts:

        def extend(carry):
            old_max, old_sum = carry
            scores = scores_of(key_part, allowed)
            new_max = jnp.maximum(old_max, jnp.max(scores, axis=-1))
            terms = jnp.where(allowed[None], jnp.exp(scores - new_max[..., None]), 0.0)
            return (new_max, old_sum * jnp.exp(old_max - new_max) + jnp.sum(terms, axis=-1))

        running_max, running_sum = lax.cond(needed, extend, keep_same, (running_max, running_sum))
    log_total = running_max + jnp.log(running_sum)

    def probs_of(key_part, allowed):
        scores = scores_of(key_part, allowed)
        return jnp.where(allowed[None], jnp.exp(scores - log_total[..., None]), 0.0)

    attended = jnp.zeros((local_rows, head_count, head_size), jnp.float32)
    for key_part, value_part, allowed, needed in key_parts:

        def gather_values(total):
            weights_low = probs_of(key_part, allowed).astype(jnp.bfloat16)
            return total + jnp.einsum(
                "hqk,khd->qhd", weights_low, value_part, preferred_element_type=jnp.float32
            )

        attended = lax.cond(needed, gather_values, keep_same, attended)
    mixed_low = attended.reshape(local_rows, model_width).astype(jnp.bfloat16)
    residual = token_rows + jnp.dot(mixed_low, attn_full[3], preferred_element_type=jnp.float32)
    normed_second, second_pull = jax.vjp(
        layer_norm, residual, ffn_full[4].astype(jnp.float32), ffn_full[5].astype(jnp.float32)
    )
    normed_two = normed_second.astype(jnp.bfloat16)
    preact = jnp.dot(normed_two, ffn_full[0], preferred_element_type=jnp.float32) + ffn_full[
        2
    ].astype(jnp.float32)
    gated, gate_pull = jax.vjp(smooth_gate, preact)
    hidden = gated.astype(jnp.bfloat16)
    output = (
        residual
        + jnp.dot(hidden, ffn_full[1], preferred_element_type=jnp.float32)
        + ffn_full[3].astype(jnp.float32)
    ).astype(jnp.bfloat16)
    up_back, down_back = (ffn_full[0], ffn_full[1])
    grad_final = cotangent.astype(jnp.float32)
    grad_down_w = jnp.einsum("tf,td->fd", hidden, cotangent, preferred_element_type=jnp.float32)
    grad_down_shift = jnp.sum(grad_final, axis=0)
    grad_hidden = jnp.einsum("td,fd->tf", cotangent, down_back, preferred_element_type=jnp.float32)
    grad_preact = gate_pull(grad_hidden)[0].astype(jnp.bfloat16)
    grad_up_shift = jnp.sum(grad_preact.astype(jnp.float32), axis=0)
    grad_up_w = jnp.einsum("td,tf->df", normed_two, grad_preact, preferred_element_type=jnp.float32)
    grad_normed_two = jnp.einsum(
        "tf,df->td", grad_preact, up_back, preferred_element_type=jnp.float32
    )
    grad_resid_two, grad_gain_two, grad_shift_two = second_pull(grad_normed_two)
    grad_residual = grad_final + grad_resid_two
    query_back, key_back, value_back, out_back = (
        attn_full[0],
        attn_full[1],
        attn_full[2],
        attn_full[3],
    )
    grad_branch = grad_residual.astype(jnp.bfloat16)
    grad_out_w = jnp.einsum("te,td->ed", mixed_low, grad_branch, preferred_element_type=jnp.float32)
    grad_mixed = jnp.einsum(
        "td,ed->te", grad_branch, out_back, preferred_element_type=jnp.float32
    ).astype(jnp.bfloat16)
    grad_heads = grad_mixed.reshape(local_rows, head_count, head_size)
    delta = jnp.zeros((head_count, local_rows), jnp.float32)
    for key_part, value_part, allowed, needed in key_parts:

        def add_delta(total):
            probs = probs_of(key_part, allowed)
            grad_probs = jnp.einsum(
                "qhd,khd->hqk", grad_heads, value_part, preferred_element_type=jnp.float32
            )
            return total + jnp.sum(probs * grad_probs, axis=-1)

        delta = lax.cond(needed, add_delta, keep_same, delta)
    grad_query_sum = jnp.zeros((local_rows, head_count, head_size), jnp.float32)
    kv_terms = []
    for key_part, value_part, allowed, needed in key_parts:

        def backward_part(total):
            probs = probs_of(key_part, allowed)
            grad_probs = jnp.einsum(
                "qhd,khd->hqk", grad_heads, value_part, preferred_element_type=jnp.float32
            )
            grad_scores = (probs * (grad_probs - delta[..., None]) * score_scale).astype(
                jnp.bfloat16
            )
            new_total = total + jnp.einsum(
                "hqk,khd->qhd", grad_scores, key_part, preferred_element_type=jnp.float32
            )
            grad_keys = jnp.einsum(
                "hqk,qhd->khd", grad_scores, query_heads, preferred_element_type=jnp.float32
            ).reshape(key_rows, model_width)
            grad_values = jnp.einsum(
                "hqk,qhd->khd",
                probs.astype(jnp.bfloat16),
                grad_heads,
                preferred_element_type=jnp.float32,
            ).reshape(key_rows, model_width)
            return (new_total, jnp.concatenate([grad_keys, grad_values], axis=1))

        def skip_part(total):
            return (total, jnp.zeros((key_rows, 2 * model_width), jnp.float32))

        grad_query_sum, kv_term = lax.cond(needed, backward_part, skip_part, grad_query_sum)
        kv_terms.append(kv_term)
    kv_shares = lax.psum_scatter(
        jnp.concatenate(kv_terms, axis=0).astype(jnp.bfloat16),
        "blk",
        scatter_dimension=0,
        tiled=True,
    ).astype(jnp.float32)
    grad_key_low = kv_shares[:, :model_width].astype(jnp.bfloat16)
    grad_value_low = kv_shares[:, model_width:].astype(jnp.bfloat16)
    grad_query_low = grad_query_sum.reshape(local_rows, model_width).astype(jnp.bfloat16)
    grad_query_w = jnp.einsum(
        "td,te->de", normed_low, grad_query_low, preferred_element_type=jnp.float32
    )
    grad_key_w = jnp.einsum(
        "td,te->de", normed_low, grad_key_low, preferred_element_type=jnp.float32
    )
    grad_value_w = jnp.einsum(
        "td,te->de", normed_low, grad_value_low, preferred_element_type=jnp.float32
    )
    grad_normed = (
        jnp.einsum("te,de->td", grad_query_low, query_back, preferred_element_type=jnp.float32)
        + jnp.einsum("te,de->td", grad_key_low, key_back, preferred_element_type=jnp.float32)
        + jnp.einsum("te,de->td", grad_value_low, value_back, preferred_element_type=jnp.float32)
    )
    grad_rows_one, grad_gain_one, grad_shift_one = first_pull(grad_normed)
    input_grad = (grad_residual + grad_rows_one).astype(jnp.bfloat16)
    shares = (
        lax.psum_scatter(grad_query_w, ("dp", "blk"), scatter_dimension=0, tiled=True),
        lax.psum_scatter(grad_key_w, ("dp", "blk"), scatter_dimension=0, tiled=True),
        lax.psum_scatter(grad_value_w, ("dp", "blk"), scatter_dimension=0, tiled=True),
        lax.psum_scatter(grad_out_w, ("dp", "blk"), scatter_dimension=0, tiled=True),
        lax.psum_scatter(grad_up_w, ("dp", "blk"), scatter_dimension=0, tiled=True),
        lax.psum_scatter(grad_down_w, ("dp", "blk"), scatter_dimension=0, tiled=True),
        lax.psum_scatter(grad_up_shift, ("dp", "blk"), scatter_dimension=0, tiled=True),
        lax.psum_scatter(grad_down_shift, ("dp", "blk"), scatter_dimension=0, tiled=True),
        lax.psum_scatter(grad_gain_one, ("dp", "blk"), scatter_dimension=0, tiled=True),
        lax.psum_scatter(grad_shift_one, ("dp", "blk"), scatter_dimension=0, tiled=True),
        lax.psum_scatter(grad_gain_two, ("dp", "blk"), scatter_dimension=0, tiled=True),
        lax.psum_scatter(grad_shift_two, ("dp", "blk"), scatter_dimension=0, tiled=True),
    )
    return (
        output,
        input_grad,
        shares[0],
        shares[1],
        shares[2],
        shares[3],
        shares[4],
        shares[5],
        shares[6],
        shares[7],
        shares[8],
        shares[9],
        shares[10],
        shares[11],
    )


def solution(mesh):
    in_specs = (
        P(("dp", "blk"), None),
        P(("dp", "blk")),
        P(("dp", "blk"), None),
        P(("dp", "blk"), None),
        P(("dp", "blk"), None),
        P(("dp", "blk"), None),
        P(("dp", "blk"), None),
        P(("dp", "blk"), None),
        P(("dp", "blk")),
        P(("dp", "blk")),
        P(("dp", "blk")),
        P(("dp", "blk")),
        P(("dp", "blk")),
        P(("dp", "blk")),
        P(("dp", "blk"), None),
    )
    out_specs = (
        P(("dp", "blk"), None),
        P(("dp", "blk"), None),
        P(("dp", "blk"), None),
        P(("dp", "blk"), None),
        P(("dp", "blk"), None),
        P(("dp", "blk"), None),
        P(("dp", "blk"), None),
        P(("dp", "blk"), None),
        P(("dp", "blk")),
        P(("dp", "blk")),
        P(("dp", "blk")),
        P(("dp", "blk")),
        P(("dp", "blk")),
        P(("dp", "blk")),
    )
    n_dp, n_blk = mesh.shape["dp"], mesh.shape["blk"]

    def layer(*args):
        fits = n_blk == RANKS and n_dp == 2 * RANKS and args[2].shape[0] // (n_dp * n_blk) % 16 == 0
        call = jax.shard_map(
            call_fused if fits else local, mesh=mesh, in_specs=in_specs, out_specs=out_specs, check_vma=False
        )
        return call(*args)

    return layer
```
